32 devices in a mesh: dp: 16 (over z, y, x), tensor: 2 (over core).
Axes of the slice: x: 2, y: 2, z: 4, core: 2. Of those that a mesh axis runs over, the one named last changes fastest.
Arguments:
- images: bfloat16 [160, 64, 768], P('dp', None, 'tensor'), may hold values from -6 to 6
- embedding: bfloat16 [160, 768], P('dp', 'tensor'), may hold values from -6 to 6
- counts: int32 [16], P('dp'), may hold values from 0 to 10, as said below
- norm_gains: float32 [3, 768], P(None, 'tensor'), may hold values from 0.5 to 1.5
- norm_shifts: float32 [3, 768], P(None, 'tensor'), may hold values from -3 to 3
- lin_biases: float32 [7, 768], P(None, 'tensor'), may hold values from -3 to 3
- conv_weights: bfloat16 [2, 9, 768, 768], P(None, None, 'dp', 'tensor'), may hold values from -0.078125 to 0.078125
- aff_weights: bfloat16 [768, 2, 768], P('dp', None, 'tensor'), may hold values from -0.21875 to 0.21875
- qkv_weights: bfloat16 [768, 3, 768], P('dp', None, 'tensor'), may hold values from -0.21875 to 0.21875
- proj_weights: bfloat16 [768, 768], P('dp', 'tensor'), may hold values from -1.75 to 1.75
- cotangent: float32 [160, 64, 768], P('dp', None, 'tensor'), may hold values from -6 to 6
Outputs:
- block_output: bfloat16 [160, 64, 768], P('dp', None, 'tensor')
- images_grad: bfloat16 [160, 64, 768], P('dp', None, 'tensor')
- embedding_grad: bfloat16 [160, 768], P('dp', 'tensor')
- gains_grad: float32 [3, 768], P(None, 'tensor')
- shifts_grad: float32 [3, 768], P(None, 'tensor')
- biases_grad: float32 [7, 768], P(None, 'tensor')
- conv_grad: float32 [2, 9, 768, 768], P(None, None, 'dp', 'tensor')
- aff_grad: float32 [768, 2, 768], P('dp', None, 'tensor')
- qkv_grad: float32 [768, 3, 768], P('dp', None, 'tensor')
- proj_grad: float32 [768, 768], P('dp', 'tensor')
The draws below stay inside these ranges and needn't reach their ends.
Inputs may be any that keep to these rules, and one draw needn't show every extreme that they name: Device d of dp holds counts[d] real images, in its first counts[d] of 10 slots; some device holds 10.
All inputs are finite; a program needn't handle non-finite values.
Results may differ from the reference program's by a relative error of at most 0.02.
Values may be sent and summed in bfloat16 or wider, within the bound.
A program may use at most 192 MiB of HBM per device.

```python
import math
import jax
import jax.numpy as jnp
from jax import lax

C = 768
HEAD_DIM = 64
GROUPS = 32
SIDE = 8
SLOTS = 10
PIXELS = 64
IMAGES = 160
N_DP = 16


def draw_counts(key, part):
    key = jax.random.fold_in(key, 7)
    draw_key, pick_key = jax.random.split(key)
    drawn = jax.random.randint(draw_key, (N_DP,), 0, SLOTS + 1)
    chosen = jax.random.randint(pick_key, (), 0, N_DP)
    return jnp.where(jnp.arange(N_DP) == chosen, SLOTS, drawn).astype(jnp.int32)


def shard_levels(own_key, extent, shards, smallest, largest):
    level, own = 1.0, jax.random.fold_in(own_key, 6)
    for dim, parts in shards:
        draws = jnp.exp(jax.random.uniform(jax.random.fold_in(own, dim), (parts,), jnp.float32, smallest / len(shards), largest / len(shards)))
        level = level * jnp.repeat(draws, extent[dim] // parts).reshape([-1 if axis == dim else 1 for axis in range(len(extent))])
    return level


def scatter_about(own_key, extent, scale, reach, pieces=(), held_as=jnp.bfloat16):
    values = scale * jax.random.normal(own_key, extent, jnp.float32)
    if pieces:
        values = values * shard_levels(own_key, extent, pieces, -0.22, 0.18)
    return jnp.clip(values, -reach, reach).astype(held_as)


def setup_inputs(seed: int = 0) -> dict:
    splits = jax.random.split(jax.random.key(seed), 12)
    images = scatter_about(splits[0], (IMAGES, PIXELS, C), 1.0, 6.0, ((0, 16), (2, 2)))
    embedding = scatter_about(splits[1], (IMAGES, C), 1.0, 6.0, ((0, 16), (1, 2)))
    counts = draw_counts(jax.random.fold_in(splits[11], 71), 0)
    norm_gains = jnp.clip(1.0 + 0.1 * jax.random.normal(splits[3], (3, C), jnp.float32), 0.5, 1.5)
    norm_shifts = scatter_about(splits[4], (3, C), 0.5, 3.0, ((1, 2),), jnp.float32)
    lin_biases = scatter_about(splits[5], (7, C), 0.5, 3.0, ((1, 2),), jnp.float32)
    conv_weights = scatter_about(splits[6], (2, 9, C, C), (9 * C) ** -0.5, 0.078125, ((2, 16), (3, 2)))
    aff_weights = scatter_about(splits[7], (C, 2, C), C ** -0.5, 0.21875, ((0, 16), (2, 2)))
    qkv_weights = scatter_about(splits[8], (C, 3, C), C ** -0.5, 0.21875, ((0, 16), (2, 2)))
    proj_weights = scatter_about(splits[9], (C, C), (C // 64) ** -0.5, 1.75, ((0, 16), (1, 2)))
    cotangent = scatter_about(splits[10], (IMAGES, PIXELS, C), 1.0, 6.0, ((0, 16), (2, 2)), jnp.float32)
    return {"images": images, "embedding": embedding, "counts": counts, "norm_gains": norm_gains, "norm_shifts": norm_shifts, "lin_biases": lin_biases, "conv_weights": conv_weights, "aff_weights": aff_weights, "qkv_weights": qkv_weights, "proj_weights": proj_weights, "cotangent": cotangent}


@jax.custom_vjp
def low(v):
    return lax.optimization_barrier(v.astype(jnp.bfloat16)).astype(jnp.float32)

@jax.custom_vjp
def low_back(v):
    return v

def low_keep(v):
    return (low(v), None)

def low_pass(kept, grad):
    return (grad,)

def back_keep(v):
    return (v, None)

def back_low(kept, grad):
    return (low(grad),)
low.defvjp(low_keep, low_pass)
low_back.defvjp(back_keep, back_low)

def group_norm(values, gain_vec, shift_vec):
    batch_size = values.shape[0]
    grouped = values.reshape(batch_size, PIXELS, -1, C // GROUPS)
    centre = lax.optimization_barrier(jnp.mean(grouped, axis=(1, 3), keepdims=True))
    spread = lax.optimization_barrier(jnp.mean(jnp.square(grouped - centre), axis=(1, 3), keepdims=True))
    normal = ((grouped - centre) * lax.rsqrt(spread + 1e-05)).reshape(values.shape)
    return normal * gain_vec + shift_vec

def convolve(source, kernel):
    batch_size = source.shape[0]
    padded = jnp.pad(source.reshape(batch_size, SIDE, SIDE, -1), ((0, 0), (1, 1), (1, 1), (0, 0)))
    summed = jnp.zeros((batch_size, PIXELS, kernel.shape[2]), jnp.float32)
    for tap_index in range(9):
        row_shift = tap_index // 3
        col_shift = tap_index % 3
        window = padded[:, row_shift:row_shift + SIDE, col_shift:col_shift + SIDE].reshape(batch_size, PIXELS, -1)
        summed = summed + jnp.einsum('bpc,cd->bpd', window, kernel[tap_index], precision=lax.Precision.HIGHEST)
    return summed

def forward(images, embedding, params, slot_mask):
    gains, shifts, biases, conv_w, aff_w, qkv_w, proj_w = params
    batch_size = images.shape[0]
    hidden0 = low(jax.nn.silu(group_norm(images, gains[0], shifts[0])))
    conv_out0 = low_back(convolve(hidden0, conv_w[0]) + biases[0])
    modulation = low_back(jnp.einsum('bc,cjd->bjd', embedding, aff_w, precision=lax.Precision.HIGHEST) + biases[5:7])
    scaled = group_norm(conv_out0, gains[1], shifts[1]) * (1.0 + modulation[:, 0:1]) + modulation[:, 1:2]
    hidden1 = low(jax.nn.silu(scaled))
    conv_out1 = low_back(convolve(hidden1, conv_w[1]) + biases[1])
    residual = images + conv_out1
    normed = low(group_norm(residual, gains[2], shifts[2]))
    bias_rows = jnp.stack([biases[2], jnp.zeros_like(biases[2]), biases[3]])
    projected = jnp.einsum('bpc,cjd->bpjd', normed, qkv_w, precision=lax.Precision.HIGHEST) + bias_rows
    projected = low_back(low(projected))
    head_shape = (batch_size, PIXELS, -1, HEAD_DIM)
    query_heads = projected[:, :, 0].reshape(head_shape)
    key_heads = projected[:, :, 1].reshape(head_shape)
    value_heads = projected[:, :, 2].reshape(head_shape)
    scores = low_back(jnp.einsum('bqhd,bkhd->bhqk', query_heads, key_heads, precision=lax.Precision.HIGHEST) * HEAD_DIM ** (-0.5))
    weights_low = low(jax.nn.softmax(scores, axis=-1))
    attended = jnp.einsum('bhqk,bkhd->bqhd', weights_low, value_heads, precision=lax.Precision.HIGHEST).reshape(batch_size, PIXELS, -1)
    attended = low_back(low(attended))
    branch = low_back(jnp.einsum('bpc,cd->bpd', attended, proj_w, precision=lax.Precision.HIGHEST) + biases[4])
    return slot_mask[:, None, None] * (residual + branch)

def reference(images, embedding, counts, norm_gains, norm_shifts, lin_biases, conv_weights, aff_weights, qkv_weights, proj_weights, cotangent):
    slot_ids = jnp.arange(IMAGES, dtype=jnp.int32)
    slot_mask = (slot_ids % SLOTS < counts[slot_ids // SLOTS]).astype(jnp.float32)
    params = tuple((argument.astype(jnp.float32) for argument in (norm_gains, norm_shifts, lin_biases, conv_weights, aff_weights, qkv_weights, proj_weights)))
    block_size = math.gcd(IMAGES, 64)
    block_count = IMAGES // block_size

    def into_blocks(array):
        return array.reshape((block_count, block_size) + array.shape[1:])

    def block_step(totals, inputs):
        image_blk, embed_blk, mask_blk, cot_blk = inputs

        def local_forward(image_arg, embed_arg, param_arg):
            return forward(image_arg, embed_arg, param_arg, mask_blk)
        result, pullback = jax.vjp(local_forward, image_blk, embed_blk, params)
        grad_image, grad_embed, grad_params = pullback(cot_blk)
        totals = jax.tree.map(jnp.add, totals, grad_params)
        return (totals, (result.astype(jnp.bfloat16), grad_image.astype(jnp.bfloat16), grad_embed.astype(jnp.bfloat16)))
    initial = jax.tree.map(jnp.zeros_like, params)
    totals, outputs = lax.scan(block_step, initial, (into_blocks(images.astype(jnp.float32)), into_blocks(embedding.astype(jnp.float32)), into_blocks(slot_mask), into_blocks(cotangent)))
    block_output = outputs[0].reshape(IMAGES, PIXELS, C)
    images_grad = outputs[1].reshape(IMAGES, PIXELS, C)
    embedding_grad = outputs[2].reshape(IMAGES, C)
    return (block_output, images_grad, embedding_grad, totals[0], totals[1], totals[2], totals[3], totals[4], totals[5], totals[6])
```

```python
import functools

import jax
import jax.numpy as jnp
from jax import lax
from jax.experimental import pallas as pl
from jax.experimental.pallas import tpu as pltpu
from jax.sharding import PartitionSpec as P

MESH = pl.DeviceIdType.MESH
GRID = (4, 2, 2)

C = 768
HEAD_DIM = 64
GROUPS = 32
SIDE = 8
PIXELS = 64


def piece_columns(width):
    convs = [(part * 3 * width, 3 * width) for part in range(6)]
    return convs[:3] + [(18 * width, 2 * width)] + convs[3:] + [(20 * width, 3 * width), (23 * width, width)]


def place():
    spot = lax.axis_index("dp")
    return spot, spot // 4, lax.rem(spot // 2, 2), lax.rem(spot, 2)


def gather_kernel(pieces, conv_ref, aff_ref, qkv_ref, proj_ref, full_ref, own_sem, zsend, zrecv, fsend, frecv, ssend, srecv):
    spot, z, y, x = place()
    width = conv_ref.shape[3]
    barrier = pltpu.get_barrier_semaphore()
    line = [lax.rem(z + j, 4) * 4 + y * 2 + x for j in (1, 2, 3)]
    xmate, ymate = z * 4 + y * 2 + 1 - x, z * 4 + (1 - y) * 2 + x
    for mate in line + [xmate, ymate]:
        pl.semaphore_signal(barrier, inc=1, device_id={"dp": mate}, device_id_type=MESH)
    own = []
    for tap in range(18):
        own.append(pltpu.make_async_copy(conv_ref.at[tap // 9, tap % 9], full_ref.at[z, y, x, :, pl.ds(tap * width, width)], own_sem.at[tap]))
    for at, (ref, start, size) in enumerate(((aff_ref, 18, 2), (qkv_ref, 20, 3), (proj_ref, 23, 1))):
        own.append(pltpu.make_async_copy(ref, full_ref.at[z, y, x, :, pl.ds(start * width, size * width)], own_sem.at[18 + at]))
    for copy in own:
        copy.start()
    for copy in own:
        copy.wait()
    pl.semaphore_wait(barrier, 5)

    def remote(at, send, recv, mate):
        return pltpu.make_async_remote_copy(src_ref=at, dst_ref=at, send_sem=send, recv_sem=recv, device_id={"dp": mate}, device_id_type=MESH)

    started = {}

    def stage(p, s):
        cols = pl.ds(*pieces[p])
        if s == 0:
            block = full_ref.at[z, y, x, :, cols]
            copies = [remote(block, zsend.at[p, j], zrecv.at[p, j], line[j]) for j in range(3)]
        else:
            for copy in started[p, s - 1]:
                copy.wait_recv()
            if s == 1:
                block = full_ref.at[:, y, x, :, cols]
                copies = [remote(block, fsend.at[p], frecv.at[p], ymate if p % 2 else xmate)]
            elif s == 2:
                block = full_ref.at[:, :, x, :, cols] if p % 2 else full_ref.at[:, y, :, :, cols]
                copies = [remote(block, ssend.at[p], srecv.at[p], xmate if p % 2 else ymate)]
            else:
                copies = []
        for copy in copies:
            copy.start()
        started[p, s] = copies

    for step in range(len(pieces) + 3):
        for p in range(len(pieces)):
            if 0 <= step - p <= 3:
                stage(p, step - p)
    for copies in started.values():
        for copy in copies:
            copy.wait_send()


def gather_weights(conv, aff, qkv, proj):
    rows, width = conv.shape[2], conv.shape[3]
    pieces = piece_columns(width)
    n = len(pieces)
    dma = pltpu.SemaphoreType.DMA
    full = pl.pallas_call(
        functools.partial(gather_kernel, pieces),
        out_shape=jax.ShapeDtypeStruct(GRID + (rows, 24 * width), jnp.bfloat16),
        in_specs=[pl.BlockSpec(memory_space=pl.ANY)] * 4,
        out_specs=pl.BlockSpec(memory_space=pl.ANY),
        scratch_shapes=[dma((21,)), dma((n, 3)), dma((n, 3)), dma((n,)), dma((n,)), dma((n,)), dma((n,))],
        compiler_params=pltpu.CompilerParams(collective_id=0, has_side_effects=True),
    )(conv, aff.reshape(rows, -1), qkv.reshape(rows, -1), proj)
    return full


def scatter_kernel(pieces, grad_ref, small_ref, out_ref, total_ref, work, r1, r2, r3, smalls, in_sem, sem1, sem2, sem3, small_sem):
    spot, z, y, x = place()
    barrier = pltpu.get_barrier_semaphore()
    everyone = [lax.rem(spot + j, 16) for j in range(1, 16)]
    line = [lax.rem(z + j, 4) for j in (1, 2, 3)]
    xmate, ymate = z * 4 + y * 2 + 1 - x, z * 4 + (1 - y) * 2 + x
    for mate in everyone:
        pl.semaphore_signal(barrier, inc=1, device_id={"dp": mate}, device_id_type=MESH)
    loads = []
    for p, (start, size) in enumerate(pieces):
        cols = pl.ds(start, size)
        loads.append(pltpu.make_async_copy(grad_ref.at[:, :, :, :, cols], work.at[:, :, :, :, cols], in_sem.at[p]))
        loads[-1].start()
    pl.semaphore_wait(barrier, 15)

    def remote(src, dst, send, recv, mate):
        copy = pltpu.make_async_remote_copy(src_ref=src, dst_ref=dst, send_sem=send, recv_sem=recv, device_id={"dp": mate}, device_id_type=MESH)
        copy.start()
        return copy

    small_copies = [remote(small_ref, smalls.at[spot], small_sem.at[0, j], small_sem.at[1, j], mate) for j, mate in enumerate(everyone)]
    smalls[spot] = small_ref[...]
    started = {}

    def stage(p, s):
        cols = pl.ds(*pieces[p])
        odd = p % 2
        copies = []
        if s == 0:
            loads[p].wait()
            block = work.at[:, 1 - y, :, :, cols] if odd else work.at[:, :, 1 - x, :, cols]
            copies = [remote(block, r1.at[:, :, :, cols], sem1.at[0, p], sem1.at[1, p], ymate if odd else xmate)]
        elif s == 1:
            for copy in started[p, 0]:
                copy.wait_recv()
            for zz in range(4):
                for other in range(2):
                    spot_now = (zz, y, other) if odd else (zz, other, x)
                    total = work[spot_now + (slice(None), cols)].astype(jnp.float32) + r1[zz, other, :, cols].astype(jnp.float32)
                    work[spot_now + (slice(None), cols)] = total.astype(jnp.bfloat16)
            block = work.at[:, y, 1 - x, :, cols] if odd else work.at[:, 1 - y, x, :, cols]
            copies = [remote(block, r2.at[:, :, cols], sem2.at[0, p], sem2.at[1, p], xmate if odd else ymate)]
        elif s == 2:
            for copy in started[p, 1]:
                copy.wait_recv()
            for zz in range(4):
                total = work[zz, y, x, :, cols].astype(jnp.float32) + r2[zz, :, cols].astype(jnp.float32)
                work[zz, y, x, :, cols] = total.astype(jnp.bfloat16)
            copies = [remote(work.at[zz, y, x, :, cols], r3.at[j, :, cols], sem3.at[0, p, j], sem3.at[1, p, j], zz * 4 + y * 2 + x) for j, zz in enumerate(line)]
        else:
            for copy in started[p, 2]:
                copy.wait_recv()
            total = work[z, y, x, :, cols].astype(jnp.float32)
            for j in range(3):
                total = total + r3[j, :, cols].astype(jnp.float32)
            out_ref[:, cols] = total
        started[p, s] = copies

    for step in range(len(pieces) + 3):
        for p in range(len(pieces)):
            if 0 <= step - p <= 3:
                stage(p, step - p)
    for copy in small_copies:
        copy.wait_recv()
    total_ref[...] = jnp.sum(smalls[...], axis=0)
    for copies in list(started.values()) + [small_copies]:
        for copy in copies:
            copy.wait_send()


def scatter_grads(grad, small):
    rows, columns = grad.shape[3:]
    pieces = piece_columns(columns // 24)
    n = len(pieces)
    dma = pltpu.SemaphoreType.DMA
    low = jnp.bfloat16
    vmem = pl.BlockSpec(memory_space=pltpu.VMEM)
    return pl.pallas_call(
        functools.partial(scatter_kernel, pieces),
        out_shape=(jax.ShapeDtypeStruct((rows, columns), jnp.float32), jax.ShapeDtypeStruct(small.shape, jnp.float32)),
        in_specs=[pl.BlockSpec(memory_space=pl.ANY), vmem],
        out_specs=(vmem, vmem),
        scratch_shapes=[
            pltpu.VMEM(grad.shape, low),
            pltpu.VMEM((4, 2, rows, columns), low),
            pltpu.VMEM((4, rows, columns), low),
            pltpu.VMEM((3, rows, columns), low),
            pltpu.VMEM((16,) + small.shape, jnp.float32),
            dma((n,)), dma((2, n)), dma((2, n)), dma((2, n, 3)), dma((2, 15)),
        ],
        compiler_params=pltpu.CompilerParams(collective_id=1, has_side_effects=True, vmem_limit_bytes=50 * 2**20),
    )(grad, small)


def group_norm(values, gain_vec, shift_vec):
    batch_size = values.shape[0]
    grouped = values.reshape(batch_size, PIXELS, -1, C // GROUPS)
    centre = jnp.mean(grouped, axis=(1, 3), keepdims=True)
    spread = jnp.mean(jnp.square(grouped - centre), axis=(1, 3), keepdims=True)
    normal = ((grouped - centre) * lax.rsqrt(spread + 1e-05)).reshape(values.shape)
    return normal * gain_vec + shift_vec


def first_norm(values, gain_vec, shift_vec):
    return jax.nn.silu(group_norm(values, gain_vec, shift_vec))


def middle(conv_values, modulation, gain_vec, shift_vec):
    scaled = (
        group_norm(conv_values, gain_vec, shift_vec) * (1.0 + modulation[:, 0:1])
        + modulation[:, 1:2]
    )
    return jax.nn.silu(scaled)


def windows(source):
    slot_count = source.shape[0]
    padded = jnp.pad(source.reshape(slot_count, SIDE, SIDE, -1), ((0, 0), (1, 1), (1, 1), (0, 0)))
    found = []
    for tap_index in range(9):
        row_shift = tap_index // 3
        col_shift = tap_index % 3
        found.append(
            padded[:, row_shift : row_shift + SIDE, col_shift : col_shift + SIDE].reshape(
                slot_count * PIXELS, -1
            )
        )
    return found


def convolve(source, kernel):
    slot_count = source.shape[0]
    summed = jnp.zeros((slot_count * PIXELS, kernel[0].shape[1]), jnp.float32)
    for tap_index, window in enumerate(windows(source)):
        summed = summed + jnp.dot(window, kernel[tap_index], preferred_element_type=jnp.float32)
    return summed.reshape(slot_count, PIXELS, -1)


def convolve_back(grad_low, kernel):
    slot_count = grad_low.shape[0]
    flattened = grad_low.reshape(slot_count * PIXELS, -1)
    summed = jnp.zeros((slot_count, SIDE + 2, SIDE + 2, kernel[0].shape[0]), jnp.float32)
    for tap_index in range(9):
        row_shift = tap_index // 3
        col_shift = tap_index % 3
        contrib = jnp.einsum(
            "rd,cd->rc", flattened, kernel[tap_index], preferred_element_type=jnp.float32
        )
        contrib = contrib.reshape(slot_count, SIDE, SIDE, -1)
        summed = summed + jnp.pad(
            contrib, ((0, 0), (row_shift, 2 - row_shift), (col_shift, 2 - col_shift), (0, 0))
        )
    return summed[:, 1 : SIDE + 1, 1 : SIDE + 1].reshape(slot_count, PIXELS, -1)


def conv_weight_grad(source, grad_low):
    slot_count = source.shape[0]
    flattened = grad_low.reshape(slot_count * PIXELS, -1)
    found = [
        jnp.einsum("rc,rd->cd", window, flattened, preferred_element_type=jnp.float32)
        for window in windows(source)
    ]
    return found


def gather_features(values_low):
    return lax.all_gather(values_low, "tensor", axis=2, tiled=True)


def back_features(partial_sum):
    return lax.psum_scatter(
        partial_sum.astype(jnp.bfloat16), "tensor", scatter_dimension=2, tiled=True
    ).astype(jnp.float32)


def body(
    fast,
    images,
    embedding,
    counts,
    norm_gains,
    norm_shifts,
    lin_biases,
    conv_weights,
    aff_weights,
    qkv_weights,
    proj_weights,
    cotangent,
):
    slot_count = images.shape[0]
    score_scale = HEAD_DIM ** (-0.5)
    slot_mask = (jnp.arange(slot_count, dtype=jnp.int32) < counts[0]).astype(jnp.float32)
    width = images.shape[2]
    if fast:
        full = gather_weights(conv_weights, aff_weights, qkv_weights, proj_weights).reshape(C, 24, width)
        conv_full = [[full[:, 9 * part + tap] for tap in range(9)] for part in range(2)]
        aff_full, qkv_full, proj_full = full[:, 18:20], full[:, 20:23], full[:, 23]
    else:
        conv_full = lax.all_gather(conv_weights, "dp", axis=2, tiled=True)
        aff_full, qkv_full, proj_full = (
            lax.all_gather(weights, "dp", axis=0, tiled=True)
            for weights in (aff_weights, qkv_weights, proj_weights)
        )
    images_f = images.astype(jnp.float32)
    hidden0 = first_norm(images_f, norm_gains[0], norm_shifts[0]).astype(jnp.bfloat16)
    hidden0_all, embed_all = (
        lax.all_gather(hidden0, "tensor", axis=2, tiled=True),
        lax.all_gather(embedding, "tensor", axis=1, tiled=True),
    )
    conv_out0 = convolve(hidden0_all, conv_full[0]) + lin_biases[0]
    modulation = (
        jnp.einsum("sc,cjd->sjd", embed_all, aff_full, preferred_element_type=jnp.float32)
        + lin_biases[5:7]
    )
    hidden1 = middle(conv_out0, modulation, norm_gains[1], norm_shifts[1]).astype(jnp.bfloat16)
    hidden1_all = gather_features(hidden1)
    residual = images_f + (convolve(hidden1_all, conv_full[1]) + lin_biases[1])
    normed = group_norm(residual, norm_gains[2], norm_shifts[2]).astype(jnp.bfloat16)
    normed_all = gather_features(normed)
    bias_rows = jnp.stack([lin_biases[2], jnp.zeros_like(lin_biases[2]), lin_biases[3]])
    projected = (
        jnp.einsum("spc,cjd->spjd", normed_all, qkv_full, preferred_element_type=jnp.float32)
        + bias_rows
    ).astype(jnp.bfloat16)
    head_shape = (slot_count, PIXELS, -1, HEAD_DIM)
    query_heads = projected[:, :, 0].reshape(head_shape)
    key_heads = projected[:, :, 1].reshape(head_shape)
    value_heads = projected[:, :, 2].reshape(head_shape)
    scores = (
        jnp.einsum("sqhd,skhd->shqk", query_heads, key_heads, preferred_element_type=jnp.float32)
        * score_scale
    )
    log_total = jax.scipy.special.logsumexp(scores, axis=-1, keepdims=True)
    probabilities = jnp.exp(scores - log_total)
    weights_low = probabilities.astype(jnp.bfloat16)
    attended = jnp.einsum(
        "shqk,skhd->sqhd", weights_low, value_heads, preferred_element_type=jnp.float32
    )
    attended = attended.reshape(slot_count, PIXELS, -1).astype(jnp.bfloat16)
    attended_all = gather_features(attended)
    branch = (
        jnp.einsum("spc,cd->spd", attended_all, proj_full, preferred_element_type=jnp.float32)
        + lin_biases[4]
    )
    block_output = (slot_mask[:, None, None] * (residual + branch)).astype(jnp.bfloat16)
    conv_back, aff_back, qkv_back, proj_back = conv_full, aff_full, qkv_full, proj_full
    grad_branch = slot_mask[:, None, None] * cotangent
    branch_low = grad_branch.astype(jnp.bfloat16)
    proj_grad = jnp.einsum(
        "spc,spd->cd", attended_all, branch_low, preferred_element_type=jnp.float32
    )
    proj_bias_grad = jnp.sum(branch_low.astype(jnp.float32), axis=(0, 1))
    attended_grad = back_features(
        jnp.einsum("spd,cd->spc", branch_low, proj_back, preferred_element_type=jnp.float32)
    )
    attended_low = attended_grad.astype(jnp.bfloat16).reshape(head_shape)
    grad_probs = jnp.einsum(
        "sqhd,skhd->shqk", attended_low, value_heads, preferred_element_type=jnp.float32
    )
    value_grad = jnp.einsum(
        "shqk,sqhd->skhd", weights_low, attended_low, preferred_element_type=jnp.float32
    )
    score_grad = probabilities * (
        grad_probs - jnp.sum(grad_probs * probabilities, axis=-1, keepdims=True)
    )
    score_low = score_grad.astype(jnp.bfloat16)
    query_grad = (
        jnp.einsum("shqk,skhd->sqhd", score_low, key_heads, preferred_element_type=jnp.float32)
        * score_scale
    )
    key_grad = (
        jnp.einsum("shqk,sqhd->skhd", score_low, query_heads, preferred_element_type=jnp.float32)
        * score_scale
    )
    flat_shape = (slot_count, PIXELS, -1)
    projected_grad = jnp.stack(
        [
            query_grad.reshape(flat_shape),
            key_grad.reshape(flat_shape),
            value_grad.reshape(flat_shape),
        ],
        axis=2,
    ).astype(jnp.bfloat16)
    qkv_grad = jnp.einsum(
        "spc,spjd->cjd", normed_all, projected_grad, preferred_element_type=jnp.float32
    )
    qkv_bias_grad = jnp.sum(projected_grad.astype(jnp.float32), axis=(0, 1))
    normed_grad = back_features(
        jnp.einsum("spjd,cjd->spc", projected_grad, qkv_back, preferred_element_type=jnp.float32)
    )
    norm_value, norm_pull = jax.vjp(group_norm, residual, norm_gains[2], norm_shifts[2])
    residual_grad, gain2_grad, shift2_grad = norm_pull(normed_grad)
    residual_grad = residual_grad + grad_branch
    conv1_low = residual_grad.astype(jnp.bfloat16)
    conv1_bias_grad = jnp.sum(conv1_low.astype(jnp.float32), axis=(0, 1))
    conv1_wgrad = conv_weight_grad(hidden1_all, conv1_low)
    hidden1_grad = back_features(convolve_back(conv1_low, conv_back[1]))
    middle_value, middle_pull = jax.vjp(
        middle, conv_out0, modulation, norm_gains[1], norm_shifts[1]
    )
    conv0_grad, modulation_grad, gain1_grad, shift1_grad = middle_pull(hidden1_grad)
    modulation_low = modulation_grad.astype(jnp.bfloat16)
    aff_bias_grad = jnp.sum(modulation_low.astype(jnp.float32), axis=0)
    aff_grad = jnp.einsum(
        "sc,sjd->cjd", embed_all, modulation_low, preferred_element_type=jnp.float32
    )
    embed_part = jnp.einsum(
        "sjd,cjd->sc", modulation_low, aff_back, preferred_element_type=jnp.float32
    )
    conv0_low = conv0_grad.astype(jnp.bfloat16)
    conv0_bias_grad = jnp.sum(conv0_low.astype(jnp.float32), axis=(0, 1))
    conv0_wgrad = conv_weight_grad(hidden0_all, conv0_low)
    hidden0_part = convolve_back(conv0_low, conv_back[0])
    hidden0_grad, embedding_sum = (
        lax.psum_scatter(
            hidden0_part.astype(jnp.bfloat16), "tensor", scatter_dimension=2, tiled=True
        ).astype(jnp.float32),
        lax.psum_scatter(
            embed_part.astype(jnp.bfloat16), "tensor", scatter_dimension=1, tiled=True
        ).astype(jnp.float32),
    )
    first_value, first_pull = jax.vjp(first_norm, images_f, norm_gains[0], norm_shifts[0])
    images_part, gain0_grad, shift0_grad = first_pull(hidden0_grad)
    images_grad = (images_part + residual_grad).astype(jnp.bfloat16)
    gains_local = jnp.stack([gain0_grad, gain1_grad, gain2_grad])
    shifts_local = jnp.stack([shift0_grad, shift1_grad, shift2_grad])
    biases_local = jnp.stack(
        [
            conv0_bias_grad,
            conv1_bias_grad,
            qkv_bias_grad[0],
            qkv_bias_grad[2],
            proj_bias_grad,
            aff_bias_grad[0],
            aff_bias_grad[1],
        ]
    )
    if fast:
        small = jnp.concatenate([gains_local, shifts_local, biases_local, jnp.zeros((3, width), jnp.float32)])
        parts = conv0_wgrad + conv1_wgrad + [aff_grad.reshape(C, -1), qkv_grad.reshape(C, -1), proj_grad]
        joined = jnp.concatenate([part.astype(jnp.bfloat16) for part in parts], axis=1)
        rows = conv_weights.shape[2]
        summed, totals = scatter_grads(joined.reshape(GRID + (rows, 24 * width)), small)
        gains_grad, shifts_grad, biases_grad = totals[:3], totals[3:6], totals[6:13]
        split = summed.reshape(rows, 24, width)
        conv_summed = split[:, :18].transpose(1, 0, 2).reshape(2, 9, rows, width)
        aff_summed, qkv_summed, proj_summed = split[:, 18:20], split[:, 20:23], split[:, 23]
    else:
        gains_grad, shifts_grad, biases_grad = lax.psum((gains_local, shifts_local, biases_local), "dp")
        conv_local = jnp.stack([jnp.stack(conv0_wgrad), jnp.stack(conv1_wgrad)])
        conv_summed, aff_summed, qkv_summed, proj_summed = (
            lax.psum_scatter(conv_local, "dp", scatter_dimension=2, tiled=True),
            lax.psum_scatter(aff_grad, "dp", scatter_dimension=0, tiled=True),
            lax.psum_scatter(qkv_grad, "dp", scatter_dimension=0, tiled=True),
            lax.psum_scatter(proj_grad, "dp", scatter_dimension=0, tiled=True),
        )
    return (
        block_output,
        images_grad,
        embedding_sum.astype(jnp.bfloat16),
        gains_grad,
        shifts_grad,
        biases_grad,
        conv_summed,
        aff_summed,
        qkv_summed,
        proj_summed,
    )


def solution(mesh):
    return jax.shard_map(
        functools.partial(body, mesh.shape["dp"] == 16),
        mesh=mesh,
        in_specs=(
            P("dp", None, "tensor"),
            P("dp", "tensor"),
            P("dp"),
            P(None, "tensor"),
            P(None, "tensor"),
            P(None, "tensor"),
            P(None, None, "dp", "tensor"),
            P("dp", None, "tensor"),
            P("dp", None, "tensor"),
            P("dp", "tensor"),
            P("dp", None, "tensor"),
        ),
        out_specs=(
            P("dp", None, "tensor"),
            P("dp", None, "tensor"),
            P("dp", "tensor"),
            P(None, "tensor"),
            P(None, "tensor"),
            P(None, "tensor"),
            P(None, None, "dp", "tensor"),
            P("dp", None, "tensor"),
            P("dp", None, "tensor"),
            P("dp", "tensor"),
        ),
        check_vma=False,
    )
```

```python
import jax
import jax.numpy as jnp
from jax import lax
from jax.experimental import pallas as pl
from jax.experimental.pallas import tpu as pltpu
from jax.sharding import PartitionSpec as P

C = 768
HEAD_DIM = 64
GROUPS = 32
SIDE = 8
PIXELS = 64
GROUP_SIZE = C // GROUPS
LOW = jnp.bfloat16
MESH = pl.DeviceIdType.MESH
NT = (((1,), (1,)), ((), ()))
TN = (((0,), (0,)), ((), ()))
GRID = (4, 2, 2)


def group_norm(values, gain_vec, shift_vec):
    batch_size = values.shape[0]
    grouped = values.reshape(batch_size, PIXELS, -1, C // GROUPS)
    centre = jnp.mean(grouped, axis=(1, 3), keepdims=True)
    spread = jnp.mean(jnp.square(grouped - centre), axis=(1, 3), keepdims=True)
    normal = ((grouped - centre) * lax.rsqrt(spread + 1e-05)).reshape(values.shape)
    return normal * gain_vec + shift_vec


def first_norm(values, gain_vec, shift_vec):
    return jax.nn.silu(group_norm(values, gain_vec, shift_vec))


def middle(conv_values, modulation, gain_vec, shift_vec):
    scaled = (
        group_norm(conv_values, gain_vec, shift_vec) * (1.0 + modulation[:, 0:1])
        + modulation[:, 1:2]
    )
    return jax.nn.silu(scaled)


def windows(source):
    slot_count = source.shape[0]
    padded = jnp.pad(source.reshape(slot_count, SIDE, SIDE, -1), ((0, 0), (1, 1), (1, 1), (0, 0)))
    found = []
    for tap_index in range(9):
        row_shift = tap_index // 3
        col_shift = tap_index % 3
        found.append(
            padded[:, row_shift : row_shift + SIDE, col_shift : col_shift + SIDE].reshape(
                slot_count * PIXELS, -1
            )
        )
    return found


def convolve(source, kernel):
    slot_count = source.shape[0]
    summed = jnp.zeros((slot_count * PIXELS, kernel.shape[2]), jnp.float32)
    for tap_index, window in enumerate(windows(source)):
        summed = summed + jnp.dot(window, kernel[tap_index], preferred_element_type=jnp.float32)
    return summed.reshape(slot_count, PIXELS, -1)


def convolve_back(grad_low, kernel):
    slot_count = grad_low.shape[0]
    flattened = grad_low.reshape(slot_count * PIXELS, -1)
    summed = jnp.zeros((slot_count, SIDE + 2, SIDE + 2, kernel.shape[1]), jnp.float32)
    for tap_index in range(9):
        row_shift = tap_index // 3
        col_shift = tap_index % 3
        contrib = jnp.einsum(
            "rd,cd->rc", flattened, kernel[tap_index], preferred_element_type=jnp.float32
        )
        contrib = contrib.reshape(slot_count, SIDE, SIDE, -1)
        summed = summed + jnp.pad(
            contrib, ((0, 0), (row_shift, 2 - row_shift), (col_shift, 2 - col_shift), (0, 0))
        )
    return summed[:, 1 : SIDE + 1, 1 : SIDE + 1].reshape(slot_count, PIXELS, -1)


def conv_weight_grad(source, grad_low):
    slot_count = source.shape[0]
    flattened = grad_low.reshape(slot_count * PIXELS, -1)
    found = [
        jnp.einsum("rc,rd->cd", window, flattened, preferred_element_type=jnp.float32)
        for window in windows(source)
    ]
    return jnp.stack(found)


def gather_features(values_low):
    return lax.all_gather(values_low, "tensor", axis=2, tiled=True)


def back_features(partial_sum):
    return lax.psum_scatter(
        partial_sum.astype(jnp.bfloat16), "tensor", scatter_dimension=2, tiled=True
    ).astype(jnp.float32)


def body(
    images,
    embedding,
    counts,
    norm_gains,
    norm_shifts,
    lin_biases,
    conv_weights,
    aff_weights,
    qkv_weights,
    proj_weights,
    cotangent,
):
    slot_count = images.shape[0]
    score_scale = HEAD_DIM ** (-0.5)
    slot_mask = (jnp.arange(slot_count, dtype=jnp.int32) < counts[0]).astype(jnp.float32)
    conv_full = lax.all_gather(conv_weights, "dp", axis=2, tiled=True)
    aff_full, qkv_full, proj_full = (
        lax.all_gather(aff_weights, "dp", axis=0, tiled=True),
        lax.all_gather(qkv_weights, "dp", axis=0, tiled=True),
        lax.all_gather(proj_weights, "dp", axis=0, tiled=True),
    )
    images_f = images.astype(jnp.float32)
    hidden0 = first_norm(images_f, norm_gains[0], norm_shifts[0]).astype(jnp.bfloat16)
    hidden0_all, embed_all = (
        lax.all_gather(hidden0, "tensor", axis=2, tiled=True),
        lax.all_gather(embedding, "tensor", axis=1, tiled=True),
    )
    conv_out0 = convolve(hidden0_all, conv_full[0]) + lin_biases[0]
    modulation = (
        jnp.einsum("sc,cjd->sjd", embed_all, aff_full, preferred_element_type=jnp.float32)
        + lin_biases[5:7]
    )
    hidden1 = middle(conv_out0, modulation, norm_gains[1], norm_shifts[1]).astype(jnp.bfloat16)
    hidden1_all = gather_features(hidden1)
    residual = images_f + (convolve(hidden1_all, conv_full[1]) + lin_biases[1])
    normed = group_norm(residual, norm_gains[2], norm_shifts[2]).astype(jnp.bfloat16)
    normed_all = gather_features(normed)
    bias_rows = jnp.stack([lin_biases[2], jnp.zeros_like(lin_biases[2]), lin_biases[3]])
    projected = (
        jnp.einsum("spc,cjd->spjd", normed_all, qkv_full, preferred_element_type=jnp.float32)
        + bias_rows
    ).astype(jnp.bfloat16)
    head_shape = (slot_count, PIXELS, -1, HEAD_DIM)
    query_heads = projected[:, :, 0].reshape(head_shape)
    key_heads = projected[:, :, 1].reshape(head_shape)
    value_heads = projected[:, :, 2].reshape(head_shape)
    scores = (
        jnp.einsum("sqhd,skhd->shqk", query_heads, key_heads, preferred_element_type=jnp.float32)
        * score_scale
    )
    log_total = jax.scipy.special.logsumexp(scores, axis=-1, keepdims=True)
    probabilities = jnp.exp(scores - log_total)
    weights_low = probabilities.astype(jnp.bfloat16)
    attended = jnp.einsum(
        "shqk,skhd->sqhd", weights_low, value_heads, preferred_element_type=jnp.float32
    )
    attended = attended.reshape(slot_count, PIXELS, -1).astype(jnp.bfloat16)
    attended_all = gather_features(attended)
    branch = (
        jnp.einsum("spc,cd->spd", attended_all, proj_full, preferred_element_type=jnp.float32)
        + lin_biases[4]
    )
    block_output = (slot_mask[:, None, None] * (residual + branch)).astype(jnp.bfloat16)
    conv_back = lax.all_gather(conv_weights, "dp", axis=2, tiled=True)
    aff_back, qkv_back, proj_back = (
        lax.all_gather(aff_weights, "dp", axis=0, tiled=True),
        lax.all_gather(qkv_weights, "dp", axis=0, tiled=True),
        lax.all_gather(proj_weights, "dp", axis=0, tiled=True),
    )
    grad_branch = slot_mask[:, None, None] * cotangent
    branch_low = grad_branch.astype(jnp.bfloat16)
    proj_grad = jnp.einsum(
        "spc,spd->cd", attended_all, branch_low, preferred_element_type=jnp.float32
    )
    proj_bias_grad = jnp.sum(branch_low.astype(jnp.float32), axis=(0, 1))
    attended_grad = back_features(
        jnp.einsum("spd,cd->spc", branch_low, proj_back, preferred_element_type=jnp.float32)
    )
    attended_low = attended_grad.astype(jnp.bfloat16).reshape(head_shape)
    grad_probs = jnp.einsum(
        "sqhd,skhd->shqk", attended_low, value_heads, preferred_element_type=jnp.float32
    )
    value_grad = jnp.einsum(
        "shqk,sqhd->skhd", weights_low, attended_low, preferred_element_type=jnp.float32
    )
    score_grad = probabilities * (
        grad_probs - jnp.sum(grad_probs * probabilities, axis=-1, keepdims=True)
    )
    score_low = score_grad.astype(jnp.bfloat16)
    query_grad = (
        jnp.einsum("shqk,skhd->sqhd", score_low, key_heads, preferred_element_type=jnp.float32)
        * score_scale
    )
    key_grad = (
        jnp.einsum("shqk,sqhd->skhd", score_low, query_heads, preferred_element_type=jnp.float32)
        * score_scale
    )
    flat_shape = (slot_count, PIXELS, -1)
    projected_grad = jnp.stack(
        [
            query_grad.reshape(flat_shape),
            key_grad.reshape(flat_shape),
            value_grad.reshape(flat_shape),
        ],
        axis=2,
    ).astype(jnp.bfloat16)
    qkv_grad = jnp.einsum(
        "spc,spjd->cjd", normed_all, projected_grad, preferred_element_type=jnp.float32
    )
    qkv_bias_grad = jnp.sum(projected_grad.astype(jnp.float32), axis=(0, 1))
    normed_grad = back_features(
        jnp.einsum("spjd,cjd->spc", projected_grad, qkv_back, preferred_element_type=jnp.float32)
    )
    norm_value, norm_pull = jax.vjp(group_norm, residual, norm_gains[2], norm_shifts[2])
    residual_grad, gain2_grad, shift2_grad = norm_pull(normed_grad)
    residual_grad = residual_grad + grad_branch
    conv1_low = residual_grad.astype(jnp.bfloat16)
    conv1_bias_grad = jnp.sum(conv1_low.astype(jnp.float32), axis=(0, 1))
    conv1_wgrad = conv_weight_grad(hidden1_all, conv1_low)
    hidden1_grad = back_features(convolve_back(conv1_low, conv_back[1]))
    middle_value, middle_pull = jax.vjp(
        middle, conv_out0, modulation, norm_gains[1], norm_shifts[1]
    )
    conv0_grad, modulation_grad, gain1_grad, shift1_grad = middle_pull(hidden1_grad)
    modulation_low = modulation_grad.astype(jnp.bfloat16)
    aff_bias_grad = jnp.sum(modulation_low.astype(jnp.float32), axis=0)
    aff_grad = jnp.einsum(
        "sc,sjd->cjd", embed_all, modulation_low, preferred_element_type=jnp.float32
    )
    embed_part = jnp.einsum(
        "sjd,cjd->sc", modulation_low, aff_back, preferred_element_type=jnp.float32
    )
    conv0_low = conv0_grad.astype(jnp.bfloat16)
    conv0_bias_grad = jnp.sum(conv0_low.astype(jnp.float32), axis=(0, 1))
    conv0_wgrad = conv_weight_grad(hidden0_all, conv0_low)
    hidden0_part = convolve_back(conv0_low, conv_back[0])
    hidden0_grad, embedding_sum = (
        lax.psum_scatter(
            hidden0_part.astype(jnp.bfloat16), "tensor", scatter_dimension=2, tiled=True
        ).astype(jnp.float32),
        lax.psum_scatter(
            embed_part.astype(jnp.bfloat16), "tensor", scatter_dimension=1, tiled=True
        ).astype(jnp.float32),
    )
    first_value, first_pull = jax.vjp(first_norm, images_f, norm_gains[0], norm_shifts[0])
    images_part, gain0_grad, shift0_grad = first_pull(hidden0_grad)
    images_grad = (images_part + residual_grad).astype(jnp.bfloat16)
    gains_local = jnp.stack([gain0_grad, gain1_grad, gain2_grad])
    shifts_local = jnp.stack([shift0_grad, shift1_grad, shift2_grad])
    biases_local = jnp.stack(
        [
            conv0_bias_grad,
            conv1_bias_grad,
            qkv_bias_grad[0],
            qkv_bias_grad[2],
            proj_bias_grad,
            aff_bias_grad[0],
            aff_bias_grad[1],
        ]
    )
    gains_grad, shifts_grad, biases_grad = lax.psum((gains_local, shifts_local, biases_local), "dp")
    conv_local = jnp.stack([conv0_wgrad, conv1_wgrad])
    conv_summed, aff_summed, qkv_summed, proj_summed = (
        lax.psum_scatter(conv_local, "dp", scatter_dimension=2, tiled=True),
        lax.psum_scatter(aff_grad, "dp", scatter_dimension=0, tiled=True),
        lax.psum_scatter(qkv_grad, "dp", scatter_dimension=0, tiled=True),
        lax.psum_scatter(proj_grad, "dp", scatter_dimension=0, tiled=True),
    )
    return (
        block_output,
        images_grad,
        embedding_sum.astype(jnp.bfloat16),
        gains_grad,
        shifts_grad,
        biases_grad,
        conv_summed,
        aff_summed,
        qkv_summed,
        proj_summed,
    )


def dot(left, right, dims=(((1,), (0,)), ((), ()))):
    return lax.dot_general(left, right, dims, preferred_element_type=jnp.float32)


def place():
    spot = lax.axis_index("dp")
    return spot, spot // 4, lax.rem(spot // 2, 2), lax.rem(spot, 2)


def halves(start, size):
    first = (size // 128 + 1) // 2 * 128
    return [(start, first, 0), (start + first, size - first, 1)]


def remote(src, dst, send, recv, device):
    copy = pltpu.make_async_remote_copy(
        src_ref=src, dst_ref=dst, send_sem=send, recv_sem=recv, device_id=device, device_id_type=MESH
    )
    copy.start()
    return copy


def group_average(width):
    row = lax.broadcasted_iota(jnp.int32, (width, width), 0) // GROUP_SIZE
    col = lax.broadcasted_iota(jnp.int32, (width, width), 1) // GROUP_SIZE
    return jnp.where(row == col, 1.0 / (GROUP_SIZE * PIXELS), 0.0).astype(jnp.float32)


def group_mean(values, average):
    return lax.dot_general(
        jnp.sum(values, axis=1), average, (((1,), (0,)), ((), ())),
        precision=lax.Precision.HIGHEST, preferred_element_type=jnp.float32,
    )


def normalize(values, average):
    away = values - group_mean(values, average)[:, None]
    scale = lax.rsqrt(group_mean(away * away, average) + 1e-05)
    return away * scale[:, None], scale


def normalize_back(grad, normal, scale, average):
    return scale[:, None] * (
        grad - group_mean(grad, average)[:, None] - normal * group_mean(grad * normal, average)[:, None]
    )


def sigmoid(values):
    return 1.0 / (1.0 + jnp.exp(-values))


def silu_slope(values):
    gate = sigmoid(values)
    return gate * (1.0 + values * (1.0 - gate))


def shift_columns(values, step):
    moved = pltpu.roll(values, step % SIDE, 1)
    column = lax.broadcasted_iota(jnp.int32, values.shape, 1)
    return jnp.where(column == (0 if step == 1 else SIDE - 1), 0.0, moved)


def shift_rows(values, step):
    if step == 0:
        return values
    zero = jnp.zeros_like(values[:, :1])
    if step == 1:
        return jnp.concatenate([zero, values[:, : SIDE - 1]], axis=1)
    return jnp.concatenate([values[:, 1:], zero], axis=1)


def both(ref):
    return jnp.concatenate([ref[0], ref[1]], axis=1)


def convolve_row(source, weights, row_tap, sums):
    rows, width = sums.shape[1:]
    products = dot(source, weights)
    for col_tap in range(3):
        part = products[:, col_tap * width : (col_tap + 1) * width]
        part = shift_rows(part.reshape(-1, SIDE, SIDE, width), 1 - row_tap).reshape(rows, width)
        sums[col_tap] = part if row_tap == 0 else sums[col_tap] + part


def convolve_end(sums):
    rows, width = sums.shape[1:]
    grids = [sums[col_tap].reshape(rows // SIDE, SIDE, width) for col_tap in range(3)]
    return (shift_columns(grids[0], 1) + grids[1] + shift_columns(grids[2], -1)).reshape(rows, width)


def spread_taps(grad, taps_ref):
    rows, width = grad.shape
    flat = grad.reshape(rows // SIDE, SIDE, width)
    for col_tap, grid in enumerate((shift_columns(flat, -1), flat, shift_columns(flat, 1))):
        for row_tap in range(3):
            moved = shift_rows(grid.reshape(-1, SIDE, SIDE, width), row_tap - 1)
            tap = row_tap * 3 + col_tap
            taps_ref[:, tap * width : (tap + 1) * width] = moved.reshape(rows, width).astype(LOW)


def expand_heads(block, lane_head, heads):
    return jnp.concatenate([jnp.where(lane_head == h, block, jnp.zeros_like(block)) for h in range(heads)], axis=0)


def contract_heads(wide, lane_head, heads):
    total = wide[:PIXELS]
    for h in range(1, heads):
        total = jnp.where(lane_head == h, wide[h * PIXELS : (h + 1) * PIXELS], total)
    return total


def attention(slots, projected, attended_grad, attended, projected_grad):
    width = attended.shape[1]
    heads = width // HEAD_DIM
    scale = HEAD_DIM ** (-0.5)
    lane_head = lax.broadcasted_iota(jnp.int32, (PIXELS, width), 1) // HEAD_DIM

    def one_slot(slot, carry):
        rows = pl.ds(pl.multiple_of(slot * PIXELS, PIXELS), PIXELS)
        query, key, value = (projected[rows, part * width : (part + 1) * width] for part in range(3))
        query_wide = expand_heads(query, lane_head, heads)
        scores = dot(query_wide, key, NT) * scale
        powers = jnp.exp(scores - jnp.max(scores, axis=1, keepdims=True))
        probabilities = powers / jnp.sum(powers, axis=1, keepdims=True)
        weights_low = probabilities.astype(LOW)
        attended[rows, :] = contract_heads(dot(weights_low, value), lane_head, heads).astype(LOW)
        grad_wide = expand_heads(attended_grad[rows, :], lane_head, heads)
        grad_probs = dot(grad_wide, value, NT)
        value_grad = dot(weights_low, grad_wide, TN)
        score_low = (
            probabilities * (grad_probs - jnp.sum(grad_probs * probabilities, axis=1, keepdims=True))
        ).astype(LOW)
        query_grad = contract_heads(dot(score_low, key), lane_head, heads) * scale
        key_grad = dot(score_low, query_wide, TN) * scale
        for part, grad in enumerate((query_grad, key_grad, value_grad)):
            projected_grad[rows, part * width : (part + 1) * width] = grad.astype(LOW)
        return carry

    lax.fori_loop(0, slots, one_slot, 0, unroll=2)


CONV0, AFF, PROJ, CONV1, QKV = 0, 9, 11, 12, 21


def forward_kernel(
    img, emb, par, cot, mask, conv, aff, qkv, proj,
    full_out, hall0, hall1, nall, attended, residual, normal1, scale1, modulation, normal2, scale2, pgrad, emb_all,
    full, sums, projected, ag_own, ag_send, ag_recv, ag_low,
    own_sem, zsend, zrecv, fsend, frecv, ssend, srecv, mate_send, mate_recv, out_sem,
):
    spot, z, y, x = place()
    core = lax.axis_index("tensor")
    width = img.shape[1]
    slots = mask.shape[0]
    shape = (slots, PIXELS, width)
    mate = {"tensor": 1 - core}
    line = [lax.rem(z + j, 4) * 4 + y * 2 + x for j in (1, 2, 3)]
    xmate, ymate = z * 4 + y * 2 + 1 - x, z * 4 + (1 - y) * 2 + x
    barrier = pltpu.get_barrier_semaphore()
    for device in [{"dp": other} for other in line + [xmate, ymate]] + [mate]:
        pl.semaphore_signal(barrier, inc=1, device_id=device, device_id_type=MESH)
    own = []
    for tap in range(18):
        column = (CONV0 + tap if tap < 9 else CONV1 + tap - 9) * width
        own.append((conv.at[tap // 9, tap % 9], column, width))
    own += [(aff, AFF * width, 2 * width), (proj, PROJ * width, width), (qkv, QKV * width, 3 * width)]
    own = [
        pltpu.make_async_copy(ref, full.at[z, y, x, :, pl.ds(column, size)], own_sem.at[at])
        for at, (ref, column, size) in enumerate(own)
    ]
    for copy in own:
        copy.start()

    started = {}
    group_count = 8
    group_width = 3 * width

    def stage(group, s):
        if not 0 <= group < group_count:
            return
        for start, size, odd in halves(group * group_width, group_width):
            cols = pl.ds(start, size)
            for copy in started.get((group, odd, s - 1), []):
                copy.wait_recv()
            copies = []
            if s == 0:
                block = full.at[z, y, x, :, cols]
                copies = [
                    remote(block, block, zsend.at[group, odd, j], zrecv.at[group, odd, j], {"dp": line[j]})
                    for j in range(3)
                ]
            elif s == 1:
                block = full.at[:, y, x, :, cols]
                first = ymate if odd else xmate
                copies = [remote(block, block, fsend.at[group, odd], frecv.at[group, odd], {"dp": first})]
            elif s == 2:
                block = full.at[:, :, x, :, cols] if odd else full.at[:, y, :, :, cols]
                second = xmate if odd else ymate
                copies = [remote(block, block, ssend.at[group, odd], srecv.at[group, odd], {"dp": second})]
            started[group, odd, s] = copies

    mate_copies = []

    def to_mate(src, dst):
        at = len(mate_copies)
        copy = remote(src, dst, mate_send.at[at], mate_recv.at[at], mate)
        mate_copies.append(copy)
        return copy

    def weights(column, count, part=None):
        block = full[:, :, :, :, pl.ds(column * width, count * width)] if part is None else full[pl.ds(2 * part, 2), :, :, :, pl.ds(column * width, count * width)]
        return block.reshape(-1, count * width)

    out_copies = []

    def keep(column, count):
        cols = pl.ds(column * width, count * width)
        copy = pltpu.make_async_copy(full.at[:, :, :, :, cols], full_out.at[:, :, :, :, cols], out_sem.at[len(out_copies)])
        copy.start()
        out_copies.append(copy)

    for copy in own:
        copy.wait()
    pl.semaphore_wait(barrier, 6)
    stage(0, 0)
    stage(1, 0)
    average = group_average(width)
    emb_all[core] = emb[...]
    normal0, _ = normalize(img[...].astype(jnp.float32).reshape(shape), average)
    scaled = normal0 * par[0:1] + par[3:4]
    hall0[core] = (scaled * sigmoid(scaled)).reshape(-1, width).astype(LOW)
    emb_copy = to_mate(emb_all.at[core], emb_all.at[core])
    hidden0_copy = to_mate(hall0.at[core], hall0.at[core])

    for step in range(1, group_count + 3):
        stage(step + 1, 0)
        stage(step - 3, 3)
        stage(step - 2, 2)
        stage(step - 1, 1)
        group = step - 3
        if group < 0:
            continue
        keep(group * 3, 3)
        if group < 3:
            if group == 0:
                hidden0_copy.wait_recv()
            convolve_row(both(hall0), weights(CONV0 + 3 * group, 3), group, sums)
        elif group == 3:
            emb_copy.wait_recv()
            changes = dot(both(emb_all), weights(AFF, 2)) + jnp.concatenate([par[11:12], par[12:13]], axis=1)
            modulation[...] = changes
            conv_out0 = (convolve_end(sums) + par[6:7]).reshape(shape)
            normal, scale = normalize(conv_out0, average)
            normal1[...] = normal.reshape(-1, width)
            scale1[...] = scale
            scaled = (normal * par[1:2] + par[4:5]) * (1.0 + changes[:slots, None, :width]) + changes[:slots, None, width:]
            hall1[core] = (scaled * sigmoid(scaled)).reshape(-1, width).astype(LOW)
            hidden1_copy = to_mate(hall1.at[core], hall1.at[core])
            branch_low = (mask[...][:, None] * cot[...].reshape(shape)).reshape(-1, width).astype(LOW)
            ag_send[...] = dot(branch_low, weights(PROJ, 1, 1 - core), NT).astype(LOW)
            ag_copy = to_mate(ag_send, ag_recv)
            ag_own[...] = dot(branch_low, weights(PROJ, 1, core), NT)
        elif group < 7:
            if group == 4:
                hidden1_copy.wait_recv()
            if group == 5:
                ag_copy.wait_recv()
                ag_low[...] = (ag_own[...] + ag_recv[...].astype(jnp.float32)).astype(LOW)
            convolve_row(both(hall1), weights(CONV1 + 3 * (group - 4), 3), group - 4, sums)
            if group == 6:
                total = img[...].astype(jnp.float32) + (convolve_end(sums) + par[7:8])
                residual[...] = total
                normal, scale = normalize(total.reshape(shape), average)
                normal2[...] = normal.reshape(-1, width)
                scale2[...] = scale
                nall[core] = (normal * par[2:3] + par[5:6]).reshape(-1, width).astype(LOW)
                normed_copy = to_mate(nall.at[core], nall.at[core])
        else:
            normed_copy.wait_recv()
            bias = jnp.concatenate([par[8:9], jnp.zeros((1, width), jnp.float32), par[9:10]], axis=1)
            projected[...] = (dot(both(nall), weights(QKV, 3)) + bias).astype(LOW)
            attention(slots, projected, ag_low, attended, pgrad)
    for copies in list(started.values()) + [mate_copies]:
        for copy in copies:
            copy.wait_send()
    for copy in out_copies:
        copy.wait()


def backward_kernel(
    img, par, cot, mask, hall0, hall1, nall, attended, residual, normal1, scale1, modulation, normal2, scale2, pgrad,
    emb_all, full,
    block_out, img_grad, emb_grad, totals, conv_grad, aff_grad, qkv_grad, proj_grad,
    work, r1, r2, r3, wbuf, qbuf, abuf, taps, aall, rgrad, own_half, mate_out, mate_in, emb_out, emb_in, low_buf, small, smalls,
    load_sem, sem1, sem2, sem3, small_sem, mate_send, mate_recv,
):
    spot, z, y, x = place()
    core = lax.axis_index("tensor")
    width = img.shape[1]
    slots = mask.shape[0]
    shape = (slots, PIXELS, width)
    mate = {"tensor": 1 - core}
    line = [lax.rem(z + j, 4) for j in (1, 2, 3)]
    everyone = [lax.rem(spot + j, 16) for j in range(1, 16)]
    xmate, ymate = z * 4 + y * 2 + 1 - x, z * 4 + (1 - y) * 2 + x
    barrier = pltpu.get_barrier_semaphore()
    for device in [{"dp": other} for other in everyone] + [mate]:
        pl.semaphore_signal(barrier, inc=1, device_id=device, device_id_type=MESH)

    loads = []

    def load(column, count, dst):
        copy = pltpu.make_async_copy(full.at[:, :, :, :, pl.ds(column * width, count * width)], dst, load_sem.at[len(loads)])
        copy.start()
        loads.append(copy)
        return copy

    qkv_load = load(QKV, 3, qbuf)
    conv1_load = load(CONV1, 9, wbuf)
    aff_load = load(AFF, 3, abuf)

    mate_copies = []

    def to_mate(src, dst):
        at = len(mate_copies)
        copy = remote(src, dst, mate_send.at[at], mate_recv.at[at], mate)
        mate_copies.append(copy)
        return copy

    groups = [(QKV, 3), (PROJ, 1), (CONV1, 3), (CONV1 + 3, 3), (CONV1 + 6, 3), (CONV0, 3), (CONV0 + 3, 3), (CONV0 + 6, 3), (AFF, 2)]
    started = {}

    def deliver(start, size, value):
        column, offset = start // width, start % width
        while size:
            now = min(size, width - offset)
            part, value = value[:, :now], value[:, now:]
            if column < AFF or CONV1 <= column < QKV:
                tap = column if column < AFF else column - CONV1 + 9
                conv_grad[tap // 9, tap % 9, :, offset : offset + now] = part
            else:
                ref, first = (aff_grad, AFF) if column < PROJ else (proj_grad, PROJ) if column < CONV1 else (qkv_grad, QKV)
                at = (column - first) * width + offset
                ref[:, at : at + now] = part
            column, offset, size = column + 1, 0, size - now

    def stage(group, s):
        if not 0 <= group < len(groups):
            return
        column, count = groups[group]
        for start, size, odd in halves(column * width, count * width):
            cols = pl.ds(start, size)
            for copy in started.get((group, odd, s - 1), []):
                copy.wait_recv()
            copies = []
            if s == 0:
                block = work.at[:, 1 - y, :, :, cols] if odd else work.at[:, :, 1 - x, :, cols]
                copies = [remote(block, r1.at[:, :, :, cols], sem1.at[0, group, odd], sem1.at[1, group, odd], {"dp": ymate if odd else xmate})]
            elif s == 1:
                for zz in range(4):
                    for other in range(2):
                        at = (zz, y, other) if odd else (zz, other, x)
                        total = work[at + (slice(None), cols)].astype(jnp.float32) + r1[zz, other, :, cols].astype(jnp.float32)
                        work[at + (slice(None), cols)] = total.astype(LOW)
                block = work.at[:, y, 1 - x, :, cols] if odd else work.at[:, 1 - y, x, :, cols]
                copies = [remote(block, r2.at[:, :, cols], sem2.at[0, group, odd], sem2.at[1, group, odd], {"dp": xmate if odd else ymate})]
            elif s == 2:
                for zz in range(4):
                    total = work[zz, y, x, :, cols].astype(jnp.float32) + r2[zz, :, cols].astype(jnp.float32)
                    work[zz, y, x, :, cols] = total.astype(LOW)
                copies = [
                    remote(work.at[zz, y, x, :, cols], r3.at[j, :, cols], sem3.at[0, group, odd, j], sem3.at[1, group, odd, j], {"dp": zz * 4 + y * 2 + x})
                    for j, zz in enumerate(line)
                ]
            else:
                total = work[z, y, x, :, cols].astype(jnp.float32)
                for j in range(3):
                    total = total + r3[j, :, cols].astype(jnp.float32)
                deliver(start, size, total)
            started[group, odd, s] = copies

    def weight_grad(column, count, source, grad):
        for part in range(2):
            product = dot(source[part], grad, TN).astype(LOW)
            work[2 * part : 2 * part + 2, :, :, :, pl.ds(column * width, count * width)] = product.reshape(2, 2, 2, -1, count * width)

    def channels(ref, part, size):
        return ref[pl.ds(2 * part, 2)].reshape(-1, size)

    def column_sum(values):
        return jnp.sum(values.reshape(-1, values.shape[-1]), axis=0, keepdims=True)

    average = group_average(width)
    small[...] = jnp.zeros_like(small)
    aall[core] = attended[...]
    pl.semaphore_wait(barrier, 16)
    attended_copy = to_mate(aall.at[core], aall.at[core])
    qkv_load.wait()
    mate_out[0] = dot(pgrad[...], channels(qbuf, 1 - core, 3 * width), NT).astype(LOW)
    normed_copy = to_mate(mate_out.at[0], mate_in.at[0])
    weight_grad(QKV, 3, nall, pgrad[...])
    stage(0, 0)
    normed_grad = dot(pgrad[...], channels(qbuf, core, 3 * width), NT)
    grad_branch = mask[...][:, None] * cot[...].reshape(shape)
    branch_low = grad_branch.reshape(-1, width).astype(LOW)
    low_buf[...] = branch_low
    attended_copy.wait_recv()
    weight_grad(PROJ, 1, aall, low_buf[...])
    stage(1, 0)
    small[10:11] = column_sum(branch_low.astype(jnp.float32))
    small[8:9] = column_sum(pgrad[:, :width].astype(jnp.float32))
    small[9:10] = column_sum(pgrad[:, 2 * width :].astype(jnp.float32))
    normed_copy.wait_recv()
    normed_grad = (normed_grad + mate_in[0].astype(jnp.float32)).reshape(shape)
    normal = normal2[...].reshape(shape)
    small[2:3] = column_sum(normed_grad * normal)
    small[5:6] = column_sum(normed_grad)
    residual_grad = grad_branch + normalize_back(normed_grad * par[2:3], normal, scale2[...], average)
    rgrad[...] = residual_grad.reshape(-1, width)
    conv1_low = rgrad[...].astype(LOW).astype(jnp.float32)
    small[7:8] = column_sum(conv1_low)
    spread_taps(conv1_low, taps)
    conv1_load.wait()
    mate_out[1] = dot(taps[...], channels(wbuf, 1 - core, 9 * width), NT).astype(LOW)
    hidden1_copy = to_mate(mate_out.at[1], mate_in.at[1])
    for part in range(3):
        weight_grad(CONV1 + 3 * part, 3, hall1, taps[:, pl.ds(part * 3 * width, 3 * width)])
        stage(2 + part, 0)
        if part == 0:
            stage(0, 1)
            stage(1, 1)
    own_half[...] = dot(taps[...], channels(wbuf, core, 9 * width), NT)
    conv0_load = load(CONV0, 9, wbuf)
    hidden1_copy.wait_recv()
    hidden1_grad = (own_half[...] + mate_in[1].astype(jnp.float32)).reshape(shape)
    normal = normal1[...].reshape(shape)
    change = 1.0 + modulation[...][:slots, None, :width]
    inner = normal * par[1:2] + par[4:5]
    grad = hidden1_grad * silu_slope(inner * change + modulation[...][:slots, None, width:])
    modulation_grad = jnp.concatenate([jnp.sum(grad * inner, axis=1), jnp.sum(grad, axis=1)], axis=1)
    grad = grad * change
    small[1:2] = column_sum(grad * normal)
    small[4:5] = column_sum(grad)
    conv0_low = normalize_back(grad * par[1:2], normal, scale1[...], average).astype(LOW).astype(jnp.float32)
    conv0_low = conv0_low.reshape(-1, width)
    small[6:7] = column_sum(conv0_low)
    spread_taps(conv0_low, taps)
    modulation_low = jnp.concatenate(
        [modulation_grad, jnp.zeros((modulation.shape[0] - slots, 2 * width), jnp.float32)], axis=0
    ).astype(LOW)
    modulation_sum = column_sum(modulation_low.astype(jnp.float32))
    small[11:12] = modulation_sum[:, :width]
    small[12:13] = modulation_sum[:, width:]
    stage(0, 2)
    stage(1, 2)
    for part in range(3):
        weight_grad(CONV0 + 3 * part, 3, hall0, taps[:, pl.ds(part * 3 * width, 3 * width)])
        stage(5 + part, 0)
        stage(2 + part, 1)
    aff_load.wait()
    weight_grad(AFF, 2, emb_all, modulation_low)
    stage(8, 0)
    emb_out[...] = dot(modulation_low, channels(abuf, 1 - core, 3 * width)[:, : 2 * width], NT).astype(LOW)
    emb_copy = to_mate(emb_out, emb_in)
    emb_own = dot(modulation_low, channels(abuf, core, 3 * width)[:, : 2 * width], NT)
    stage(0, 3)
    stage(1, 3)
    stage(2, 2)
    conv0_load.wait()
    mate_out[2] = dot(taps[...], channels(wbuf, 1 - core, 9 * width), NT).astype(LOW)
    hidden0_copy = to_mate(mate_out.at[2], mate_in.at[2])
    own_half[...] = dot(taps[...], channels(wbuf, core, 9 * width), NT)
    stage(3, 2)
    emb_copy.wait_recv()
    emb_grad[...] = (emb_own + emb_in[...].astype(jnp.float32)).astype(LOW)
    stage(4, 2)
    hidden0_copy.wait_recv()
    hidden0_grad = (own_half[...] + mate_in[2].astype(jnp.float32)).reshape(shape)
    normal, scale = normalize(img[...].astype(jnp.float32).reshape(shape), average)
    grad = hidden0_grad * silu_slope(normal * par[0:1] + par[3:4])
    small[0:1] = column_sum(grad * normal)
    small[3:4] = column_sum(grad)
    images_part = normalize_back(grad * par[0:1], normal, scale, average)
    img_grad[...] = (images_part.reshape(-1, width) + rgrad[...]).astype(LOW)
    smalls[spot] = small[...]
    small_copies = [
        remote(small, smalls.at[spot], small_sem.at[0, j], small_sem.at[1, j], {"dp": other})
        for j, other in enumerate(everyone)
    ]
    stage(2, 3)
    stage(5, 1)
    branch = dot(both(aall), abuf[:, :, :, :, pl.ds(2 * width, width)].reshape(-1, width)) + par[10:11]
    total = mask[...][:, None] * (residual[...] + branch).reshape(shape)
    block_out[...] = total.reshape(-1, width).astype(LOW)
    stage(3, 3)
    for group in range(6, len(groups) + 2):
        stage(group, 1)
        stage(group - 1, 2)
        stage(group - 2, 3)
    for copy in small_copies:
        copy.wait_recv()
    totals[...] = jnp.sum(smalls[...], axis=0)
    for copies in list(started.values()) + [mate_copies, small_copies]:
        for copy in copies:
            copy.wait_send()


def fast_body(
    images, embedding, counts, norm_gains, norm_shifts, lin_biases, conv_weights, aff_weights, qkv_weights, proj_weights, cotangent
):
    slots, _, width = images.shape
    rows = slots * PIXELS
    depth = conv_weights.shape[2]
    padded = -(-slots // 16) * 16
    low, f32 = LOW, jnp.float32
    img = images.reshape(rows, width)
    cot = cotangent.reshape(rows, width)
    emb = jnp.pad(embedding, ((0, padded - slots), (0, 0)))
    par = jnp.concatenate([norm_gains, norm_shifts, lin_biases, jnp.zeros((3, width), f32)])
    real = (jnp.arange(slots, dtype=jnp.int32) < counts[0]).astype(f32)
    mask = jnp.broadcast_to(real[:, None], (slots, width))
    vmem, anyw = pl.BlockSpec(memory_space=pltpu.VMEM), pl.BlockSpec(memory_space=pl.ANY)
    dma, buf, shape = pltpu.SemaphoreType.DMA, pltpu.VMEM, jax.ShapeDtypeStruct
    whole = GRID + (depth, 24 * width)
    pair = (2, rows, width)
    kept = pl.pallas_call(
        forward_kernel,
        name="gather_forward",
        out_shape=(
            shape(whole, low), shape(pair, low), shape(pair, low), shape(pair, low), shape((rows, width), low),
            shape((rows, width), f32), shape((rows, width), f32), shape((slots, width), f32), shape((padded, 2 * width), f32),
            shape((rows, width), f32), shape((slots, width), f32), shape((rows, 3 * width), low), shape((2, padded, width), low),
        ),
        in_specs=[vmem] * 5 + [anyw] * 4,
        out_specs=(anyw,) + (vmem,) * 12,
        scratch_shapes=[
            buf(whole, low), buf((3, rows, width), f32), buf((rows, 3 * width), low), buf((rows, width), f32),
            buf((rows, width), low), buf((rows, width), low), buf((rows, width), low),
            dma((21,)), dma((8, 2, 3)), dma((8, 2, 3)), dma((8, 2)), dma((8, 2)), dma((8, 2)), dma((8, 2)), dma((5,)), dma((5,)), dma((8,)),
        ],
        compiler_params=pltpu.CompilerParams(collective_id=0, has_side_effects=True, vmem_limit_bytes=56 * 2**20),
    )(img, emb, par, cot, mask, conv_weights, aff_weights.reshape(depth, -1), qkv_weights.reshape(depth, -1), proj_weights)
    full, hall0, hall1, nall, attended, residual, normal1, scale1, modulation, normal2, scale2, pgrad, emb_all = kept
    block_out, img_grad, emb_grad, totals, conv_grad, aff_grad, qkv_grad, proj_grad = pl.pallas_call(
        backward_kernel,
        name="backward_scatter",
        out_shape=(
            shape((rows, width), low), shape((rows, width), low), shape((padded, width), low), shape(par.shape, f32),
            shape(conv_weights.shape, f32), shape((depth, 2 * width), f32), shape((depth, 3 * width), f32), shape((depth, width), f32),
        ),
        in_specs=[vmem] * 16 + [anyw],
        out_specs=(vmem,) * 8,
        scratch_shapes=[
            buf(whole, low), buf((4, 2, depth, 24 * width), low), buf((4, depth, 24 * width), low), buf((3, depth, 24 * width), low),
            buf(GRID + (depth, 9 * width), low), buf(GRID + (depth, 3 * width), low), buf(GRID + (depth, 3 * width), low),
            buf((rows, 9 * width), low), buf(pair, low), buf((rows, width), f32), buf((rows, width), f32),
            buf((3, rows, width), low), buf((3, rows, width), low), buf((padded, width), low), buf((padded, width), low),
            buf((rows, width), low), buf(par.shape, f32), buf((16,) + par.shape, f32),
            dma((4,)), dma((2, 9, 2)), dma((2, 9, 2)), dma((2, 9, 2, 3)), dma((2, 15)), dma((5,)), dma((5,)),
        ],
        compiler_params=pltpu.CompilerParams(collective_id=1, has_side_effects=True, vmem_limit_bytes=63 * 2**20),
    )(img, par, cot, mask, hall0, hall1, nall, attended, residual, normal1, scale1, modulation, normal2, scale2, pgrad, emb_all, full)
    return (
        block_out.reshape(images.shape),
        img_grad.reshape(images.shape),
        emb_grad[:slots],
        totals[:3],
        totals[3:6],
        totals[6:13],
        conv_grad,
        aff_grad.reshape(aff_weights.shape),
        qkv_grad.reshape(qkv_weights.shape),
        proj_grad,
    )


def solution(mesh):
    return jax.shard_map(
        fast_body if mesh.shape["dp"] == 16 else body,
        mesh=mesh,
        in_specs=(
            P("dp", None, "tensor"),
            P("dp", "tensor"),
            P("dp"),
            P(None, "tensor"),
            P(None, "tensor"),
            P(None, "tensor"),
            P(None, None, "dp", "tensor"),
            P("dp", None, "tensor"),
            P("dp", None, "tensor"),
            P("dp", "tensor"),
            P("dp", None, "tensor"),
        ),
        out_specs=(
            P("dp", None, "tensor"),
            P("dp", None, "tensor"),
            P("dp", "tensor"),
            P(None, "tensor"),
            P(None, "tensor"),
            P(None, "tensor"),
            P(None, None, "dp", "tensor"),
            P("dp", None, "tensor"),
            P("dp", None, "tensor"),
            P("dp", "tensor"),
        ),
        check_vma=False,
    )
```

```python
import math

import jax
import jax.numpy as jnp
from jax import lax
from jax.experimental import pallas as pl
from jax.experimental.pallas import tpu as pltpu
from jax.sharding import PartitionSpec as P

C = 768
HEAD_DIM = 64
GROUPS = 32
SIDE = 8
PIXELS = 64
GROUP_SIZE = C // GROUPS
LOW = jnp.bfloat16
MESH = pl.DeviceIdType.MESH
NT = (((1,), (1,)), ((), ()))
TN = (((0,), (0,)), ((), ()))
GRID = (2, 2, 2, 2)


def group_norm(values, gain_vec, shift_vec):
    batch_size = values.shape[0]
    grouped = values.reshape(batch_size, PIXELS, -1, C // GROUPS)
    centre = jnp.mean(grouped, axis=(1, 3), keepdims=True)
    spread = jnp.mean(jnp.square(grouped - centre), axis=(1, 3), keepdims=True)
    normal = ((grouped - centre) * lax.rsqrt(spread + 1e-05)).reshape(values.shape)
    return normal * gain_vec + shift_vec


def first_norm(values, gain_vec, shift_vec):
    return jax.nn.silu(group_norm(values, gain_vec, shift_vec))


def middle(conv_values, modulation, gain_vec, shift_vec):
    scaled = (
        group_norm(conv_values, gain_vec, shift_vec) * (1.0 + modulation[:, 0:1])
        + modulation[:, 1:2]
    )
    return jax.nn.silu(scaled)


def windows(source):
    slot_count = source.shape[0]
    padded = jnp.pad(source.reshape(slot_count, SIDE, SIDE, -1), ((0, 0), (1, 1), (1, 1), (0, 0)))
    found = []
    for tap_index in range(9):
        row_shift = tap_index // 3
        col_shift = tap_index % 3
        found.append(
            padded[:, row_shift : row_shift + SIDE, col_shift : col_shift + SIDE].reshape(
                slot_count * PIXELS, -1
            )
        )
    return found


def convolve(source, kernel):
    slot_count = source.shape[0]
    summed = jnp.zeros((slot_count * PIXELS, kernel.shape[2]), jnp.float32)
    for tap_index, window in enumerate(windows(source)):
        summed = summed + jnp.dot(window, kernel[tap_index], preferred_element_type=jnp.float32)
    return summed.reshape(slot_count, PIXELS, -1)


def convolve_back(grad_low, kernel):
    slot_count = grad_low.shape[0]
    flattened = grad_low.reshape(slot_count * PIXELS, -1)
    summed = jnp.zeros((slot_count, SIDE + 2, SIDE + 2, kernel.shape[1]), jnp.float32)
    for tap_index in range(9):
        row_shift = tap_index // 3
        col_shift = tap_index % 3
        contrib = jnp.einsum(
            "rd,cd->rc", flattened, kernel[tap_index], preferred_element_type=jnp.float32
        )
        contrib = contrib.reshape(slot_count, SIDE, SIDE, -1)
        summed = summed + jnp.pad(
            contrib, ((0, 0), (row_shift, 2 - row_shift), (col_shift, 2 - col_shift), (0, 0))
        )
    return summed[:, 1 : SIDE + 1, 1 : SIDE + 1].reshape(slot_count, PIXELS, -1)


def conv_weight_grad(source, grad_low):
    slot_count = source.shape[0]
    flattened = grad_low.reshape(slot_count * PIXELS, -1)
    found = [
        jnp.einsum("rc,rd->cd", window, flattened, preferred_element_type=jnp.float32)
        for window in windows(source)
    ]
    return jnp.stack(found)


def gather_features(values_low):
    return lax.all_gather(values_low, "tensor", axis=2, tiled=True)


def back_features(partial_sum):
    return lax.psum_scatter(
        partial_sum.astype(jnp.bfloat16), "tensor", scatter_dimension=2, tiled=True
    ).astype(jnp.float32)


def body(
    images,
    embedding,
    counts,
    norm_gains,
    norm_shifts,
    lin_biases,
    conv_weights,
    aff_weights,
    qkv_weights,
    proj_weights,
    cotangent,
):
    slot_count = images.shape[0]
    score_scale = HEAD_DIM ** (-0.5)
    slot_mask = (jnp.arange(slot_count, dtype=jnp.int32) < counts[0]).astype(jnp.float32)
    conv_full = lax.all_gather(conv_weights, "dp", axis=2, tiled=True)
    aff_full, qkv_full, proj_full = (
        lax.all_gather(aff_weights, "dp", axis=0, tiled=True),
        lax.all_gather(qkv_weights, "dp", axis=0, tiled=True),
        lax.all_gather(proj_weights, "dp", axis=0, tiled=True),
    )
    images_f = images.astype(jnp.float32)
    hidden0 = first_norm(images_f, norm_gains[0], norm_shifts[0]).astype(jnp.bfloat16)
    hidden0_all, embed_all = (
        lax.all_gather(hidden0, "tensor", axis=2, tiled=True),
        lax.all_gather(embedding, "tensor", axis=1, tiled=True),
    )
    conv_out0 = convolve(hidden0_all, conv_full[0]) + lin_biases[0]
    modulation = (
        jnp.einsum("sc,cjd->sjd", embed_all, aff_full, preferred_element_type=jnp.float32)
        + lin_biases[5:7]
    )
    hidden1 = middle(conv_out0, modulation, norm_gains[1], norm_shifts[1]).astype(jnp.bfloat16)
    hidden1_all = gather_features(hidden1)
    residual = images_f + (convolve(hidden1_all, conv_full[1]) + lin_biases[1])
    normed = group_norm(residual, norm_gains[2], norm_shifts[2]).astype(jnp.bfloat16)
    normed_all = gather_features(normed)
    bias_rows = jnp.stack([lin_biases[2], jnp.zeros_like(lin_biases[2]), lin_biases[3]])
    projected = (
        jnp.einsum("spc,cjd->spjd", normed_all, qkv_full, preferred_element_type=jnp.float32)
        + bias_rows
    ).astype(jnp.bfloat16)
    head_shape = (slot_count, PIXELS, -1, HEAD_DIM)
    query_heads = projected[:, :, 0].reshape(head_shape)
    key_heads = projected[:, :, 1].reshape(head_shape)
    value_heads = projected[:, :, 2].reshape(head_shape)
    scores = (
        jnp.einsum("sqhd,skhd->shqk", query_heads, key_heads, preferred_element_type=jnp.float32)
        * score_scale
    )
    log_total = jax.scipy.special.logsumexp(scores, axis=-1, keepdims=True)
    probabilities = jnp.exp(scores - log_total)
    weights_low = probabilities.astype(jnp.bfloat16)
    attended = jnp.einsum(
        "shqk,skhd->sqhd", weights_low, value_heads, preferred_element_type=jnp.float32
    )
    attended = attended.reshape(slot_count, PIXELS, -1).astype(jnp.bfloat16)
    attended_all = gather_features(attended)
    branch = (
        jnp.einsum("spc,cd->spd", attended_all, proj_full, preferred_element_type=jnp.float32)
        + lin_biases[4]
    )
    block_output = (slot_mask[:, None, None] * (residual + branch)).astype(jnp.bfloat16)
    conv_back = lax.all_gather(conv_weights, "dp", axis=2, tiled=True)
    aff_back, qkv_back, proj_back = (
        lax.all_gather(aff_weights, "dp", axis=0, tiled=True),
        lax.all_gather(qkv_weights, "dp", axis=0, tiled=True),
        lax.all_gather(proj_weights, "dp", axis=0, tiled=True),
    )
    grad_branch = slot_mask[:, None, None] * cotangent
    branch_low = grad_branch.astype(jnp.bfloat16)
    proj_grad = jnp.einsum(
        "spc,spd->cd", attended_all, branch_low, preferred_element_type=jnp.float32
    )
    proj_bias_grad = jnp.sum(branch_low.astype(jnp.float32), axis=(0, 1))
    attended_grad = back_features(
        jnp.einsum("spd,cd->spc", branch_low, proj_back, preferred_element_type=jnp.float32)
    )
    attended_low = attended_grad.astype(jnp.bfloat16).reshape(head_shape)
    grad_probs = jnp.einsum(
        "sqhd,skhd->shqk", attended_low, value_heads, preferred_element_type=jnp.float32
    )
    value_grad = jnp.einsum(
        "shqk,sqhd->skhd", weights_low, attended_low, preferred_element_type=jnp.float32
    )
    score_grad = probabilities * (
        grad_probs - jnp.sum(grad_probs * probabilities, axis=-1, keepdims=True)
    )
    score_low = score_grad.astype(jnp.bfloat16)
    query_grad = (
        jnp.einsum("shqk,skhd->sqhd", score_low, key_heads, preferred_element_type=jnp.float32)
        * score_scale
    )
    key_grad = (
        jnp.einsum("shqk,sqhd->skhd", score_low, query_heads, preferred_element_type=jnp.float32)
        * score_scale
    )
    flat_shape = (slot_count, PIXELS, -1)
    projected_grad = jnp.stack(
        [
            query_grad.reshape(flat_shape),
            key_grad.reshape(flat_shape),
            value_grad.reshape(flat_shape),
        ],
        axis=2,
    ).astype(jnp.bfloat16)
    qkv_grad = jnp.einsum(
        "spc,spjd->cjd", normed_all, projected_grad, preferred_element_type=jnp.float32
    )
    qkv_bias_grad = jnp.sum(projected_grad.astype(jnp.float32), axis=(0, 1))
    normed_grad = back_features(
        jnp.einsum("spjd,cjd->spc", projected_grad, qkv_back, preferred_element_type=jnp.float32)
    )
    norm_value, norm_pull = jax.vjp(group_norm, residual, norm_gains[2], norm_shifts[2])
    residual_grad, gain2_grad, shift2_grad = norm_pull(normed_grad)
    residual_grad = residual_grad + grad_branch
    conv1_low = residual_grad.astype(jnp.bfloat16)
    conv1_bias_grad = jnp.sum(conv1_low.astype(jnp.float32), axis=(0, 1))
    conv1_wgrad = conv_weight_grad(hidden1_all, conv1_low)
    hidden1_grad = back_features(convolve_back(conv1_low, conv_back[1]))
    middle_value, middle_pull = jax.vjp(
        middle, conv_out0, modulation, norm_gains[1], norm_shifts[1]
    )
    conv0_grad, modulation_grad, gain1_grad, shift1_grad = middle_pull(hidden1_grad)
    modulation_low = modulation_grad.astype(jnp.bfloat16)
    aff_bias_grad = jnp.sum(modulation_low.astype(jnp.float32), axis=0)
    aff_grad = jnp.einsum(
        "sc,sjd->cjd", embed_all, modulation_low, preferred_element_type=jnp.float32
    )
    embed_part = jnp.einsum(
        "sjd,cjd->sc", modulation_low, aff_back, preferred_element_type=jnp.float32
    )
    conv0_low = conv0_grad.astype(jnp.bfloat16)
    conv0_bias_grad = jnp.sum(conv0_low.astype(jnp.float32), axis=(0, 1))
    conv0_wgrad = conv_weight_grad(hidden0_all, conv0_low)
    hidden0_part = convolve_back(conv0_low, conv_back[0])
    hidden0_grad, embedding_sum = (
        lax.psum_scatter(
            hidden0_part.astype(jnp.bfloat16), "tensor", scatter_dimension=2, tiled=True
        ).astype(jnp.float32),
        lax.psum_scatter(
            embed_part.astype(jnp.bfloat16), "tensor", scatter_dimension=1, tiled=True
        ).astype(jnp.float32),
    )
    first_value, first_pull = jax.vjp(first_norm, images_f, norm_gains[0], norm_shifts[0])
    images_part, gain0_grad, shift0_grad = first_pull(hidden0_grad)
    images_grad = (images_part + residual_grad).astype(jnp.bfloat16)
    gains_local = jnp.stack([gain0_grad, gain1_grad, gain2_grad])
    shifts_local = jnp.stack([shift0_grad, shift1_grad, shift2_grad])
    biases_local = jnp.stack(
        [
            conv0_bias_grad,
            conv1_bias_grad,
            qkv_bias_grad[0],
            qkv_bias_grad[2],
            proj_bias_grad,
            aff_bias_grad[0],
            aff_bias_grad[1],
        ]
    )
    gains_grad, shifts_grad, biases_grad = lax.psum((gains_local, shifts_local, biases_local), "dp")
    conv_local = jnp.stack([conv0_wgrad, conv1_wgrad])
    conv_summed, aff_summed, qkv_summed, proj_summed = (
        lax.psum_scatter(conv_local, "dp", scatter_dimension=2, tiled=True),
        lax.psum_scatter(aff_grad, "dp", scatter_dimension=0, tiled=True),
        lax.psum_scatter(qkv_grad, "dp", scatter_dimension=0, tiled=True),
        lax.psum_scatter(proj_grad, "dp", scatter_dimension=0, tiled=True),
    )
    return (
        block_output,
        images_grad,
        embedding_sum.astype(jnp.bfloat16),
        gains_grad,
        shifts_grad,
        biases_grad,
        conv_summed,
        aff_summed,
        qkv_summed,
        proj_summed,
    )


def dot(left, right, dims=(((1,), (0,)), ((), ()))):
    return lax.dot_general(left, right, dims, preferred_element_type=jnp.float32)


def device(pair, level, y, x, core):
    return {"dp": ((2 * pair + level) * 2 + y) * 2 + x, "tensor": core}


class Place:
    def __init__(self):
        spot, core = lax.axis_index("dp"), lax.axis_index("tensor")
        self.pair, self.level = spot // 8, lax.rem(spot // 4, 2)
        self.y, self.x, self.core = lax.rem(spot // 2, 2), lax.rem(spot, 2), core
        pair, level, y, x = self.pair, self.level, self.y, self.x
        self.home = level == core
        self.away = level != core
        self.mate = device(pair, 1 - level, y, x, core)
        self.xmate = device(pair, level, y, 1 - x, core)
        self.ymate = device(pair, level, 1 - y, x, core)
        self.cmate = device(pair, level, y, x, 1 - core)
        self.swap = device(pair, core, y, x, level)
        self.far = device(1 - pair, core, y, x, level)

    def greet(self):
        barrier = pltpu.get_barrier_semaphore()
        for other in (self.mate, self.xmate, self.ymate, self.cmate, self.far):
            pl.semaphore_signal(barrier, inc=1, device_id=other, device_id_type=MESH)

        @pl.when(self.away)
        def _():
            pl.semaphore_signal(barrier, inc=1, device_id=self.swap, device_id_type=MESH)

    def meet(self):
        barrier = pltpu.get_barrier_semaphore()

        @pl.when(self.home)
        def _():
            pl.semaphore_wait(barrier, 5)

        @pl.when(self.away)
        def _():
            pl.semaphore_wait(barrier, 6)


class Swap:
    def __init__(self, place, src, dst, sems):
        self.place = place
        self.local = pltpu.make_async_copy(src, dst, sems.at[0])
        self.remote = remote_copy(src, dst, sems.at[1], sems.at[2], place.swap)
        pl.when(place.home)(self.local.start)
        pl.when(place.away)(self.remote.start)

    def wait_recv(self):
        pl.when(self.place.home)(self.local.wait)
        pl.when(self.place.away)(self.remote.wait_recv)

    def wait_send(self):
        pl.when(self.place.away)(self.remote.wait_send)


class Share:
    def __init__(self, place, src, dst_ref, sems):
        self.place = place
        core = place.core
        dst = dst_ref.at[core]
        self.near_copy = remote_copy(src, dst, sems.at[0], sems.at[1], place.cmate)
        self.mate_copy = remote_copy(src, dst, sems.at[2], sems.at[3 + core], place.mate)
        self.swap_copy = remote_copy(src, dst, sems.at[2], sems.at[3 + core], place.swap)
        self.local = pltpu.make_async_copy(src, dst, sems.at[5])
        self.others = [remote_copy(src, dst, sems.at[2], sems.at[3 + part], place.mate) for part in range(2)]

        @pl.when(place.home)
        def _():
            self.mate_copy.start()
            self.local.start()

        @pl.when(place.away)
        def _():
            self.swap_copy.start()
            self.near_copy.start()

    def wait_recv(self):
        @pl.when(self.place.home)
        def _():
            self.local.wait()
            self.near_copy.wait_recv()

        @pl.when(self.place.away)
        def _():
            self.others[0].wait_recv()
            self.others[1].wait_recv()

    def wait_send(self):
        self.mate_copy.wait_send()
        pl.when(self.place.away)(self.near_copy.wait_send)


def halves(start, size):
    first = (size // 128 + 1) // 2 * 128
    return [(start, first, 0), (start + first, size - first, 1)]


def remote_copy(src, dst, send, recv, target):
    return pltpu.make_async_remote_copy(
        src_ref=src, dst_ref=dst, send_sem=send, recv_sem=recv, device_id=target, device_id_type=MESH
    )


def remote(src, dst, send, recv, target):
    copy = remote_copy(src, dst, send, recv, target)
    copy.start()
    return copy


def group_average(width):
    row = lax.broadcasted_iota(jnp.int32, (width, width), 0) // GROUP_SIZE
    col = lax.broadcasted_iota(jnp.int32, (width, width), 1) // GROUP_SIZE
    return jnp.where(row == col, 1.0 / (GROUP_SIZE * PIXELS), 0.0).astype(jnp.float32)


def group_mean(values, average):
    return lax.dot_general(
        jnp.sum(values, axis=1), average, (((1,), (0,)), ((), ())),
        precision=lax.Precision.HIGHEST, preferred_element_type=jnp.float32,
    )


def normalize(values, average):
    away = values - group_mean(values, average)[:, None]
    scale = lax.rsqrt(group_mean(away * away, average) + 1e-05)
    return away * scale[:, None], scale


def normalize_back(grad, normal, scale, average):
    return scale[:, None] * (
        grad - group_mean(grad, average)[:, None] - normal * group_mean(grad * normal, average)[:, None]
    )


def sigmoid(values):
    return 1.0 / (1.0 + jnp.exp(-values))


def silu_slope(values):
    gate = sigmoid(values)
    return gate * (1.0 + values * (1.0 - gate))


def shift_columns(values, step):
    moved = pltpu.roll(values, step % SIDE, 1)
    column = lax.broadcasted_iota(jnp.int32, values.shape, 1)
    return jnp.where(column == (0 if step == 1 else SIDE - 1), 0.0, moved)


def shift_rows(values, step):
    if step == 0:
        return values
    zero = jnp.zeros_like(values[:, :1])
    if step == 1:
        return jnp.concatenate([zero, values[:, : SIDE - 1]], axis=1)
    return jnp.concatenate([values[:, 1:], zero], axis=1)


def both(ref):
    return jnp.concatenate([ref[0], ref[1]], axis=1)


def convolve_row(source, weights, row_tap, sums, first=False):
    rows, width = sums.shape[1:]
    products = dot(source, weights)
    for col_tap in range(3):
        part = products[:, col_tap * width : (col_tap + 1) * width]
        part = shift_rows(part.reshape(-1, SIDE, SIDE, width), 1 - row_tap).reshape(rows, width)
        sums[col_tap] = part if first else sums[col_tap] + part


def convolve_end(sums):
    rows, width = sums.shape[1:]
    grids = [sums[col_tap].reshape(rows // SIDE, SIDE, width) for col_tap in range(3)]
    return (shift_columns(grids[0], 1) + grids[1] + shift_columns(grids[2], -1)).reshape(rows, width)


def spread_taps(grad, taps_ref):
    rows, width = grad.shape
    flat = grad.reshape(rows // SIDE, SIDE, width)
    for col_tap, grid in enumerate((shift_columns(flat, -1), flat, shift_columns(flat, 1))):
        for row_tap in range(3):
            moved = shift_rows(grid.reshape(-1, SIDE, SIDE, width), row_tap - 1)
            tap = row_tap * 3 + col_tap
            taps_ref[:, tap * width : (tap + 1) * width] = moved.reshape(rows, width).astype(LOW)


def expand_heads(block, lane_head, heads):
    return jnp.concatenate([jnp.where(lane_head == h, block, jnp.zeros_like(block)) for h in range(heads)], axis=0)


def contract_heads(wide, lane_head, heads):
    total = wide[:PIXELS]
    for h in range(1, heads):
        total = jnp.where(lane_head == h, wide[h * PIXELS : (h + 1) * PIXELS], total)
    return total


def attention(slots, projected, attended_grad, attended, projected_grad):
    width = attended.shape[1]
    heads = width // HEAD_DIM
    scale = HEAD_DIM ** (-0.5)
    lane_head = lax.broadcasted_iota(jnp.int32, (PIXELS, width), 1) // HEAD_DIM

    def one_slot(slot, carry):
        rows = pl.ds(pl.multiple_of(slot * PIXELS, PIXELS), PIXELS)
        query, key, value = (projected[rows, part * width : (part + 1) * width] for part in range(3))
        query_wide = expand_heads(query, lane_head, heads)
        scores = dot(query_wide, key, NT) * scale
        powers = jnp.exp(scores - jnp.max(scores, axis=1, keepdims=True))
        probabilities = powers / jnp.sum(powers, axis=1, keepdims=True)
        weights_low = probabilities.astype(LOW)
        attended[rows, :] = contract_heads(dot(weights_low, value), lane_head, heads).astype(LOW)
        grad_wide = expand_heads(attended_grad[rows, :], lane_head, heads)
        grad_probs = dot(grad_wide, value, NT)
        value_grad = dot(weights_low, grad_wide, TN)
        score_low = (
            probabilities * (grad_probs - jnp.sum(grad_probs * probabilities, axis=1, keepdims=True))
        ).astype(LOW)
        query_grad = contract_heads(dot(score_low, key), lane_head, heads) * scale
        key_grad = dot(score_low, query_wide, TN) * scale
        for part, grad in enumerate((query_grad, key_grad, value_grad)):
            projected_grad[rows, part * width : (part + 1) * width] = grad.astype(LOW)
        return carry

    lax.fori_loop(0, slots, one_slot, 0, unroll=2)


CONV0, AFF, PROJ, CONV1, QKV = 0, 9, 11, 12, 21
LAG = 2


def forward_kernel(
    counts, img, emb, gains, shifts, biases, cot, conv, aff, qkv, proj,
    full_out, hall0, hall1, nall, attended, residual, normal1, scale1, modulation, normal2, scale2, pgrad, emb_all,
    img_here, branch, par, mask,
    full, sums, wide, projected, ag_own, ag_send, ag_recv, ag_low, emb_own, par_own, mask_own, branch_own, hidden_own,
    first_local, first_send, first_recv, sends, recvs, swap_sem, share_sem, mate_send, mate_recv, out_sem,
):
    place = Place()
    pair, level, y, x, core = place.pair, place.level, place.y, place.x, place.core
    width = img.shape[1]
    slots = mask.shape[0]
    shape = (slots, PIXELS, width)
    place.greet()
    groups = [
        [(conv.at[0, tap], CONV0 + tap, 1) for tap in (0, 1, 2)],
        [(conv.at[0, tap], CONV0 + tap, 1) for tap in (3, 4, 5)],
        [(aff, AFF, 2), (proj, PROJ, 1)],
        [(conv.at[0, tap], CONV0 + tap, 1) for tap in (6, 7, 8)],
        [(conv.at[1, tap], CONV1 + tap, 1) for tap in (0, 1, 2)],
        [(conv.at[1, tap], CONV1 + tap, 1) for tap in (3, 4, 5)],
        [(conv.at[1, tap], CONV1 + tap, 1) for tap in (6, 7, 8)],
        [(qkv, QKV, 3)],
    ]
    started = {}

    def stage(group, s):
        if not 0 <= group < len(groups):
            return
        if s == 0:
            found = []
            for at, (src, column, count) in enumerate(groups[group]):
                dst = full.at[pair, level, y, x, :, pl.ds(column * width, count * width)]
                found.append(remote(src, dst, first_send.at[group, at], first_recv.at[group, at], place.far))
                found.append(Swap(place, src, dst, first_local.at[group, at]))
            started[group, 0] = found
            return
        if s == 1:
            for copy in started[group, 0]:
                copy.wait_recv()
        column = groups[group][0][1]
        for start, size, odd in halves(column * width, 3 * width):
            cols = pl.ds(start, size)
            for copy in started.get((group, odd, s - 1), []):
                copy.wait_recv()
            if s == 1:
                block, target = full.at[:, core, y, x, :, cols], (place.ymate if odd else place.xmate)
            elif s == 2:
                block = full.at[:, core, :, x, :, cols] if odd else full.at[:, core, y, :, :, cols]
                target = place.xmate if odd else place.ymate
            elif s == 3:
                block, target = full.at[:, core, :, :, :, cols], place.cmate
            else:
                continue
            started[group, odd, s] = [remote(block, block, sends.at[group, odd, s - 1], recvs.at[group, odd, s - 1], target)]

    mate_copies = []

    def to_mate(src, dst):
        at = len(mate_copies)
        copy = remote(src, dst, mate_send.at[at], mate_recv.at[at], place.mate)
        mate_copies.append(copy)
        return copy

    def weights(column, count, part=None):
        cols = pl.ds(column * width, count * width)
        block = full[:, :, :, :, :, cols] if part is None else full[part, :, :, :, :, cols]
        return block.reshape(-1, count * width)

    choose = lax.broadcasted_iota(jnp.int32, (emb_own.shape[0], slots), 0) == lax.broadcasted_iota(jnp.int32, (emb_own.shape[0], slots), 1)
    emb_own[...] = dot(choose.astype(LOW), emb[...]).astype(LOW)
    par_own[...] = jnp.zeros_like(par_own)
    par_own[0:3] = gains[...]
    par_own[3:6] = shifts[...]
    par_own[6:13] = biases[...]
    mask_own[...] = (lax.broadcasted_iota(jnp.int32, mask_own.shape, 0) < counts[0]).astype(jnp.float32)
    average = group_average(width)
    place.meet()
    stage(0, 0)
    par_copy = Swap(place, par_own, par, swap_sem.at[0])
    mask_copy = Swap(place, mask_own, mask, swap_sem.at[1])
    emb_copy = Share(place, emb_own, emb_all, share_sem.at[0])
    normal0, _ = normalize(img[...].astype(jnp.float32).reshape(shape), average)
    scaled = normal0 * par_own[0:1] + par_own[3:4]
    hidden_own[...] = (scaled * sigmoid(scaled)).reshape(-1, width).astype(LOW)
    hidden0_copy = Share(place, hidden_own, hall0, share_sem.at[1])
    branch_own[...] = (mask_own[...][:, None] * cot[...].reshape(shape)).reshape(-1, width).astype(LOW)
    extra_copies = [par_copy, mask_copy, emb_copy, hidden0_copy]
    out_copies = []
    for step in range(1, len(groups) + 4 * LAG):
        stage(step, 0)
        for s in (4, 3, 2, 1):
            stage(step - s * LAG, s)
        if step == 2:
            branch_copy = Swap(place, branch_own, branch, swap_sem.at[2])
            img_copy = Swap(place, img, img_here, swap_sem.at[3])
            extra_copies += [branch_copy, img_copy]
        group = step - 4 * LAG
        if group < 0:
            continue
        column = groups[group][0][1]
        cols = pl.ds(column * width, 3 * width)
        out_copies.append(pltpu.make_async_copy(full.at[:, :, :, :, :, cols], full_out.at[:, :, :, :, :, cols], out_sem.at[group]))
        out_copies[-1].start()
        if column < AFF:
            if group == 0:
                par_copy.wait_recv()
                emb_copy.wait_recv()
                hidden0_copy.wait_recv()
            convolve_row(both(hall0), weights(column, 3), column // 3, sums, group == 0)
        if column == AFF:
            changes = dot(both(emb_all), weights(AFF, 2)) + jnp.concatenate([par[11:12], par[12:13]], axis=1)
            modulation[...] = changes
            branch_copy.wait_recv()
            ag_send[...] = dot(branch[...], weights(PROJ, 1, 1 - level), NT).astype(LOW)
            ag_copy = to_mate(ag_send, ag_recv)
            ag_own[...] = dot(branch[...], weights(PROJ, 1, level), NT)
        if column == CONV0 + 6:
            conv_out0 = (convolve_end(sums) + par[6:7]).reshape(shape)
            normal, scale = normalize(conv_out0, average)
            normal1[...] = normal.reshape(-1, width)
            scale1[...] = scale
            scaled = (normal * par[1:2] + par[4:5]) * (1.0 + changes[:slots, None, :width]) + changes[:slots, None, width:]
            hall1[level] = (scaled * sigmoid(scaled)).reshape(-1, width).astype(LOW)
            hidden1_copy = to_mate(hall1.at[level], hall1.at[level])
        if CONV1 <= column < QKV:
            convolve_row(hall1[level], weights(column, 3, level), (column - CONV1) // 3, sums, column == CONV1)
        if column == CONV1 + 6:
            ag_copy.wait_recv()
            ag_low[...] = (ag_own[...] + ag_recv[...].astype(jnp.float32)).astype(LOW)
            hidden1_copy.wait_recv()
            for row_tap in range(3):
                convolve_row(hall1[1 - level], weights(CONV1 + 3 * row_tap, 3, 1 - level), row_tap, sums)
            img_copy.wait_recv()
            total = img_here[...].astype(jnp.float32) + (convolve_end(sums) + par[7:8])
            residual[...] = total
            normal, scale = normalize(total.reshape(shape), average)
            normal2[...] = normal.reshape(-1, width)
            scale2[...] = scale
            nall[level] = (normal * par[2:3] + par[5:6]).reshape(-1, width).astype(LOW)
            normed_copy = to_mate(nall.at[level], nall.at[level])
    bias = jnp.concatenate([par[8:9], jnp.zeros((1, width), jnp.float32), par[9:10]], axis=1)
    wide[...] = dot(nall[level], weights(QKV, 3, level)) + bias
    normed_copy.wait_recv()
    projected[...] = (wide[...] + dot(nall[1 - level], weights(QKV, 3, 1 - level))).astype(LOW)
    attention(slots, projected, ag_low, attended, pgrad)
    mask_copy.wait_recv()
    for copies in list(started.values()) + [mate_copies, extra_copies]:
        for copy in copies:
            copy.wait_send()
    for copy in out_copies:
        copy.wait()


def backward_kernel(
    img, branch, par, mask, hall0, hall1, nall, attended, residual, normal1, scale1, modulation, normal2, scale2, pgrad,
    emb_all, full,
    block_out, img_grad, emb_grad, totals, conv_grad, aff_grad, qkv_grad, proj_grad,
    work, r0, r1, r2, last, wbuf, qbuf, abuf, taps, aall, rgrad, own_half, mate_out, mate_in, emb_out, emb_in, emb_sum, emb_end,
    img_out, block_own, small, small_in, small_last,
    load_sem, sends, recvs, swap_sem, far_send, far_recv, small_send, small_recv, mate_send, mate_recv, end_sem,
):
    place = Place()
    pair, level, y, x, core = place.pair, place.level, place.y, place.x, place.core
    width = img.shape[1]
    slots = mask.shape[0]
    shape = (slots, PIXELS, width)
    place.greet()
    loads = []

    def load(column, count, dst):
        src = full.at[:, :, :, :, :, pl.ds(column * width, count * width)]
        loads.append(pltpu.make_async_copy(src, dst, load_sem.at[len(loads)]))
        loads[-1].start()
        return loads[-1]

    qkv_load = load(QKV, 3, qbuf)
    conv1_load = load(CONV1, 9, wbuf)
    aff_load = load(AFF, 3, abuf)
    mate_copies = []

    def to_mate(src, dst):
        at = len(mate_copies)
        copy = remote(src, dst, mate_send.at[at], mate_recv.at[at], place.mate)
        mate_copies.append(copy)
        return copy

    groups = {
        "qkv": (0, QKV, 3), "proj": (1, PROJ, 1), "conv1a": (2, CONV1, 3), "conv1b": (3, CONV1 + 3, 3), "conv1c": (4, CONV1 + 6, 3),
        "conv0a": (5, CONV0, 3), "conv0b": (6, CONV0 + 3, 3), "conv0c": (7, CONV0 + 6, 3), "aff": (8, AFF, 2),
    }
    started = {}

    def deliver(start, size, value):
        column, offset = start // width, start % width
        while size:
            now = min(size, width - offset)
            part, value = value[:, :now], value[:, now:]
            if column < AFF or CONV1 <= column < QKV:
                tap = column if column < AFF else column - CONV1 + 9
                conv_grad[tap // 9, tap % 9, :, offset : offset + now] = part
            else:
                ref, first = (aff_grad, AFF) if column < PROJ else (proj_grad, PROJ) if column < CONV1 else (qkv_grad, QKV)
                at = (column - first) * width + offset
                ref[:, at : at + now] = part
            column, offset, size = column + 1, 0, size - now

    def add(at, cols, received):
        total = work[at + (slice(None), cols)].astype(jnp.float32) + received.astype(jnp.float32)
        work[at + (slice(None), cols)] = total.astype(LOW)

    def stage(name, s):
        group, column, count = groups[name]
        for start, size, odd in halves(column * width, count * width):
            cols = pl.ds(start, size)
            for copy in started.get((group, odd, s - 1), []):
                copy.wait_recv()
            if s == 0:
                src, dst, target = work.at[:, 1 - core, :, :, :, cols], r0.at[:, :, :, :, cols], place.cmate
            elif s == 1:
                for pp in range(2):
                    for yy in range(2):
                        for xx in range(2):
                            add((pp, core, yy, xx), cols, r0[pp, yy, xx, :, cols])
                src = work.at[:, core, 1 - y, :, :, cols] if odd else work.at[:, core, :, 1 - x, :, cols]
                dst, target = r1.at[:, :, :, cols], (place.ymate if odd else place.xmate)
            elif s == 2:
                for pp in range(2):
                    for other in range(2):
                        add((pp, core, y, other) if odd else (pp, core, other, x), cols, r1[pp, other, :, cols])
                src = work.at[:, core, y, 1 - x, :, cols] if odd else work.at[:, core, 1 - y, x, :, cols]
                dst, target = r2.at[:, :, cols], (place.xmate if odd else place.ymate)
            elif s == 3:
                for pp in range(2):
                    add((pp, core, y, x), cols, r2[pp, :, cols])
                far = remote(
                    work.at[1 - pair, core, y, x, :, cols], last.at[1, :, cols], far_send.at[group, odd], far_recv.at[group, odd], place.far
                )
                started[group, odd, 3] = [
                    far, Swap(place, work.at[pair, core, y, x, :, cols], last.at[0, :, cols], swap_sem.at[group, odd])
                ]
                continue
            else:
                deliver(start, size, last[0, :, cols].astype(jnp.float32) + last[1, :, cols].astype(jnp.float32))
                continue
            started[group, odd, s] = [remote(src, dst, sends.at[group, odd, s], recvs.at[group, odd, s], target)]

    def weight_grad(name, source, grad):
        group, column, count = groups[name]
        for part in range(2):
            product = dot(source[part], grad, TN).astype(LOW)
            work[part, :, :, :, :, pl.ds(column * width, count * width)] = product.reshape(2, 2, 2, -1, count * width)
        stage(name, 0)

    def channels(ref, part):
        return ref[part].reshape(-1, ref.shape[-1])

    def column_sum(values):
        return jnp.sum(values.reshape(-1, values.shape[-1]), axis=0, keepdims=True)

    def three(part):
        return taps[:, pl.ds(part * 3 * width, 3 * width)]

    average = group_average(width)
    small[0] = jnp.zeros_like(small[0])
    aall[level] = attended[...]
    place.meet()
    qkv_load.wait()
    mate_out[0] = dot(pgrad[...], channels(qbuf, 1 - level), NT).astype(LOW)
    normed_copy = to_mate(mate_out.at[0], mate_in.at[0])
    attended_copy = to_mate(aall.at[level], aall.at[level])
    weight_grad("qkv", nall, pgrad[...])
    own_half[...] = dot(pgrad[...], channels(qbuf, level), NT)
    small[0, 10:11] = column_sum(branch[...].astype(jnp.float32))
    small[0, 8:9] = column_sum(pgrad[:, :width].astype(jnp.float32))
    small[0, 9:10] = column_sum(pgrad[:, 2 * width :].astype(jnp.float32))
    stage("qkv", 1)
    normed_copy.wait_recv()
    normed_grad = (own_half[...] + mate_in[0].astype(jnp.float32)).reshape(shape)
    normal = normal2[...].reshape(shape)
    small[0, 2:3] = column_sum(normed_grad * normal)
    small[0, 5:6] = column_sum(normed_grad)
    residual_grad = normalize_back(normed_grad * par[2:3], normal, scale2[...], average).reshape(-1, width)
    rgrad[...] = residual_grad + branch[...].astype(jnp.float32)
    conv1_low = rgrad[...].astype(LOW).astype(jnp.float32)
    small[0, 7:8] = column_sum(conv1_low)
    spread_taps(conv1_low, taps)
    conv1_load.wait()
    mate_out[1] = dot(taps[...], channels(wbuf, 1 - level), NT).astype(LOW)
    hidden1_copy = to_mate(mate_out.at[1], mate_in.at[1])
    stage("qkv", 2)
    weight_grad("conv1a", hall1, three(0))
    weight_grad("conv1b", hall1, three(1))
    stage("conv1a", 1)
    weight_grad("conv1c", hall1, three(2))
    stage("conv1b", 1)
    own_half[...] = dot(taps[...], channels(wbuf, level), NT)
    conv0_load = load(CONV0, 9, wbuf)
    stage("qkv", 3)
    attended_copy.wait_recv()
    weight_grad("proj", aall, branch[...])
    stage("conv1c", 1)
    stage("conv1a", 2)
    stage("proj", 1)
    hidden1_copy.wait_recv()
    hidden1_grad = (own_half[...] + mate_in[1].astype(jnp.float32)).reshape(shape)
    normal = normal1[...].reshape(shape)
    changes = modulation[...]
    change = 1.0 + changes[:slots, None, :width]
    inner = normal * par[1:2] + par[4:5]
    grad = hidden1_grad * silu_slope(inner * change + changes[:slots, None, width:])
    modulation_grad = jnp.concatenate([jnp.sum(grad * inner, axis=1), jnp.sum(grad, axis=1)], axis=1)
    grad = grad * change
    small[0, 1:2] = column_sum(grad * normal)
    small[0, 4:5] = column_sum(grad)
    conv0_low = normalize_back(grad * par[1:2], normal, scale1[...], average).astype(LOW).astype(jnp.float32)
    conv0_low = conv0_low.reshape(-1, width)
    small[0, 6:7] = column_sum(conv0_low)
    spread_taps(conv0_low, taps)
    modulation_low = jnp.concatenate(
        [modulation_grad, jnp.zeros((modulation.shape[0] - slots, 2 * width), jnp.float32)], axis=0
    ).astype(LOW)
    modulation_sum = column_sum(modulation_low.astype(jnp.float32))
    small[0, 11:12] = modulation_sum[:, :width]
    small[0, 12:13] = modulation_sum[:, width:]
    conv0_load.wait()
    mate_out[2] = dot(taps[...], channels(wbuf, 1 - level), NT).astype(LOW)
    hidden0_copy = to_mate(mate_out.at[2], mate_in.at[2])
    weight_grad("conv0a", hall0, three(0))
    stage("conv1b", 2)
    weight_grad("conv0b", hall0, three(1))
    stage("conv0a", 1)
    stage("proj", 2)
    weight_grad("conv0c", hall0, three(2))
    stage("conv1c", 2)
    aff_load.wait()
    weight_grad("aff", emb_all, modulation_low)
    stage("conv0b", 1)
    emb_out[...] = dot(modulation_low, channels(abuf, 1 - level)[:, : 2 * width], NT).astype(LOW)
    emb_copy = to_mate(emb_out, emb_in)
    emb_own = dot(modulation_low, channels(abuf, level)[:, : 2 * width], NT)
    stage("conv1a", 3)
    stage("conv0c", 1)
    stage("conv0a", 2)
    stage("aff", 1)
    stage("conv1b", 3)
    stage("proj", 3)
    own_half[...] = dot(taps[...], channels(wbuf, level), NT)
    joined = dot(both(aall), abuf[:, :, :, :, :, pl.ds(2 * width, width)].reshape(-1, width)) + par[10:11]
    block = mask[...][:, None] * (residual[...] + joined).reshape(shape)
    block_own[...] = block.reshape(-1, width).astype(LOW)
    block_copy = Swap(place, block_own, block_out, end_sem.at[0])
    stage("conv0b", 2)
    stage("conv1c", 3)
    stage("conv0c", 2)
    stage("aff", 2)
    emb_copy.wait_recv()
    emb_sum[...] = (emb_own + emb_in[...].astype(jnp.float32)).astype(LOW)
    emb_end_copy = Swap(place, emb_sum, emb_end, end_sem.at[1])
    hidden0_copy.wait_recv()
    hidden0_grad = (own_half[...] + mate_in[2].astype(jnp.float32)).reshape(shape)
    normal, scale = normalize(img[...].astype(jnp.float32).reshape(shape), average)
    grad = hidden0_grad * silu_slope(normal * par[0:1] + par[3:4])
    small[0, 0:1] = column_sum(grad * normal)
    small[0, 3:4] = column_sum(grad)
    images_part = normalize_back(grad * par[0:1], normal, scale, average)
    img_out[...] = (images_part.reshape(-1, width) + rgrad[...]).astype(LOW)
    img_copy = Swap(place, img_out, img_grad, end_sem.at[2])
    small_copies = []

    def small_step(at, target):
        copy = remote(small.at[at], small_in.at[at], small_send.at[at], small_recv.at[at], target)
        small_copies.append(copy)

    def small_add(at):
        small_copies[at].wait_recv()
        small[at + 1] = small[at] + small_in[at]

    small_step(0, place.cmate)
    stage("conv0a", 3)
    small_add(0)
    small_step(1, place.xmate)
    stage("conv0b", 3)
    small_add(1)
    small_step(2, place.ymate)
    stage("qkv", 4)
    stage("conv1a", 4)
    stage("conv0c", 3)
    small_add(2)
    stage("aff", 3)
    small_far = remote(small.at[3], small_last.at[1], small_send.at[3], small_recv.at[3], place.far)
    small_near = Swap(place, small.at[3], small_last.at[0], end_sem.at[3])
    for name in ("conv1b", "proj", "conv1c", "conv0a", "conv0b"):
        stage(name, 4)
    small_far.wait_recv()
    small_near.wait_recv()
    totals[...] = small_last[0] + small_last[1]
    small_copies += [small_far, small_near]
    stage("conv0c", 4)
    stage("aff", 4)
    emb_end_copy.wait_recv()
    emb_grad[...] = emb_end[...][:slots]
    block_copy.wait_recv()
    img_copy.wait_recv()
    for copies in list(started.values()) + [mate_copies, small_copies, [block_copy, emb_end_copy, img_copy]]:
        for copy in copies:
            copy.wait_send()


def fast_body(
    images, embedding, counts, norm_gains, norm_shifts, lin_biases, conv_weights, aff_weights, qkv_weights, proj_weights, cotangent
):
    slots, _, width = images.shape
    rows = slots * PIXELS
    depth = conv_weights.shape[2]
    padded = -(-slots // 16) * 16
    low, f32 = LOW, jnp.float32
    vmem, anyw = pl.BlockSpec(memory_space=pltpu.VMEM), pl.BlockSpec(memory_space=pl.ANY)
    smem = pl.BlockSpec(memory_space=pltpu.SMEM)
    dma, buf, shape = pltpu.SemaphoreType.DMA, pltpu.VMEM, jax.ShapeDtypeStruct

    def whole(columns):
        return GRID + (depth, columns * width)

    pair = (2, rows, width)
    one = (rows, width)
    par = (16, width)
    kept = pl.pallas_call(
        forward_kernel,
        name="gather_forward",
        out_shape=(
            shape(whole(24), low), shape(pair, low), shape(pair, low), shape(pair, low), shape(one, low),
            shape(one, f32), shape(one, f32), shape((slots, width), f32), shape((padded, 2 * width), f32),
            shape(one, f32), shape((slots, width), f32), shape((rows, 3 * width), low), shape((2, padded, width), low),
            shape(one, low), shape(one, low), shape(par, f32), shape((slots, width), f32),
        ),
        in_specs=[smem] + [vmem] * 6 + [anyw] * 4,
        out_specs=(anyw,) + (vmem,) * 16,
        scratch_shapes=[
            buf(whole(24), low), buf((3, rows, width), f32), buf((rows, 3 * width), f32), buf((rows, 3 * width), low), buf(one, f32),
            buf(one, low), buf(one, low), buf(one, low), buf((padded, width), low), buf(par, f32), buf((slots, width), f32),
            buf(one, low), buf(one, low),
            dma((8, 3, 3)), dma((8, 3)), dma((8, 3)), dma((8, 2, 3)), dma((8, 2, 3)), dma((4, 3)), dma((2, 6)), dma((3,)), dma((3,)), dma((8,)),
        ],
        compiler_params=pltpu.CompilerParams(collective_id=0, has_side_effects=True, vmem_limit_bytes=60 * 2**20),
    )(
        counts, images.reshape(one), embedding, norm_gains, norm_shifts, lin_biases, cotangent.reshape(one),
        conv_weights, aff_weights.reshape(depth, -1), qkv_weights.reshape(depth, -1), proj_weights,
    )
    full, hall0, hall1, nall, attended, residual, normal1, scale1, modulation, normal2, scale2, pgrad, emb_all, img, branch, par_here, mask = kept
    block_out, img_grad, emb_grad, totals, conv_grad, aff_grad, qkv_grad, proj_grad = pl.pallas_call(
        backward_kernel,
        name="backward_scatter",
        out_shape=(
            shape(one, low), shape(one, low), shape((slots, width), low), shape(par, f32),
            shape(conv_weights.shape, f32), shape((depth, 2 * width), f32), shape((depth, 3 * width), f32), shape((depth, width), f32),
        ),
        in_specs=[vmem] * 16 + [anyw],
        out_specs=(vmem,) * 8,
        scratch_shapes=[
            buf(whole(24), low), buf((2, 2, 2, depth, 24 * width), low), buf((2, 2, depth, 24 * width), low),
            buf((2, depth, 24 * width), low), buf((2, depth, 24 * width), low),
            buf(whole(9), low), buf(whole(3), low), buf(whole(3), low),
            buf((rows, 9 * width), low), buf(pair, low), buf(one, f32), buf(one, f32),
            buf((3, rows, width), low), buf((3, rows, width), low), buf((padded, width), low), buf((padded, width), low), buf((padded, width), low), buf((padded, width), low),
            buf(one, low), buf(one, low), buf((4,) + par, f32), buf((3,) + par, f32), buf((2,) + par, f32),
            dma((4,)), dma((9, 2, 3)), dma((9, 2, 3)), dma((9, 2, 3)), dma((9, 2)), dma((9, 2)), dma((4,)), dma((4,)), dma((5,)), dma((5,)), dma((4, 3)),
        ],
        compiler_params=pltpu.CompilerParams(collective_id=1, has_side_effects=True, vmem_limit_bytes=63 * 2**20),
    )(img, branch, par_here, mask, hall0, hall1, nall, attended, residual, normal1, scale1, modulation, normal2, scale2, pgrad, emb_all, full)
    return (
        block_out.reshape(images.shape),
        img_grad.reshape(images.shape),
        emb_grad,
        totals[:3],
        totals[3:6],
        totals[6:13],
        conv_grad,
        aff_grad.reshape(aff_weights.shape),
        qkv_grad.reshape(qkv_weights.shape),
        proj_grad,
    )


def solution(mesh):
    return jax.shard_map(
        fast_body if mesh.shape["dp"] == 16 else body,
        mesh=mesh,
        in_specs=(
            P("dp", None, "tensor"),
            P("dp", "tensor"),
            P("dp"),
            P(None, "tensor"),
            P(None, "tensor"),
            P(None, "tensor"),
            P(None, None, "dp", "tensor"),
            P("dp", None, "tensor"),
            P("dp", None, "tensor"),
            P("dp", "tensor"),
            P("dp", None, "tensor"),
        ),
        out_specs=(
            P("dp", None, "tensor"),
            P("dp", None, "tensor"),
            P("dp", "tensor"),
            P(None, "tensor"),
            P(None, "tensor"),
            P(None, "tensor"),
            P(None, None, "dp", "tensor"),
            P("dp", None, "tensor"),
            P("dp", None, "tensor"),
            P("dp", "tensor"),
        ),
        check_vma=False,
    )
```

```python
import math

import jax
import jax.numpy as jnp
from jax import lax
from jax.experimental import pallas as pl
from jax.experimental.pallas import tpu as pltpu
from jax.sharding import PartitionSpec as P

C = 768
HEAD_DIM = 64
GROUPS = 32
SIDE = 8
PIXELS = 64
GROUP_SIZE = C // GROUPS
LOW = jnp.bfloat16
MESH = pl.DeviceIdType.MESH
NT = (((1,), (1,)), ((), ()))
TN = (((0,), (0,)), ((), ()))
GRID = (2, 2, 2, 2)


def group_norm(values, gain_vec, shift_vec):
    batch_size = values.shape[0]
    grouped = values.reshape(batch_size, PIXELS, -1, C // GROUPS)
    centre = jnp.mean(grouped, axis=(1, 3), keepdims=True)
    spread = jnp.mean(jnp.square(grouped - centre), axis=(1, 3), keepdims=True)
    normal = ((grouped - centre) * lax.rsqrt(spread + 1e-05)).reshape(values.shape)
    return normal * gain_vec + shift_vec


def first_norm(values, gain_vec, shift_vec):
    return jax.nn.silu(group_norm(values, gain_vec, shift_vec))


def middle(conv_values, modulation, gain_vec, shift_vec):
    scaled = (
        group_norm(conv_values, gain_vec, shift_vec) * (1.0 + modulation[:, 0:1])
        + modulation[:, 1:2]
    )
    return jax.nn.silu(scaled)


def windows(source):
    slot_count = source.shape[0]
    padded = jnp.pad(source.reshape(slot_count, SIDE, SIDE, -1), ((0, 0), (1, 1), (1, 1), (0, 0)))
    found = []
    for tap_index in range(9):
        row_shift = tap_index // 3
        col_shift = tap_index % 3
        found.append(
            padded[:, row_shift : row_shift + SIDE, col_shift : col_shift + SIDE].reshape(
                slot_count * PIXELS, -1
            )
        )
    return found


def convolve(source, kernel):
    slot_count = source.shape[0]
    summed = jnp.zeros((slot_count * PIXELS, kernel.shape[2]), jnp.float32)
    for tap_index, window in enumerate(windows(source)):
        summed = summed + jnp.dot(window, kernel[tap_index], preferred_element_type=jnp.float32)
    return summed.reshape(slot_count, PIXELS, -1)


def convolve_back(grad_low, kernel):
    slot_count = grad_low.shape[0]
    flattened = grad_low.reshape(slot_count * PIXELS, -1)
    summed = jnp.zeros((slot_count, SIDE + 2, SIDE + 2, kernel.shape[1]), jnp.float32)
    for tap_index in range(9):
        row_shift = tap_index // 3
        col_shift = tap_index % 3
        contrib = jnp.einsum(
            "rd,cd->rc", flattened, kernel[tap_index], preferred_element_type=jnp.float32
        )
        contrib = contrib.reshape(slot_count, SIDE, SIDE, -1)
        summed = summed + jnp.pad(
            contrib, ((0, 0), (row_shift, 2 - row_shift), (col_shift, 2 - col_shift), (0, 0))
        )
    return summed[:, 1 : SIDE + 1, 1 : SIDE + 1].reshape(slot_count, PIXELS, -1)


def conv_weight_grad(source, grad_low):
    slot_count = source.shape[0]
    flattened = grad_low.reshape(slot_count * PIXELS, -1)
    found = [
        jnp.einsum("rc,rd->cd", window, flattened, preferred_element_type=jnp.float32)
        for window in windows(source)
    ]
    return jnp.stack(found)


def gather_features(values_low):
    return lax.all_gather(values_low, "tensor", axis=2, tiled=True)


def back_features(partial_sum):
    return lax.psum_scatter(
        partial_sum.astype(jnp.bfloat16), "tensor", scatter_dimension=2, tiled=True
    ).astype(jnp.float32)


def body(
    images,
    embedding,
    counts,
    norm_gains,
    norm_shifts,
    lin_biases,
    conv_weights,
    aff_weights,
    qkv_weights,
    proj_weights,
    cotangent,
):
    slot_count = images.shape[0]
    score_scale = HEAD_DIM ** (-0.5)
    slot_mask = (jnp.arange(slot_count, dtype=jnp.int32) < counts[0]).astype(jnp.float32)
    conv_full = lax.all_gather(conv_weights, "dp", axis=2, tiled=True)
    aff_full, qkv_full, proj_full = (
        lax.all_gather(aff_weights, "dp", axis=0, tiled=True),
        lax.all_gather(qkv_weights, "dp", axis=0, tiled=True),
        lax.all_gather(proj_weights, "dp", axis=0, tiled=True),
    )
    images_f = images.astype(jnp.float32)
    hidden0 = first_norm(images_f, norm_gains[0], norm_shifts[0]).astype(jnp.bfloat16)
    hidden0_all, embed_all = (
        lax.all_gather(hidden0, "tensor", axis=2, tiled=True),
        lax.all_gather(embedding, "tensor", axis=1, tiled=True),
    )
    conv_out0 = convolve(hidden0_all, conv_full[0]) + lin_biases[0]
    modulation = (
        jnp.einsum("sc,cjd->sjd", embed_all, aff_full, preferred_element_type=jnp.float32)
        + lin_biases[5:7]
    )
    hidden1 = middle(conv_out0, modulation, norm_gains[1], norm_shifts[1]).astype(jnp.bfloat16)
    hidden1_all = gather_features(hidden1)
    residual = images_f + (convolve(hidden1_all, conv_full[1]) + lin_biases[1])
    normed = group_norm(residual, norm_gains[2], norm_shifts[2]).astype(jnp.bfloat16)
    normed_all = gather_features(normed)
    bias_rows = jnp.stack([lin_biases[2], jnp.zeros_like(lin_biases[2]), lin_biases[3]])
    projected = (
        jnp.einsum("spc,cjd->spjd", normed_all, qkv_full, preferred_element_type=jnp.float32)
        + bias_rows
    ).astype(jnp.bfloat16)
    head_shape = (slot_count, PIXELS, -1, HEAD_DIM)
    query_heads = projected[:, :, 0].reshape(head_shape)
    key_heads = projected[:, :, 1].reshape(head_shape)
    value_heads = projected[:, :, 2].reshape(head_shape)
    scores = (
        jnp.einsum("sqhd,skhd->shqk", query_heads, key_heads, preferred_element_type=jnp.float32)
        * score_scale
    )
    log_total = jax.scipy.special.logsumexp(scores, axis=-1, keepdims=True)
    probabilities = jnp.exp(scores - log_total)
    weights_low = probabilities.astype(jnp.bfloat16)
    attended = jnp.einsum(
        "shqk,skhd->sqhd", weights_low, value_heads, preferred_element_type=jnp.float32
    )
    attended = attended.reshape(slot_count, PIXELS, -1).astype(jnp.bfloat16)
    attended_all = gather_features(attended)
    branch = (
        jnp.einsum("spc,cd->spd", attended_all, proj_full, preferred_element_type=jnp.float32)
        + lin_biases[4]
    )
    block_output = (slot_mask[:, None, None] * (residual + branch)).astype(jnp.bfloat16)
    conv_back = lax.all_gather(conv_weights, "dp", axis=2, tiled=True)
    aff_back, qkv_back, proj_back = (
        lax.all_gather(aff_weights, "dp", axis=0, tiled=True),
        lax.all_gather(qkv_weights, "dp", axis=0, tiled=True),
        lax.all_gather(proj_weights, "dp", axis=0, tiled=True),
    )
    grad_branch = slot_mask[:, None, None] * cotangent
    branch_low = grad_branch.astype(jnp.bfloat16)
    proj_grad = jnp.einsum(
        "spc,spd->cd", attended_all, branch_low, preferred_element_type=jnp.float32
    )
    proj_bias_grad = jnp.sum(branch_low.astype(jnp.float32), axis=(0, 1))
    attended_grad = back_features(
        jnp.einsum("spd,cd->spc", branch_low, proj_back, preferred_element_type=jnp.float32)
    )
    attended_low = attended_grad.astype(jnp.bfloat16).reshape(head_shape)
    grad_probs = jnp.einsum(
        "sqhd,skhd->shqk", attended_low, value_heads, preferred_element_type=jnp.float32
    )
    value_grad = jnp.einsum(
        "shqk,sqhd->skhd", weights_low, attended_low, preferred_element_type=jnp.float32
    )
    score_grad = probabilities * (
        grad_probs - jnp.sum(grad_probs * probabilities, axis=-1, keepdims=True)
    )
    score_low = score_grad.astype(jnp.bfloat16)
    query_grad = (
        jnp.einsum("shqk,skhd->sqhd", score_low, key_heads, preferred_element_type=jnp.float32)
        * score_scale
    )
    key_grad = (
        jnp.einsum("shqk,sqhd->skhd", score_low, query_heads, preferred_element_type=jnp.float32)
        * score_scale
    )
    flat_shape = (slot_count, PIXELS, -1)
    projected_grad = jnp.stack(
        [
            query_grad.reshape(flat_shape),
            key_grad.reshape(flat_shape),
            value_grad.reshape(flat_shape),
        ],
        axis=2,
    ).astype(jnp.bfloat16)
    qkv_grad = jnp.einsum(
        "spc,spjd->cjd", normed_all, projected_grad, preferred_element_type=jnp.float32
    )
    qkv_bias_grad = jnp.sum(projected_grad.astype(jnp.float32), axis=(0, 1))
    normed_grad = back_features(
        jnp.einsum("spjd,cjd->spc", projected_grad, qkv_back, preferred_element_type=jnp.float32)
    )
    norm_value, norm_pull = jax.vjp(group_norm, residual, norm_gains[2], norm_shifts[2])
    residual_grad, gain2_grad, shift2_grad = norm_pull(normed_grad)
    residual_grad = residual_grad + grad_branch
    conv1_low = residual_grad.astype(jnp.bfloat16)
    conv1_bias_grad = jnp.sum(conv1_low.astype(jnp.float32), axis=(0, 1))
    conv1_wgrad = conv_weight_grad(hidden1_all, conv1_low)
    hidden1_grad = back_features(convolve_back(conv1_low, conv_back[1]))
    middle_value, middle_pull = jax.vjp(
        middle, conv_out0, modulation, norm_gains[1], norm_shifts[1]
    )
    conv0_grad, modulation_grad, gain1_grad, shift1_grad = middle_pull(hidden1_grad)
    modulation_low = modulation_grad.astype(jnp.bfloat16)
    aff_bias_grad = jnp.sum(modulation_low.astype(jnp.float32), axis=0)
    aff_grad = jnp.einsum(
        "sc,sjd->cjd", embed_all, modulation_low, preferred_element_type=jnp.float32
    )
    embed_part = jnp.einsum(
        "sjd,cjd->sc", modulation_low, aff_back, preferred_element_type=jnp.float32
    )
    conv0_low = conv0_grad.astype(jnp.bfloat16)
    conv0_bias_grad = jnp.sum(conv0_low.astype(jnp.float32), axis=(0, 1))
    conv0_wgrad = conv_weight_grad(hidden0_all, conv0_low)
    hidden0_part = convolve_back(conv0_low, conv_back[0])
    hidden0_grad, embedding_sum = (
        lax.psum_scatter(
            hidden0_part.astype(jnp.bfloat16), "tensor", scatter_dimension=2, tiled=True
        ).astype(jnp.float32),
        lax.psum_scatter(
            embed_part.astype(jnp.bfloat16), "tensor", scatter_dimension=1, tiled=True
        ).astype(jnp.float32),
    )
    first_value, first_pull = jax.vjp(first_norm, images_f, norm_gains[0], norm_shifts[0])
    images_part, gain0_grad, shift0_grad = first_pull(hidden0_grad)
    images_grad = (images_part + residual_grad).astype(jnp.bfloat16)
    gains_local = jnp.stack([gain0_grad, gain1_grad, gain2_grad])
    shifts_local = jnp.stack([shift0_grad, shift1_grad, shift2_grad])
    biases_local = jnp.stack(
        [
            conv0_bias_grad,
            conv1_bias_grad,
            qkv_bias_grad[0],
            qkv_bias_grad[2],
            proj_bias_grad,
            aff_bias_grad[0],
            aff_bias_grad[1],
        ]
    )
    gains_grad, shifts_grad, biases_grad = lax.psum((gains_local, shifts_local, biases_local), "dp")
    conv_local = jnp.stack([conv0_wgrad, conv1_wgrad])
    conv_summed, aff_summed, qkv_summed, proj_summed = (
        lax.psum_scatter(conv_local, "dp", scatter_dimension=2, tiled=True),
        lax.psum_scatter(aff_grad, "dp", scatter_dimension=0, tiled=True),
        lax.psum_scatter(qkv_grad, "dp", scatter_dimension=0, tiled=True),
        lax.psum_scatter(proj_grad, "dp", scatter_dimension=0, tiled=True),
    )
    return (
        block_output,
        images_grad,
        embedding_sum.astype(jnp.bfloat16),
        gains_grad,
        shifts_grad,
        biases_grad,
        conv_summed,
        aff_summed,
        qkv_summed,
        proj_summed,
    )


def dot(left, right, dims=(((1,), (0,)), ((), ()))):
    return lax.dot_general(left, right, dims, preferred_element_type=jnp.float32)


def device(pair, level, y, x, core):
    return {"dp": ((2 * pair + level) * 2 + y) * 2 + x, "tensor": core}


class Place:
    def __init__(self):
        spot, core = lax.axis_index("dp"), lax.axis_index("tensor")
        self.pair, self.level = spot // 8, lax.rem(spot // 4, 2)
        self.y, self.x, self.core = lax.rem(spot // 2, 2), lax.rem(spot, 2), core
        pair, level, y, x = self.pair, self.level, self.y, self.x
        self.home = level == core
        self.away = level != core
        self.mate = device(pair, 1 - level, y, x, core)
        self.pmate = device(1 - pair, level, y, x, core)
        self.xmate = device(pair, level, y, 1 - x, core)
        self.ymate = device(pair, level, 1 - y, x, core)
        self.cmate = device(pair, level, y, x, 1 - core)
        self.swap = device(pair, core, y, x, level)
        self.far = device(1 - pair, core, y, x, level)

    def greet(self):
        barrier = pltpu.get_barrier_semaphore()
        for other in (self.mate, self.pmate, self.xmate, self.ymate, self.cmate, self.far):
            pl.semaphore_signal(barrier, inc=1, device_id=other, device_id_type=MESH)

        @pl.when(self.away)
        def _():
            pl.semaphore_signal(barrier, inc=1, device_id=self.swap, device_id_type=MESH)

    def meet(self):
        barrier = pltpu.get_barrier_semaphore()

        @pl.when(self.home)
        def _():
            pl.semaphore_wait(barrier, 6)

        @pl.when(self.away)
        def _():
            pl.semaphore_wait(barrier, 7)


class Swap:
    def __init__(self, place, src, dst, sems):
        self.place = place
        self.local = pltpu.make_async_copy(src, dst, sems.at[0])
        self.remote = remote_copy(src, dst, sems.at[1], sems.at[2], place.swap)
        pl.when(place.home)(self.local.start)
        pl.when(place.away)(self.remote.start)

    def wait_recv(self):
        pl.when(self.place.home)(self.local.wait)
        pl.when(self.place.away)(self.remote.wait_recv)

    def wait_send(self):
        pl.when(self.place.away)(self.remote.wait_send)


class Share:
    def __init__(self, place, src, dst_ref, sems):
        self.place = place
        core = place.core
        dst = dst_ref.at[core]
        self.near_copy = remote_copy(src, dst, sems.at[0], sems.at[1], place.cmate)
        self.mate_copy = remote_copy(src, dst, sems.at[2], sems.at[3 + core], place.mate)
        self.swap_copy = remote_copy(src, dst, sems.at[2], sems.at[3 + core], place.swap)
        self.local = pltpu.make_async_copy(src, dst, sems.at[5])
        self.others = [remote_copy(src, dst, sems.at[2], sems.at[3 + part], place.mate) for part in range(2)]

        @pl.when(place.home)
        def _():
            self.mate_copy.start()
            self.local.start()

        @pl.when(place.away)
        def _():
            self.swap_copy.start()
            self.near_copy.start()

    def wait_recv(self):
        @pl.when(self.place.home)
        def _():
            self.local.wait()
            self.near_copy.wait_recv()

        @pl.when(self.place.away)
        def _():
            self.others[0].wait_recv()
            self.others[1].wait_recv()

    def wait_send(self):
        self.mate_copy.wait_send()
        pl.when(self.place.away)(self.near_copy.wait_send)


class Return:
    def __init__(self, place, src_ref, dst_ref, sems):
        self.place, self.src_ref, self.dst_ref, self.sems = place, src_ref, dst_ref, sems
        core = place.core
        self.near_copy = remote_copy(src_ref.at[1 - core], dst_ref.at[0], sems.at[0], sems.at[1], place.cmate)
        self.swap_copy = remote_copy(src_ref.at[1 - core], dst_ref.at[1], sems.at[0], sems.at[2], place.swap)
        self.local = pltpu.make_async_copy(src_ref.at[core], dst_ref.at[0], sems.at[3])
        self.mate_copy = remote_copy(src_ref.at[core], dst_ref.at[1], sems.at[4], sems.at[2], place.mate)

    def start_other(self):
        pl.when(self.place.home)(self.near_copy.start)
        pl.when(self.place.away)(self.swap_copy.start)

    def start_own(self):
        pl.when(self.place.home)(self.local.start)
        pl.when(self.place.away)(self.mate_copy.start)

    def wait_recv(self):
        pl.when(self.place.home)(self.local.wait)
        pl.when(self.place.away)(self.near_copy.wait_recv)
        self.swap_copy.wait_recv()

    def wait_send(self):
        self.near_copy.wait_send()
        pl.when(self.place.away)(self.mate_copy.wait_send)


def halves(start, size):
    first = (size // 128 + 1) // 2 * 128
    return [(start, first, 0), (start + first, size - first, 1)]


def remote_copy(src, dst, send, recv, target):
    return pltpu.make_async_remote_copy(
        src_ref=src, dst_ref=dst, send_sem=send, recv_sem=recv, device_id=target, device_id_type=MESH
    )


def remote(src, dst, send, recv, target):
    copy = remote_copy(src, dst, send, recv, target)
    copy.start()
    return copy


def group_average(width):
    row = lax.broadcasted_iota(jnp.int32, (width, width), 0) // GROUP_SIZE
    col = lax.broadcasted_iota(jnp.int32, (width, width), 1) // GROUP_SIZE
    return jnp.where(row == col, 1.0 / (GROUP_SIZE * PIXELS), 0.0).astype(jnp.float32)


def group_mean(values, average):
    return lax.dot_general(
        jnp.sum(values, axis=1), average, (((1,), (0,)), ((), ())),
        precision=lax.Precision.HIGHEST, preferred_element_type=jnp.float32,
    )


def normalize(values, average):
    away = values - group_mean(values, average)[:, None]
    scale = lax.rsqrt(group_mean(away * away, average) + 1e-05)
    return away * scale[:, None], scale


def normalize_back(grad, normal, scale, average):
    return scale[:, None] * (
        grad - group_mean(grad, average)[:, None] - normal * group_mean(grad * normal, average)[:, None]
    )


def sigmoid(values):
    return 1.0 / (1.0 + jnp.exp(-values))


def silu_slope(values):
    gate = sigmoid(values)
    return gate * (1.0 + values * (1.0 - gate))


def shift_columns(values, step):
    moved = pltpu.roll(values, step % SIDE, 1)
    column = lax.broadcasted_iota(jnp.int32, values.shape, 1)
    return jnp.where(column == (0 if step == 1 else SIDE - 1), 0.0, moved)


def shift_rows(values, step):
    if step == 0:
        return values
    zero = jnp.zeros_like(values[:, :1])
    if step == 1:
        return jnp.concatenate([zero, values[:, : SIDE - 1]], axis=1)
    return jnp.concatenate([values[:, 1:], zero], axis=1)


def both(ref):
    return jnp.concatenate([ref[0], ref[1]], axis=1)


def convolve_row(source, weights, row_tap, sums, first=False):
    rows, width = sums.shape[1:]
    products = dot(source, weights)
    for col_tap in range(3):
        part = products[:, col_tap * width : (col_tap + 1) * width]
        part = shift_rows(part.reshape(-1, SIDE, SIDE, width), 1 - row_tap).reshape(rows, width)
        sums[col_tap] = part if first else sums[col_tap] + part


def convolve_end(sums):
    rows, width = sums.shape[1:]
    grids = [sums[col_tap].reshape(rows // SIDE, SIDE, width) for col_tap in range(3)]
    return (shift_columns(grids[0], 1) + grids[1] + shift_columns(grids[2], -1)).reshape(rows, width)


def spread_taps(grad, taps_ref):
    rows, width = grad.shape
    flat = grad.reshape(rows // SIDE, SIDE, width)
    for col_tap, grid in enumerate((shift_columns(flat, -1), flat, shift_columns(flat, 1))):
        for row_tap in range(3):
            moved = shift_rows(grid.reshape(-1, SIDE, SIDE, width), row_tap - 1)
            tap = row_tap * 3 + col_tap
            taps_ref[:, tap * width : (tap + 1) * width] = moved.reshape(rows, width).astype(LOW)


def expand_heads(block, lane_head, heads):
    return jnp.concatenate([jnp.where(lane_head == h, block, jnp.zeros_like(block)) for h in range(heads)], axis=0)


def contract_heads(wide, lane_head, heads):
    total = wide[:PIXELS]
    for h in range(1, heads):
        total = jnp.where(lane_head == h, wide[h * PIXELS : (h + 1) * PIXELS], total)
    return total


def attention(slots, projected, attended_grad, attended, projected_grad):
    width = attended.shape[1]
    heads = width // HEAD_DIM
    scale = HEAD_DIM ** (-0.5)
    lane_head = lax.broadcasted_iota(jnp.int32, (PIXELS, width), 1) // HEAD_DIM

    def one_slot(slot, carry):
        rows = pl.ds(pl.multiple_of(slot * PIXELS, PIXELS), PIXELS)
        query, key, value = (projected[rows, part * width : (part + 1) * width] for part in range(3))
        query_wide = expand_heads(query, lane_head, heads)
        scores = dot(query_wide, key, NT) * scale
        powers = jnp.exp(scores - jnp.max(scores, axis=1, keepdims=True))
        probabilities = powers / jnp.sum(powers, axis=1, keepdims=True)
        weights_low = probabilities.astype(LOW)
        attended[rows, :] = contract_heads(dot(weights_low, value), lane_head, heads).astype(LOW)
        grad_wide = expand_heads(attended_grad[rows, :], lane_head, heads)
        grad_probs = dot(grad_wide, value, NT)
        value_grad = dot(weights_low, grad_wide, TN)
        score_low = (
            probabilities * (grad_probs - jnp.sum(grad_probs * probabilities, axis=1, keepdims=True))
        ).astype(LOW)
        query_grad = contract_heads(dot(score_low, key), lane_head, heads) * scale
        key_grad = dot(score_low, query_wide, TN) * scale
        for part, grad in enumerate((query_grad, key_grad, value_grad)):
            projected_grad[rows, part * width : (part + 1) * width] = grad.astype(LOW)
        return carry

    lax.fori_loop(0, slots, one_slot, 0, unroll=2)


CONV0, AFF, CONV1, PROJ, QKV = 0, 9, 11, 20, 21
LAG = 2


def own_parameters(gains, shifts, biases, par):
    par[...] = jnp.zeros_like(par)
    par[0:3] = gains[...]
    par[3:6] = shifts[...]
    par[6:13] = biases[...]


def slot_mask(counts, slots, width):
    return (lax.broadcasted_iota(jnp.int32, (slots, width), 0) < counts[0]).astype(jnp.float32)


def forward_kernel(
    counts, img, emb, gains, shifts, biases, cot, aff, qkv, conv, proj,
    full_out, hall0_out, hall1_out, normal1_out, scale1_out, modulation_out, emb_all_out, par_out,
    nall_out, attended_out, residual_out, normal2_out, scale2_out, pgrad_out,
    full, hall0, hall1, normal1, scale1, modulation, emb_all, par, nall, attended, residual, normal2, scale2, pgrad,
    sums, wide, projected, ag_own, ag_send, ag_recv, ag_low, emb_own, par_own, hidden_own, conv_own, conv_in, aff_own, qkv_own,
    own_sem, first_local, first_send, first_recv, sends, recvs, swap_sem, share_sem, mate_send, mate_recv, out_sem,
):
    place = Place()
    pair, level, y, x, core = place.pair, place.level, place.y, place.x, place.core
    width = img.shape[1]
    slots = scale1.shape[0]
    shape = (slots, PIXELS, width)
    place.greet()
    groups = [
        (CONV0, 3, [(conv.at[0, tap], CONV0 + tap, 1) for tap in (0, 1, 2)], True),
        (CONV0 + 3, 3, [(conv.at[0, tap], CONV0 + tap, 1) for tap in (3, 4, 5)], True),
        (AFF, 2, [(aff_own, AFF, 2)], True),
        (CONV0 + 6, 3, [(conv.at[0, tap], CONV0 + tap, 1) for tap in (6, 7, 8)], True),
        (CONV1, 3, [(conv.at[1, tap], CONV1 + tap, 1) for tap in (0, 1, 2)], True),
        (CONV1 + 3, 3, [(conv.at[1, tap], CONV1 + tap, 1) for tap in (3, 4, 5)], True),
        (CONV1 + 6, 3, [(conv.at[1, tap], CONV1 + tap, 1) for tap in (6, 7, 8)], True),
        (PROJ, 1, [(proj, PROJ, 1)], False),
        (QKV, 3, [(qkv_own, QKV, 3)], False),
    ]
    started = {}

    def stage(group, s):
        if not 0 <= group < len(groups):
            return
        column, count, sources, wide_way = groups[group]
        if s == 0 and wide_way:
            found = []
            for at, (src, first, many) in enumerate(sources):
                dst = full.at[pair, level, y, x, :, pl.ds(first * width, many * width)]
                found.append(remote(src, dst, first_send.at[group, at], first_recv.at[group, at], place.far))
                found.append(Swap(place, src, dst, first_local.at[group, at]))
            started[group, 0] = found
            return
        if s == 0:
            src, first, many = sources[0]
            dst = full.at[pair, level, y, x, :, pl.ds(first * width, many * width)]
            local = pltpu.make_async_copy(src, dst, own_sem.at[group - 7])
            local.start()
            started[group, 0] = [remote(src, dst, first_send.at[group, 0], first_recv.at[group, 0], place.mate)]
            started[group, "local"] = local
            return
        if s == 1:
            for copy in started[group, 0]:
                copy.wait_recv()
            if not wide_way:
                started.pop((group, "local")).wait()
        for start, size, odd in halves(column * width, count * width):
            cols = pl.ds(start, size)
            for copy in started.get((group, odd, s - 1), []):
                copy.wait_recv()
            first, second = (place.ymate, place.xmate) if odd else (place.xmate, place.ymate)
            if wide_way:
                if s == 1:
                    block, target = full.at[:, core, y, x, :, cols], first
                elif s == 2:
                    block, target = (full.at[:, core, :, x, :, cols] if odd else full.at[:, core, y, :, :, cols]), second
                elif s == 3:
                    block, target = full.at[:, core, :, :, :, cols], place.cmate
            else:
                if s == 1:
                    block, target = full.at[pair, :, y, x, :, cols], place.pmate
                elif s == 2:
                    block, target = full.at[:, :, y, x, :, cols], first
                elif s == 3:
                    block, target = (full.at[:, :, :, x, :, cols] if odd else full.at[:, :, y, :, :, cols]), second
            if s < 4:
                started[group, odd, s] = [remote(block, block, sends.at[group, odd, s - 1], recvs.at[group, odd, s - 1], target)]

    pair_copies = []

    def to(target, src, dst):
        at = len(pair_copies)
        pair_copies.append(remote(src, dst, mate_send.at[at], mate_recv.at[at], target))
        return pair_copies[-1]

    def weights(column, count, part=None):
        cols = pl.ds(column * width, count * width)
        block = full[:, :, :, :, :, cols] if part is None else full[part, :, :, :, :, cols]
        return block.reshape(-1, count * width)

    out_copies = []

    def keep(src, dst):
        out_copies.append(pltpu.make_async_copy(src, dst, out_sem.at[len(out_copies)]))
        out_copies[-1].start()

    for part in range(2):
        aff_own[:, part * width : (part + 1) * width] = aff[:, part, :]
    for part in range(3):
        qkv_own[:, part * width : (part + 1) * width] = qkv[:, part, :]
    padded = emb_own.shape[0]
    choose = lax.broadcasted_iota(jnp.int32, (padded, slots), 0) == lax.broadcasted_iota(jnp.int32, (padded, slots), 1)
    emb_own[...] = dot(choose.astype(LOW), emb[...]).astype(LOW)
    own_parameters(gains, shifts, biases, par_own)
    average = group_average(width)
    place.meet()
    stage(0, 0)
    par_copy = Swap(place, par_own, par, swap_sem.at[0])
    emb_copy = Share(place, emb_own, emb_all, share_sem.at[0])
    normal0, _ = normalize(img[...].astype(jnp.float32).reshape(shape), average)
    scaled = normal0 * par_own[0:1] + par_own[3:4]
    hidden_own[...] = (scaled * sigmoid(scaled)).reshape(-1, width).astype(LOW)
    hidden0_copy = Share(place, hidden_own, hall0, share_sem.at[1])
    branch_low = (slot_mask(counts, slots, width)[:, None] * cot[...].reshape(shape)).reshape(-1, width).astype(LOW)
    for step in range(1, len(groups) + 4 * LAG):
        stage(step, 0)
        for s in (4, 3, 2, 1):
            stage(step - s * LAG, s)
        group = step - 4 * LAG
        if group < 0:
            continue
        column, count = groups[group][:2]
        cols = pl.ds(column * width, count * width)
        keep(full.at[:, :, :, :, :, cols], full_out.at[:, :, :, :, :, cols])
        if column < AFF:
            if column == CONV0:
                par_copy.wait_recv()
                emb_copy.wait_recv()
                hidden0_copy.wait_recv()
                keep(par, par_out)
                keep(emb_all, emb_all_out)
                keep(hall0, hall0_out)
            convolve_row(both(hall0), weights(column, 3), column // 3, sums, column == CONV0)
        if column == AFF:
            changes = dot(both(emb_all), weights(AFF, 2)) + jnp.concatenate([par[11:12], par[12:13]], axis=1)
            modulation[...] = changes
            keep(modulation, modulation_out)
        if column == CONV0 + 6:
            conv_out0 = (convolve_end(sums) + par[6:7]).reshape(shape)
            normal, scale = normalize(conv_out0, average)
            scaled = (normal * par[1:2] + par[4:5]) * (1.0 + changes[:slots, None, :width]) + changes[:slots, None, width:]
            hall1[level] = (scaled * sigmoid(scaled)).reshape(-1, width).astype(LOW)
            hidden1_copy = to(place.mate, hall1.at[level], hall1.at[level])
            normal1[...] = normal.reshape(-1, width)
            scale1[...] = scale
            keep(normal1, normal1_out)
            keep(scale1, scale1_out)
        if CONV1 <= column < PROJ:
            convolve_row(hall1[level], weights(column, 3, level), (column - CONV1) // 3, sums, column == CONV1)
        if column == CONV1 + 6:
            hidden1_copy.wait_recv()
            keep(hall1, hall1_out)
            for row_tap in range(3):
                convolve_row(hall1[1 - level], weights(CONV1 + 3 * row_tap, 3, 1 - level), row_tap, sums)
            conv_own[...] = convolve_end(sums).astype(LOW)
            conv_copy = Swap(place, conv_own, conv_in, swap_sem.at[1])
        if column == PROJ:
            ag_send[...] = dot(branch_low, weights(PROJ, 1, 1 - core), NT).astype(LOW)
            ag_copy = to(place.cmate, ag_send, ag_recv)
            ag_own[...] = dot(branch_low, weights(PROJ, 1, core), NT)
    conv_copy.wait_recv()
    total = img[...].astype(jnp.float32) + (conv_in[...].astype(jnp.float32) + par_own[7:8])
    normal, scale = normalize(total.reshape(shape), average)
    nall[core] = (normal * par_own[2:3] + par_own[5:6]).reshape(-1, width).astype(LOW)
    normed_copy = to(place.cmate, nall.at[core], nall.at[core])
    residual[...] = total
    normal2[...] = normal.reshape(-1, width)
    scale2[...] = scale
    keep(residual, residual_out)
    keep(normal2, normal2_out)
    keep(scale2, scale2_out)
    bias = jnp.concatenate([par_own[8:9], jnp.zeros((1, width), jnp.float32), par_own[9:10]], axis=1)
    wide[...] = dot(nall[core], weights(QKV, 3, core)) + bias
    ag_copy.wait_recv()
    ag_low[...] = (ag_own[...] + ag_recv[...].astype(jnp.float32)).astype(LOW)
    normed_copy.wait_recv()
    keep(nall, nall_out)
    projected[...] = (wide[...] + dot(nall[1 - core], weights(QKV, 3, 1 - core))).astype(LOW)
    attention(slots, projected, ag_low, attended, pgrad)
    keep(pgrad, pgrad_out)
    keep(attended, attended_out)
    for copies in list(started.values()) + [pair_copies, [par_copy, emb_copy, hidden0_copy, conv_copy]]:
        for copy in copies:
            copy.wait_send()
    for copy in out_copies:
        copy.wait()


def backward_kernel(
    counts, img, gains, shifts, biases, cot,
    full, hall0_in, hall1_in, normal1_in, scale1_in, modulation_in, emb_all_in, par_in,
    nall_in, attended_in, residual_in, normal2_in, scale2_in, pgrad_in,
    block_out, img_grad, emb_grad, totals, conv_grad, aff_grad, qkv_grad, proj_grad,
    hall0, hall1, normal1, scale1, modulation, emb_all, par, nall, normal2, scale2, pgrad,
    work, r0, r1, r2, last, wbuf, qbuf, abuf, pbuf, taps, aall, rgrad, own_half, mate_out, mate_in, ret_in, low_own, low_in,
    emb_out, emb_in, emb_sum, emb_end, branch, par_own, small_here, small_there, small, small_in,
    load_sem, sends, recvs, swap_sem, small_send, small_recv, mate_send, mate_recv, end_sem, ret_sem,
):
    place = Place()
    pair, level, y, x, core = place.pair, place.level, place.y, place.x, place.core
    width = img.shape[1]
    slots = scale1.shape[0]
    shape = (slots, PIXELS, width)
    place.greet()
    loads = []

    def load(src, dst):
        loads.append(pltpu.make_async_copy(src, dst, load_sem.at[len(loads)]))
        loads[-1].start()
        return loads[-1]

    def load_weights(column, count, dst):
        return load(full.at[:, :, :, :, :, pl.ds(column * width, count * width)], dst)

    pgrad_load = load(pgrad_in, pgrad)
    qkv_load = load_weights(QKV, 3, qbuf)
    attended_load = load(attended_in, aall.at[core])
    normed_loads = [load(nall_in, nall), load(normal2_in, normal2), load(scale2_in, scale2)]
    conv1_loads = [load_weights(CONV1, 9, wbuf), load(hall1_in, hall1)]
    middle_loads = [load(normal1_in, normal1), load(scale1_in, scale1), load(modulation_in, modulation), load(par_in, par)]
    conv0_loads = [load(hall0_in, hall0), load(emb_all_in, emb_all), load_weights(AFF, 2, abuf)]
    end_loads = [load_weights(PROJ, 1, pbuf)]
    pair_copies = []

    def to(at, target, src, dst):
        pair_copies.append(remote(src, dst, mate_send.at[at], mate_recv.at[at], target))
        return pair_copies[-1]

    groups = {
        "qkv": (0, QKV, 3, False), "proj": (1, PROJ, 1, False),
        "conv1a": (2, CONV1, 3, True), "conv1b": (3, CONV1 + 3, 3, True), "conv1c": (4, CONV1 + 6, 3, True),
        "conv0a": (5, CONV0, 3, True), "conv0b": (6, CONV0 + 3, 3, True), "conv0c": (7, CONV0 + 6, 3, True), "aff": (8, AFF, 2, True),
    }
    started = {}

    def deliver(start, size, value):
        column, offset = start // width, start % width
        while size:
            now = min(size, width - offset)
            part, value = value[:, :now], value[:, now:]
            if column < AFF or CONV1 <= column < PROJ:
                tap = column if column < AFF else column - CONV1 + 9
                conv_grad[tap // 9, tap % 9, :, offset : offset + now] = part
            else:
                ref, first = (aff_grad, AFF) if column < CONV1 else (proj_grad, PROJ) if column < QKV else (qkv_grad, QKV)
                at = (column - first) * width + offset
                ref[:, at : at + now] = part
            column, offset, size = column + 1, 0, size - now

    def add(at, cols, received):
        total = work[at + (slice(None), cols)].astype(jnp.float32) + received.astype(jnp.float32)
        work[at + (slice(None), cols)] = total.astype(LOW)

    def stage(name, s):
        group, column, count, wide_way = groups[name]
        for start, size, odd in halves(column * width, count * width):
            cols = pl.ds(start, size)
            for copy in started.get((group, odd, s - 1), []):
                copy.wait_recv()
            first, second = (place.ymate, place.xmate) if odd else (place.xmate, place.ymate)
            if wide_way:
                if s == 0:
                    src, dst, target = work.at[:, 1 - core, :, :, :, cols], r0.at[:, :, :, :, cols], place.cmate
                elif s == 1:
                    for pp in range(2):
                        for yy in range(2):
                            for xx in range(2):
                                add((pp, core, yy, xx), cols, r0[pp, yy, xx, :, cols])
                    src = work.at[:, core, 1 - y, :, :, cols] if odd else work.at[:, core, :, 1 - x, :, cols]
                    dst, target = r1.at[:, :, :, cols], first
                elif s == 2:
                    for pp in range(2):
                        for other in range(2):
                            add((pp, core, y, other) if odd else (pp, core, other, x), cols, r1[pp, other, :, cols])
                    src = work.at[:, core, y, 1 - x, :, cols] if odd else work.at[:, core, 1 - y, x, :, cols]
                    dst, target = r2.at[:, :, cols], second
                elif s == 3:
                    for pp in range(2):
                        add((pp, core, y, x), cols, r2[pp, :, cols])
                    far = remote(
                        work.at[1 - pair, core, y, x, :, cols], last.at[1, :, cols], sends.at[group, odd, 3], recvs.at[group, odd, 3], place.far
                    )
                    started[group, odd, 3] = [
                        far, Swap(place, work.at[pair, core, y, x, :, cols], last.at[0, :, cols], swap_sem.at[group, odd])
                    ]
                    continue
                else:
                    deliver(start, size, last[0, :, cols].astype(jnp.float32) + last[1, :, cols].astype(jnp.float32))
                    continue
            else:
                if s == 0:
                    src = work.at[:, :, 1 - y, :, :, cols] if odd else work.at[:, :, :, 1 - x, :, cols]
                    dst, target = r0.at[:, :, :, :, cols], first
                elif s == 1:
                    for pp in range(2):
                        for ll in range(2):
                            for other in range(2):
                                add((pp, ll, y, other) if odd else (pp, ll, other, x), cols, r0[pp, ll, other, :, cols])
                    src = work.at[:, :, y, 1 - x, :, cols] if odd else work.at[:, :, 1 - y, x, :, cols]
                    dst, target = r1.at[:, :, :, cols], second
                elif s == 2:
                    for pp in range(2):
                        for ll in range(2):
                            add((pp, ll, y, x), cols, r1[pp, ll, :, cols])
                    src, dst, target = work.at[1 - pair, :, y, x, :, cols], r2.at[:, :, cols], place.pmate
                elif s == 3:
                    for ll in range(2):
                        add((pair, ll, y, x), cols, r2[ll, :, cols])
                    src, dst, target = work.at[pair, 1 - level, y, x, :, cols], last.at[1, :, cols], place.mate
                else:
                    deliver(start, size, work[pair, level, y, x, :, cols].astype(jnp.float32) + last[1, :, cols].astype(jnp.float32))
                    continue
            started[group, odd, s] = [remote(src, dst, sends.at[group, odd, s], recvs.at[group, odd, s], target)]

    def weight_grad(name, source, grad):
        group, column, count, _ = groups[name]
        for part in range(2):
            product = dot(source[part], grad, TN).astype(LOW)
            work[part, :, :, :, :, pl.ds(column * width, count * width)] = product.reshape(2, 2, 2, -1, count * width)
        stage(name, 0)

    def channels(ref, part):
        return ref[part].reshape(-1, ref.shape[-1])

    def column_sum(values):
        return jnp.sum(values.reshape(-1, values.shape[-1]), axis=0, keepdims=True)

    def three(part):
        return taps[:, pl.ds(part * 3 * width, 3 * width)]

    average = group_average(width)
    own_parameters(gains, shifts, biases, par_own)
    small_here[...] = jnp.zeros_like(small_here)
    small_there[...] = jnp.zeros_like(small_there)
    place.meet()
    attended_load.wait()
    attended_copy = to(0, place.cmate, aall.at[core], aall.at[core])
    pgrad_load.wait()
    qkv_load.wait()
    mate_out[0] = dot(pgrad[...], channels(qbuf, 1 - core), NT).astype(LOW)
    normed_copy = to(1, place.cmate, mate_out.at[0], mate_in.at[0])
    own_half[...] = dot(pgrad[...], channels(qbuf, core), NT)
    mask = slot_mask(counts, slots, width)
    branch[...] = (mask[:, None] * cot[...].reshape(shape)).reshape(-1, width).astype(LOW)
    for load_now in normed_loads:
        load_now.wait()
    normed_copy.wait_recv()
    normed_grad = (own_half[...] + mate_in[0].astype(jnp.float32)).reshape(shape)
    normal = normal2[...].reshape(shape)
    residual_grad = normalize_back(normed_grad * par_own[2:3], normal, scale2[...], average) + mask[:, None] * cot[...].reshape(shape)
    residual_grad = residual_grad.reshape(-1, width)
    low_own[...] = residual_grad.astype(LOW)
    low_copy = Swap(place, low_own, low_in, end_sem.at[0])
    rgrad[...] = residual_grad
    small_here[2:3] = column_sum(normed_grad * normal)
    small_here[5:6] = column_sum(normed_grad)
    weight_grad("qkv", nall, pgrad[...])
    attended_copy.wait_recv()
    weight_grad("proj", aall, branch[...])
    small_here[7:8] = column_sum(low_own[...].astype(jnp.float32))
    small_here[8:9] = column_sum(pgrad[:, :width].astype(jnp.float32))
    small_here[9:10] = column_sum(pgrad[:, 2 * width :].astype(jnp.float32))
    small_here[10:11] = column_sum(branch[...].astype(jnp.float32))
    low_copy.wait_recv()
    spread_taps(low_in[...].astype(jnp.float32), taps)
    for load_now in conv1_loads:
        load_now.wait()
    mate_out[1] = dot(taps[...], channels(wbuf, 1 - level), NT).astype(LOW)
    hidden1_copy = to(2, place.mate, mate_out.at[1], mate_in.at[1])
    weight_grad("conv1a", hall1, three(0))
    stage("qkv", 1)
    weight_grad("conv1b", hall1, three(1))
    stage("conv1a", 1)
    stage("proj", 1)
    weight_grad("conv1c", hall1, three(2))
    stage("conv1b", 1)
    own_half[...] = dot(taps[...], channels(wbuf, level), NT)
    conv0_loads.append(load_weights(CONV0, 9, wbuf))
    stage("conv1c", 1)
    stage("qkv", 2)
    stage("conv1a", 2)
    for load_now in middle_loads:
        load_now.wait()
    hidden1_copy.wait_recv()
    hidden1_grad = (own_half[...] + mate_in[1].astype(jnp.float32)).reshape(shape)
    normal = normal1[...].reshape(shape)
    changes = modulation[...]
    change = 1.0 + changes[:slots, None, :width]
    inner = normal * par[1:2] + par[4:5]
    grad = hidden1_grad * silu_slope(inner * change + changes[:slots, None, width:])
    modulation_grad = jnp.concatenate([jnp.sum(grad * inner, axis=1), jnp.sum(grad, axis=1)], axis=1)
    grad = grad * change
    small_there[1:2] = column_sum(grad * normal)
    small_there[4:5] = column_sum(grad)
    conv0_low = normalize_back(grad * par[1:2], normal, scale1[...], average).astype(LOW).astype(jnp.float32)
    conv0_low = conv0_low.reshape(-1, width)
    small_there[6:7] = column_sum(conv0_low)
    spread_taps(conv0_low, taps)
    end_loads.append(load(residual_in, own_half))
    modulation_low = jnp.concatenate(
        [modulation_grad, jnp.zeros((modulation.shape[0] - slots, 2 * width), jnp.float32)], axis=0
    ).astype(LOW)
    modulation_sum = column_sum(modulation_low.astype(jnp.float32))
    small_there[11:12] = modulation_sum[:, :width]
    small_there[12:13] = modulation_sum[:, width:]
    for load_now in conv0_loads:
        load_now.wait()
    for copy in (normed_copy, hidden1_copy):
        copy.wait_send()
    pair_copies[:] = [copy for copy in pair_copies if copy is not normed_copy and copy is not hidden1_copy]
    back = Return(place, mate_out, ret_in, ret_sem)
    mate_out[1 - core] = dot(taps[...], channels(wbuf, 1 - core), NT).astype(LOW)
    back.start_other()
    weight_grad("conv0a", hall0, three(0))
    stage("conv1b", 2)
    mate_out[core] = dot(taps[...], channels(wbuf, core), NT).astype(LOW)
    back.start_own()
    small_swap = Swap(place, small_there, small_in.at[4], end_sem.at[1])
    weight_grad("conv0b", hall0, three(1))
    stage("conv0a", 1)
    stage("proj", 2)
    weight_grad("conv0c", hall0, three(2))
    stage("conv1c", 2)
    stage("conv0b", 1)
    weight_grad("aff", emb_all, modulation_low)
    emb_out[...] = dot(modulation_low, channels(abuf, 1 - level), NT).astype(LOW)
    emb_copy = to(3, place.mate, emb_out, emb_in)
    emb_own = dot(modulation_low, channels(abuf, level), NT)
    stage("qkv", 3)
    stage("conv1a", 3)
    stage("conv0c", 1)
    stage("conv0a", 2)
    stage("aff", 1)
    stage("conv1b", 3)
    stage("proj", 3)
    for load_now in end_loads:
        load_now.wait()
    joined = dot(both(aall), pbuf[...].reshape(-1, width)) + par_own[10:11]
    block = mask[:, None] * (own_half[...] + joined).reshape(shape)
    block_out[...] = block.reshape(-1, width).astype(LOW)
    stage("conv0b", 2)
    stage("conv1c", 3)
    emb_copy.wait_recv()
    emb_sum[...] = (emb_own + emb_in[...].astype(jnp.float32)).astype(LOW)
    emb_end_copy = Swap(place, emb_sum, emb_end, end_sem.at[2])
    stage("conv0c", 2)
    stage("aff", 2)
    normal, scale = normalize(img[...].astype(jnp.float32).reshape(shape), average)
    slope = silu_slope(normal * par_own[0:1] + par_own[3:4])
    stage("conv0a", 3)
    back.wait_recv()
    grad = (ret_in[0].astype(jnp.float32) + ret_in[1].astype(jnp.float32)).reshape(shape) * slope
    small_here[0:1] = column_sum(grad * normal)
    small_here[3:4] = column_sum(grad)
    small_swap.wait_recv()
    small[0] = small_here[...] + small_in[4]
    small_copies = []

    def small_step(at, target):
        small_copies.append(remote(small.at[at], small_in.at[at], small_send.at[at], small_recv.at[at], target))

    def small_add(at):
        small_copies[at].wait_recv()
        small[at + 1] = small[at] + small_in[at]

    small_step(0, place.mate)
    images_part = normalize_back(grad * par_own[0:1], normal, scale, average)
    img_grad[...] = (images_part.reshape(-1, width) + rgrad[...]).astype(LOW)
    small_add(0)
    small_step(1, place.pmate)
    stage("qkv", 4)
    stage("conv1a", 4)
    stage("conv0b", 3)
    small_add(1)
    small_step(2, place.xmate)
    stage("conv1b", 4)
    stage("proj", 4)
    stage("conv0c", 3)
    small_add(2)
    small_step(3, place.ymate)
    stage("aff", 3)
    stage("conv1c", 4)
    stage("conv0a", 4)
    emb_end_copy.wait_recv()
    emb_grad[...] = emb_end[...][:slots]
    stage("conv0b", 4)
    small_add(3)
    totals[...] = small[4]
    stage("conv0c", 4)
    stage("aff", 4)
    for copies in list(started.values()) + [pair_copies, small_copies, [low_copy, back, small_swap, emb_end_copy]]:
        for copy in copies:
            copy.wait_send()


def finish_kernel(
    block, img, emb, totals, conv, aff, qkv, proj,
    block_out, img_out, emb_out, gains_out, shifts_out, biases_out, conv_out, aff_out, qkv_out, proj_out,
):
    width = proj.shape[1]
    block_out[...] = block[...]
    img_out[...] = img[...]
    emb_out[...] = emb[...]
    gains_out[...] = totals[0:3]
    shifts_out[...] = totals[3:6]
    biases_out[...] = totals[6:13]
    conv_out[...] = conv[...]
    for part in range(2):
        aff_out[:, part, :] = aff[:, part * width : (part + 1) * width]
    for part in range(3):
        qkv_out[:, part, :] = qkv[:, part * width : (part + 1) * width]
    proj_out[...] = proj[...]


def fast_body(
    images, embedding, counts, norm_gains, norm_shifts, lin_biases, conv_weights, aff_weights, qkv_weights, proj_weights, cotangent
):
    slots, _, width = images.shape
    rows = slots * PIXELS
    depth = conv_weights.shape[2]
    padded = -(-slots // 16) * 16
    low, f32 = LOW, jnp.float32
    vmem, anyw = pl.BlockSpec(memory_space=pltpu.VMEM), pl.BlockSpec(memory_space=pl.ANY)
    smem = pl.BlockSpec(memory_space=pltpu.SMEM)
    dma, buf, shape = pltpu.SemaphoreType.DMA, pltpu.VMEM, jax.ShapeDtypeStruct

    def whole(columns):
        return GRID + (depth, columns * width)

    pair = (2, rows, width)
    one = (rows, width)
    par = (16, width)
    few = (padded, width)
    middle = [
        (pair, low), (pair, low), (one, f32), ((slots, width), f32), ((padded, 2 * width), f32), ((2,) + few, low), (par, f32),
        (pair, low), (one, low), (one, f32), (one, f32), ((slots, width), f32), ((rows, 3 * width), low),
    ]
    img, cot = images.reshape(one), cotangent.reshape(one)
    kept = pl.pallas_call(
        forward_kernel,
        name="gather_forward",
        out_shape=[shape(whole(24), low)] + [shape(*each) for each in middle],
        in_specs=[smem] + [vmem] * 8 + [anyw] * 2,
        out_specs=[anyw] * 14,
        scratch_shapes=[buf(whole(24), low)] + [buf(*each) for each in middle] + [
            buf((3, rows, width), f32), buf((rows, 3 * width), f32), buf((rows, 3 * width), low), buf(one, f32),
            buf(one, low), buf(one, low), buf(one, low), buf(few, low), buf(par, f32),
            buf(one, low), buf(one, low), buf(one, low), buf((depth, 2 * width), low), buf((depth, 3 * width), low),
            dma((2,)), dma((9, 3, 3)), dma((9, 3)), dma((9, 3)), dma((9, 2, 3)), dma((9, 2, 3)), dma((2, 3)), dma((2, 6)), dma((3,)), dma((3,)), dma((22,)),
        ],
        compiler_params=pltpu.CompilerParams(collective_id=0, has_side_effects=True, vmem_limit_bytes=60 * 2**20),
    )(counts, img, embedding, norm_gains, norm_shifts, lin_biases, cot, aff_weights, qkv_weights, conv_weights, proj_weights)
    results = pl.pallas_call(
        backward_kernel,
        name="backward_scatter",
        out_shape=[
            shape(one, low), shape(one, low), shape((slots, width), low), shape(par, f32),
            shape(conv_weights.shape, f32), shape((depth, 2 * width), f32), shape((depth, 3 * width), f32), shape((depth, width), f32),
        ],
        in_specs=[smem] + [vmem] * 5 + [anyw] * 14,
        out_specs=[vmem] * 8,
        scratch_shapes=[buf(*each) for at, each in enumerate(middle) if at not in (8, 9)] + [
            buf(whole(24), low), buf((2, 2, 2, depth, 24 * width), low), buf((2, 2, depth, 24 * width), low),
            buf((2, depth, 24 * width), low), buf((2, depth, 24 * width), low),
            buf(whole(9), low), buf(whole(3), low), buf(whole(2), low), buf(whole(1), low),
            buf((rows, 9 * width), low), buf(pair, low), buf(one, f32), buf(one, f32),
            buf(pair, low), buf(pair, low), buf(pair, low), buf(one, low), buf(one, low),
            buf(few, low), buf(few, low), buf(few, low), buf(few, low),
            buf(one, low), buf(par, f32), buf(par, f32), buf(par, f32), buf((5,) + par, f32), buf((5,) + par, f32),
            dma((18,)), dma((9, 2, 4)), dma((9, 2, 4)), dma((9, 2, 3)), dma((4,)), dma((4,)), dma((4,)), dma((4,)), dma((3, 3)), dma((5,)),
        ],
        compiler_params=pltpu.CompilerParams(collective_id=1, has_side_effects=True, vmem_limit_bytes=63 * 2**20),
    )(counts, img, norm_gains, norm_shifts, lin_biases, cot, *kept)
    ends = pl.pallas_call(
        finish_kernel,
        name="finish",
        out_shape=[
            shape(one, low), shape(one, low), shape(embedding.shape, low), shape(norm_gains.shape, f32), shape(norm_shifts.shape, f32),
            shape(lin_biases.shape, f32), shape(conv_weights.shape, f32), shape(aff_weights.shape, f32), shape(qkv_weights.shape, f32),
            shape(proj_weights.shape, f32),
        ],
        in_specs=[vmem] * 8,
        out_specs=[vmem] * 10,
        compiler_params=pltpu.CompilerParams(vmem_limit_bytes=32 * 2**20),
    )(*results)
    return (ends[0].reshape(images.shape), ends[1].reshape(images.shape), *ends[2:])


def solution(mesh):
    return jax.shard_map(
        fast_body if mesh.shape["dp"] == 16 else body,
        mesh=mesh,
        in_specs=(
            P("dp", None, "tensor"),
            P("dp", "tensor"),
            P("dp"),
            P(None, "tensor"),
            P(None, "tensor"),
            P(None, "tensor"),
            P(None, None, "dp", "tensor"),
            P("dp", None, "tensor"),
            P("dp", None, "tensor"),
            P("dp", "tensor"),
            P("dp", None, "tensor"),
        ),
        out_specs=(
            P("dp", None, "tensor"),
            P("dp", None, "tensor"),
            P("dp", "tensor"),
            P(None, "tensor"),
            P(None, "tensor"),
            P(None, "tensor"),
            P(None, None, "dp", "tensor"),
            P("dp", None, "tensor"),
            P("dp", None, "tensor"),
            P("dp", "tensor"),
        ),
        check_vma=False,
    )
```

```python
import math

import jax
import jax.numpy as jnp
from jax import lax
from jax.experimental import pallas as pl
from jax.experimental.pallas import tpu as pltpu
from jax.sharding import PartitionSpec as P

C = 768
HEAD_DIM = 64
GROUPS = 32
SIDE = 8
PIXELS = 64
GROUP_SIZE = C // GROUPS
LOW = jnp.bfloat16
MESH = pl.DeviceIdType.MESH
NT = (((1,), (1,)), ((), ()))
TN = (((0,), (0,)), ((), ()))
GRID = (2, 2, 2, 2)


def group_norm(values, gain_vec, shift_vec):
    batch_size = values.shape[0]
    grouped = values.reshape(batch_size, PIXELS, -1, C // GROUPS)
    centre = jnp.mean(grouped, axis=(1, 3), keepdims=True)
    spread = jnp.mean(jnp.square(grouped - centre), axis=(1, 3), keepdims=True)
    normal = ((grouped - centre) * lax.rsqrt(spread + 1e-05)).reshape(values.shape)
    return normal * gain_vec + shift_vec


def first_norm(values, gain_vec, shift_vec):
    return jax.nn.silu(group_norm(values, gain_vec, shift_vec))


def middle(conv_values, modulation, gain_vec, shift_vec):
    scaled = (
        group_norm(conv_values, gain_vec, shift_vec) * (1.0 + modulation[:, 0:1])
        + modulation[:, 1:2]
    )
    return jax.nn.silu(scaled)


def windows(source):
    slot_count = source.shape[0]
    padded = jnp.pad(source.reshape(slot_count, SIDE, SIDE, -1), ((0, 0), (1, 1), (1, 1), (0, 0)))
    found = []
    for tap_index in range(9):
        row_shift = tap_index // 3
        col_shift = tap_index % 3
        found.append(
            padded[:, row_shift : row_shift + SIDE, col_shift : col_shift + SIDE].reshape(
                slot_count * PIXELS, -1
            )
        )
    return found


def convolve(source, kernel):
    slot_count = source.shape[0]
    summed = jnp.zeros((slot_count * PIXELS, kernel.shape[2]), jnp.float32)
    for tap_index, window in enumerate(windows(source)):
        summed = summed + jnp.dot(window, kernel[tap_index], preferred_element_type=jnp.float32)
    return summed.reshape(slot_count, PIXELS, -1)


def convolve_back(grad_low, kernel):
    slot_count = grad_low.shape[0]
    flattened = grad_low.reshape(slot_count * PIXELS, -1)
    summed = jnp.zeros((slot_count, SIDE + 2, SIDE + 2, kernel.shape[1]), jnp.float32)
    for tap_index in range(9):
        row_shift = tap_index // 3
        col_shift = tap_index % 3
        contrib = jnp.einsum(
            "rd,cd->rc", flattened, kernel[tap_index], preferred_element_type=jnp.float32
        )
        contrib = contrib.reshape(slot_count, SIDE, SIDE, -1)
        summed = summed + jnp.pad(
            contrib, ((0, 0), (row_shift, 2 - row_shift), (col_shift, 2 - col_shift), (0, 0))
        )
    return summed[:, 1 : SIDE + 1, 1 : SIDE + 1].reshape(slot_count, PIXELS, -1)


def conv_weight_grad(source, grad_low):
    slot_count = source.shape[0]
    flattened = grad_low.reshape(slot_count * PIXELS, -1)
    found = [
        jnp.einsum("rc,rd->cd", window, flattened, preferred_element_type=jnp.float32)
        for window in windows(source)
    ]
    return jnp.stack(found)


def gather_features(values_low):
    return lax.all_gather(values_low, "tensor", axis=2, tiled=True)


def back_features(partial_sum):
    return lax.psum_scatter(
        partial_sum.astype(jnp.bfloat16), "tensor", scatter_dimension=2, tiled=True
    ).astype(jnp.float32)


def body(
    images,
    embedding,
    counts,
    norm_gains,
    norm_shifts,
    lin_biases,
    conv_weights,
    aff_weights,
    qkv_weights,
    proj_weights,
    cotangent,
):
    slot_count = images.shape[0]
    score_scale = HEAD_DIM ** (-0.5)
    slot_mask = (jnp.arange(slot_count, dtype=jnp.int32) < counts[0]).astype(jnp.float32)
    conv_full = lax.all_gather(conv_weights, "dp", axis=2, tiled=True)
    aff_full, qkv_full, proj_full = (
        lax.all_gather(aff_weights, "dp", axis=0, tiled=True),
        lax.all_gather(qkv_weights, "dp", axis=0, tiled=True),
        lax.all_gather(proj_weights, "dp", axis=0, tiled=True),
    )
    images_f = images.astype(jnp.float32)
    hidden0 = first_norm(images_f, norm_gains[0], norm_shifts[0]).astype(jnp.bfloat16)
    hidden0_all, embed_all = (
        lax.all_gather(hidden0, "tensor", axis=2, tiled=True),
        lax.all_gather(embedding, "tensor", axis=1, tiled=True),
    )
    conv_out0 = convolve(hidden0_all, conv_full[0]) + lin_biases[0]
    modulation = (
        jnp.einsum("sc,cjd->sjd", embed_all, aff_full, preferred_element_type=jnp.float32)
        + lin_biases[5:7]
    )
    hidden1 = middle(conv_out0, modulation, norm_gains[1], norm_shifts[1]).astype(jnp.bfloat16)
    hidden1_all = gather_features(hidden1)
    residual = images_f + (convolve(hidden1_all, conv_full[1]) + lin_biases[1])
    normed = group_norm(residual, norm_gains[2], norm_shifts[2]).astype(jnp.bfloat16)
    normed_all = gather_features(normed)
    bias_rows = jnp.stack([lin_biases[2], jnp.zeros_like(lin_biases[2]), lin_biases[3]])
    projected = (
        jnp.einsum("spc,cjd->spjd", normed_all, qkv_full, preferred_element_type=jnp.float32)
        + bias_rows
    ).astype(jnp.bfloat16)
    head_shape = (slot_count, PIXELS, -1, HEAD_DIM)
    query_heads = projected[:, :, 0].reshape(head_shape)
    key_heads = projected[:, :, 1].reshape(head_shape)
    value_heads = projected[:, :, 2].reshape(head_shape)
    scores = (
        jnp.einsum("sqhd,skhd->shqk", query_heads, key_heads, preferred_element_type=jnp.float32)
        * score_scale
    )
    log_total = jax.scipy.special.logsumexp(scores, axis=-1, keepdims=True)
    probabilities = jnp.exp(scores - log_total)
    weights_low = probabilities.astype(jnp.bfloat16)
    attended = jnp.einsum(
        "shqk,skhd->sqhd", weights_low, value_heads, preferred_element_type=jnp.float32
    )
    attended = attended.reshape(slot_count, PIXELS, -1).astype(jnp.bfloat16)
    attended_all = gather_features(attended)
    branch = (
        jnp.einsum("spc,cd->spd", attended_all, proj_full, preferred_element_type=jnp.float32)
        + lin_biases[4]
    )
    block_output = (slot_mask[:, None, None] * (residual + branch)).astype(jnp.bfloat16)
    conv_back = lax.all_gather(conv_weights, "dp", axis=2, tiled=True)
    aff_back, qkv_back, proj_back = (
        lax.all_gather(aff_weights, "dp", axis=0, tiled=True),
        lax.all_gather(qkv_weights, "dp", axis=0, tiled=True),
        lax.all_gather(proj_weights, "dp", axis=0, tiled=True),
    )
    grad_branch = slot_mask[:, None, None] * cotangent
    branch_low = grad_branch.astype(jnp.bfloat16)
    proj_grad = jnp.einsum(
        "spc,spd->cd", attended_all, branch_low, preferred_element_type=jnp.float32
    )
    proj_bias_grad = jnp.sum(branch_low.astype(jnp.float32), axis=(0, 1))
    attended_grad = back_features(
        jnp.einsum("spd,cd->spc", branch_low, proj_back, preferred_element_type=jnp.float32)
    )
    attended_low = attended_grad.astype(jnp.bfloat16).reshape(head_shape)
    grad_probs = jnp.einsum(
        "sqhd,skhd->shqk", attended_low, value_heads, preferred_element_type=jnp.float32
    )
    value_grad = jnp.einsum(
        "shqk,sqhd->skhd", weights_low, attended_low, preferred_element_type=jnp.float32
    )
    score_grad = probabilities * (
        grad_probs - jnp.sum(grad_probs * probabilities, axis=-1, keepdims=True)
    )
    score_low = score_grad.astype(jnp.bfloat16)
    query_grad = (
        jnp.einsum("shqk,skhd->sqhd", score_low, key_heads, preferred_element_type=jnp.float32)
        * score_scale
    )
    key_grad = (
        jnp.einsum("shqk,sqhd->skhd", score_low, query_heads, preferred_element_type=jnp.float32)
        * score_scale
    )
    flat_shape = (slot_count, PIXELS, -1)
    projected_grad = jnp.stack(
        [
            query_grad.reshape(flat_shape),
            key_grad.reshape(flat_shape),
            value_grad.reshape(flat_shape),
        ],
        axis=2,
    ).astype(jnp.bfloat16)
    qkv_grad = jnp.einsum(
        "spc,spjd->cjd", normed_all, projected_grad, preferred_element_type=jnp.float32
    )
    qkv_bias_grad = jnp.sum(projected_grad.astype(jnp.float32), axis=(0, 1))
    normed_grad = back_features(
        jnp.einsum("spjd,cjd->spc", projected_grad, qkv_back, preferred_element_type=jnp.float32)
    )
    norm_value, norm_pull = jax.vjp(group_norm, residual, norm_gains[2], norm_shifts[2])
    residual_grad, gain2_grad, shift2_grad = norm_pull(normed_grad)
    residual_grad = residual_grad + grad_branch
    conv1_low = residual_grad.astype(jnp.bfloat16)
    conv1_bias_grad = jnp.sum(conv1_low.astype(jnp.float32), axis=(0, 1))
    conv1_wgrad = conv_weight_grad(hidden1_all, conv1_low)
    hidden1_grad = back_features(convolve_back(conv1_low, conv_back[1]))
    middle_value, middle_pull = jax.vjp(
        middle, conv_out0, modulation, norm_gains[1], norm_shifts[1]
    )
    conv0_grad, modulation_grad, gain1_grad, shift1_grad = middle_pull(hidden1_grad)
    modulation_low = modulation_grad.astype(jnp.bfloat16)
    aff_bias_grad = jnp.sum(modulation_low.astype(jnp.float32), axis=0)
    aff_grad = jnp.einsum(
        "sc,sjd->cjd", embed_all, modulation_low, preferred_element_type=jnp.float32
    )
    embed_part = jnp.einsum(
        "sjd,cjd->sc", modulation_low, aff_back, preferred_element_type=jnp.float32
    )
    conv0_low = conv0_grad.astype(jnp.bfloat16)
    conv0_bias_grad = jnp.sum(conv0_low.astype(jnp.float32), axis=(0, 1))
    conv0_wgrad = conv_weight_grad(hidden0_all, conv0_low)
    hidden0_part = convolve_back(conv0_low, conv_back[0])
    hidden0_grad, embedding_sum = (
        lax.psum_scatter(
            hidden0_part.astype(jnp.bfloat16), "tensor", scatter_dimension=2, tiled=True
        ).astype(jnp.float32),
        lax.psum_scatter(
            embed_part.astype(jnp.bfloat16), "tensor", scatter_dimension=1, tiled=True
        ).astype(jnp.float32),
    )
    first_value, first_pull = jax.vjp(first_norm, images_f, norm_gains[0], norm_shifts[0])
    images_part, gain0_grad, shift0_grad = first_pull(hidden0_grad)
    images_grad = (images_part + residual_grad).astype(jnp.bfloat16)
    gains_local = jnp.stack([gain0_grad, gain1_grad, gain2_grad])
    shifts_local = jnp.stack([shift0_grad, shift1_grad, shift2_grad])
    biases_local = jnp.stack(
        [
            conv0_bias_grad,
            conv1_bias_grad,
            qkv_bias_grad[0],
            qkv_bias_grad[2],
            proj_bias_grad,
            aff_bias_grad[0],
            aff_bias_grad[1],
        ]
    )
    gains_grad, shifts_grad, biases_grad = lax.psum((gains_local, shifts_local, biases_local), "dp")
    conv_local = jnp.stack([conv0_wgrad, conv1_wgrad])
    conv_summed, aff_summed, qkv_summed, proj_summed = (
        lax.psum_scatter(conv_local, "dp", scatter_dimension=2, tiled=True),
        lax.psum_scatter(aff_grad, "dp", scatter_dimension=0, tiled=True),
        lax.psum_scatter(qkv_grad, "dp", scatter_dimension=0, tiled=True),
        lax.psum_scatter(proj_grad, "dp", scatter_dimension=0, tiled=True),
    )
    return (
        block_output,
        images_grad,
        embedding_sum.astype(jnp.bfloat16),
        gains_grad,
        shifts_grad,
        biases_grad,
        conv_summed,
        aff_summed,
        qkv_summed,
        proj_summed,
    )


def dot(left, right, dims=(((1,), (0,)), ((), ()))):
    return lax.dot_general(left, right, dims, preferred_element_type=jnp.float32)


def device(pair, level, y, x, core):
    return {"dp": ((2 * pair + level) * 2 + y) * 2 + x, "tensor": core}


class Place:
    def __init__(self):
        spot, core = lax.axis_index("dp"), lax.axis_index("tensor")
        self.pair, self.level = spot // 8, lax.rem(spot // 4, 2)
        self.y, self.x, self.core = lax.rem(spot // 2, 2), lax.rem(spot, 2), core
        pair, level, y, x = self.pair, self.level, self.y, self.x
        self.home = level == core
        self.away = level != core
        self.mate = device(pair, 1 - level, y, x, core)
        self.pmate = device(1 - pair, level, y, x, core)
        self.xmate = device(pair, level, y, 1 - x, core)
        self.ymate = device(pair, level, 1 - y, x, core)
        self.cmate = device(pair, level, y, x, 1 - core)
        self.swap = device(pair, core, y, x, level)
        self.far = device(1 - pair, core, y, x, level)

    def greet(self):
        barrier = pltpu.get_barrier_semaphore()
        for other in (self.mate, self.pmate, self.xmate, self.ymate, self.cmate, self.far):
            pl.semaphore_signal(barrier, inc=1, device_id=other, device_id_type=MESH)

        @pl.when(self.away)
        def _():
            pl.semaphore_signal(barrier, inc=1, device_id=self.swap, device_id_type=MESH)

    def meet(self):
        barrier = pltpu.get_barrier_semaphore()

        @pl.when(self.home)
        def _():
            pl.semaphore_wait(barrier, 6)

        @pl.when(self.away)
        def _():
            pl.semaphore_wait(barrier, 7)


class Swap:
    def __init__(self, place, src, dst, sems):
        self.place = place
        self.local = pltpu.make_async_copy(src, dst, sems.at[0])
        self.remote = remote_copy(src, dst, sems.at[1], sems.at[2], place.swap)
        pl.when(place.home)(self.local.start)
        pl.when(place.away)(self.remote.start)

    def wait_recv(self):
        pl.when(self.place.home)(self.local.wait)
        pl.when(self.place.away)(self.remote.wait_recv)

    def wait_send(self):
        pl.when(self.place.away)(self.remote.wait_send)


class Share:
    def __init__(self, place, src, dst_ref, sems):
        self.place = place
        core = place.core
        dst = dst_ref.at[core]
        self.near_copy = remote_copy(src, dst, sems.at[0], sems.at[1], place.cmate)
        self.mate_copy = remote_copy(src, dst, sems.at[2], sems.at[3 + core], place.mate)
        self.swap_copy = remote_copy(src, dst, sems.at[2], sems.at[3 + core], place.swap)
        self.local = pltpu.make_async_copy(src, dst, sems.at[5])
        self.others = [remote_copy(src, dst, sems.at[2], sems.at[3 + part], place.mate) for part in range(2)]

        @pl.when(place.home)
        def _():
            self.mate_copy.start()
            self.local.start()

        @pl.when(place.away)
        def _():
            self.swap_copy.start()
            self.near_copy.start()

    def wait_recv(self):
        @pl.when(self.place.home)
        def _():
            self.local.wait()
            self.near_copy.wait_recv()

        @pl.when(self.place.away)
        def _():
            self.others[0].wait_recv()
            self.others[1].wait_recv()

    def wait_send(self):
        self.mate_copy.wait_send()
        pl.when(self.place.away)(self.near_copy.wait_send)


class Return:
    def __init__(self, place, src_ref, dst_ref, sems):
        self.place, self.src_ref, self.dst_ref, self.sems = place, src_ref, dst_ref, sems
        core = place.core
        self.near_copy = remote_copy(src_ref.at[1 - core], dst_ref.at[0], sems.at[0], sems.at[1], place.cmate)
        self.swap_copy = remote_copy(src_ref.at[1 - core], dst_ref.at[1], sems.at[0], sems.at[2], place.swap)
        self.local = pltpu.make_async_copy(src_ref.at[core], dst_ref.at[0], sems.at[3])
        self.mate_copy = remote_copy(src_ref.at[core], dst_ref.at[1], sems.at[4], sems.at[2], place.mate)

    def start_other(self):
        pl.when(self.place.home)(self.near_copy.start)
        pl.when(self.place.away)(self.swap_copy.start)

    def start_own(self):
        pl.when(self.place.home)(self.local.start)
        pl.when(self.place.away)(self.mate_copy.start)

    def wait_recv(self):
        pl.when(self.place.home)(self.local.wait)
        pl.when(self.place.away)(self.near_copy.wait_recv)
        self.swap_copy.wait_recv()

    def wait_send(self):
        self.near_copy.wait_send()
        pl.when(self.place.away)(self.mate_copy.wait_send)


def halves(start, size):
    first = (size // 128 + 1) // 2 * 128
    return [(start, first, 0), (start + first, size - first, 1)]


def remote_copy(src, dst, send, recv, target):
    return pltpu.make_async_remote_copy(
        src_ref=src, dst_ref=dst, send_sem=send, recv_sem=recv, device_id=target, device_id_type=MESH
    )


def remote(src, dst, send, recv, target):
    copy = remote_copy(src, dst, send, recv, target)
    copy.start()
    return copy


def group_average(width):
    row = lax.broadcasted_iota(jnp.int32, (width, width), 0) // GROUP_SIZE
    col = lax.broadcasted_iota(jnp.int32, (width, width), 1) // GROUP_SIZE
    return jnp.where(row == col, 1.0 / (GROUP_SIZE * PIXELS), 0.0).astype(jnp.float32)


def group_mean(values, average):
    return lax.dot_general(
        jnp.sum(values, axis=1), average, (((1,), (0,)), ((), ())),
        precision=lax.Precision.HIGHEST, preferred_element_type=jnp.float32,
    )


def normalize(values, average):
    away = values - group_mean(values, average)[:, None]
    scale = lax.rsqrt(group_mean(away * away, average) + 1e-05)
    return away * scale[:, None], scale


def normalize_back(grad, normal, scale, average):
    return scale[:, None] * (
        grad - group_mean(grad, average)[:, None] - normal * group_mean(grad * normal, average)[:, None]
    )


def sigmoid(values):
    return 1.0 / (1.0 + jnp.exp(-values))


def silu_slope(values):
    gate = sigmoid(values)
    return gate * (1.0 + values * (1.0 - gate))


def shift_columns(values, step):
    moved = pltpu.roll(values, step % SIDE, 1)
    column = lax.broadcasted_iota(jnp.int32, values.shape, 1)
    return jnp.where(column == (0 if step == 1 else SIDE - 1), 0.0, moved)


def shift_rows(values, step):
    if step == 0:
        return values
    zero = jnp.zeros_like(values[:, :1])
    if step == 1:
        return jnp.concatenate([zero, values[:, : SIDE - 1]], axis=1)
    return jnp.concatenate([values[:, 1:], zero], axis=1)


def both(ref):
    return jnp.concatenate([ref[0], ref[1]], axis=1)


def convolve_row(source, weights, row_tap, sums, first=False):
    rows, width = sums.shape[1:]
    products = dot(source, weights)
    for col_tap in range(3):
        part = products[:, col_tap * width : (col_tap + 1) * width]
        part = shift_rows(part.reshape(-1, SIDE, SIDE, width), 1 - row_tap).reshape(rows, width)
        sums[col_tap] = part if first else sums[col_tap] + part


def convolve_end(sums):
    rows, width = sums.shape[1:]
    grids = [sums[col_tap].reshape(rows // SIDE, SIDE, width) for col_tap in range(3)]
    return (shift_columns(grids[0], 1) + grids[1] + shift_columns(grids[2], -1)).reshape(rows, width)


def spread_taps(grad, taps_ref):
    rows, width = grad.shape
    flat = grad.reshape(rows // SIDE, SIDE, width)
    for col_tap, grid in enumerate((shift_columns(flat, -1), flat, shift_columns(flat, 1))):
        for row_tap in range(3):
            moved = shift_rows(grid.reshape(-1, SIDE, SIDE, width), row_tap - 1)
            tap = row_tap * 3 + col_tap
            taps_ref[:, tap * width : (tap + 1) * width] = moved.reshape(rows, width).astype(LOW)


def expand_heads(block, lane_head, heads):
    return jnp.concatenate([jnp.where(lane_head == h, block, jnp.zeros_like(block)) for h in range(heads)], axis=0)


def contract_heads(wide, lane_head, heads):
    total = wide[:PIXELS]
    for h in range(1, heads):
        total = jnp.where(lane_head == h, wide[h * PIXELS : (h + 1) * PIXELS], total)
    return total


def attention(slots, projected, attended_grad, attended, projected_grad):
    width = attended.shape[1]
    heads = width // HEAD_DIM
    scale = HEAD_DIM ** (-0.5)
    lane_head = lax.broadcasted_iota(jnp.int32, (PIXELS, width), 1) // HEAD_DIM

    def one_slot(slot, carry):
        rows = pl.ds(pl.multiple_of(slot * PIXELS, PIXELS), PIXELS)
        query, key, value = (projected[rows, part * width : (part + 1) * width] for part in range(3))
        query_wide = expand_heads(query, lane_head, heads)
        scores = dot(query_wide, key, NT) * scale
        powers = jnp.exp(scores - jnp.max(scores, axis=1, keepdims=True))
        probabilities = powers / jnp.sum(powers, axis=1, keepdims=True)
        weights_low = probabilities.astype(LOW)
        attended[rows, :] = contract_heads(dot(weights_low, value), lane_head, heads).astype(LOW)
        grad_wide = expand_heads(attended_grad[rows, :], lane_head, heads)
        grad_probs = dot(grad_wide, value, NT)
        value_grad = dot(weights_low, grad_wide, TN)
        score_low = (
            probabilities * (grad_probs - jnp.sum(grad_probs * probabilities, axis=1, keepdims=True))
        ).astype(LOW)
        query_grad = contract_heads(dot(score_low, key), lane_head, heads) * scale
        key_grad = dot(score_low, query_wide, TN) * scale
        for part, grad in enumerate((query_grad, key_grad, value_grad)):
            projected_grad[rows, part * width : (part + 1) * width] = grad.astype(LOW)
        return carry

    lax.fori_loop(0, slots, one_slot, 0, unroll=2)


CONV0, AFF, CONV1, PROJ, QKV = 0, 9, 11, 20, 21
LAG = 2


def own_parameters(gains, shifts, biases, par):
    par[...] = jnp.zeros_like(par)
    par[0:3] = gains[...]
    par[3:6] = shifts[...]
    par[6:13] = biases[...]


def slot_mask(counts, slots, width):
    return (lax.broadcasted_iota(jnp.int32, (slots, width), 0) < counts[0]).astype(jnp.float32)


def forward_kernel(
    counts, img, emb, gains, shifts, biases, cot, aff, qkv, conv, proj,
    full_out, hall0_out, hall1_out, normal1_out, scale1_out, modulation_out, emb_all_out, par_out,
    nall_out, attended_out, residual_out, normal2_out, scale2_out, pgrad_out,
    full, hall0, hall1, normal1, scale1, modulation, emb_all, par, nall, attended, residual, normal2, scale2, pgrad,
    sums, wide, projected, ag_own, ag_send, ag_recv, ag_low, emb_own, par_own, hidden_own, conv_own, conv_in, aff_own,
    first_local, first_send, first_recv, sends, recvs, swap_sem, share_sem, mate_send, mate_recv, out_sem,
):
    place = Place()
    pair, level, y, x, core = place.pair, place.level, place.y, place.x, place.core
    width = img.shape[1]
    slots = scale1.shape[0]
    shape = (slots, PIXELS, width)
    place.greet()
    groups = [
        (CONV0, 3, [(conv.at[0, tap], CONV0 + tap, 1) for tap in (0, 1, 2)], True),
        (CONV0 + 3, 3, [(conv.at[0, tap], CONV0 + tap, 1) for tap in (3, 4, 5)], True),
        (AFF, 2, [(aff_own, AFF, 2)], True),
        (CONV0 + 6, 3, [(conv.at[0, tap], CONV0 + tap, 1) for tap in (6, 7, 8)], True),
        (CONV1, 3, [(conv.at[1, tap], CONV1 + tap, 1) for tap in (0, 1, 2)], True),
        (CONV1 + 3, 3, [(conv.at[1, tap], CONV1 + tap, 1) for tap in (3, 4, 5)], True),
        (CONV1 + 6, 3, [(conv.at[1, tap], CONV1 + tap, 1) for tap in (6, 7, 8)], True),
        (PROJ, 1, [(proj, PROJ, 1)], False),
        (QKV, 3, [(qkv.at[part], QKV + part, 1) for part in range(3)], False),
    ]
    started = {}

    def stage(group, s):
        if not 0 <= group < len(groups):
            return
        column, count, sources, wide_way = groups[group]
        if s == 0 and wide_way:
            found = []
            for at, (src, first, many) in enumerate(sources):
                dst = full.at[pair, level, y, x, :, pl.ds(first * width, many * width)]
                found.append(remote(src, dst, first_send.at[group, at], first_recv.at[group, at], place.far))
                found.append(Swap(place, src, dst, first_local.at[group, at]))
            started[group, 0] = found
            return
        if s == 0:
            started[group, 0], started[group, "local"] = [], []
            for at, (src, first, many) in enumerate(sources):
                dst = full.at[pair, level, y, x, :, pl.ds(first * width, many * width)]
                local = pltpu.make_async_copy(src, dst, first_local.at[group, at, 0])
                local.start()
                started[group, "local"].append(local)
                started[group, 0].append(remote(src, dst, first_send.at[group, at], first_recv.at[group, at], place.mate))
            return
        if s == 1:
            for copy in started[group, 0]:
                copy.wait_recv()
            for copy in started.pop((group, "local"), []):
                copy.wait()
        for start, size, odd in halves(column * width, count * width):
            cols = pl.ds(start, size)
            for copy in started.get((group, odd, s - 1), []):
                copy.wait_recv()
            first, second = (place.ymate, place.xmate) if odd else (place.xmate, place.ymate)
            if wide_way:
                if s == 1:
                    block, target = full.at[:, core, y, x, :, cols], first
                elif s == 2:
                    block, target = (full.at[:, core, :, x, :, cols] if odd else full.at[:, core, y, :, :, cols]), second
                elif s == 3:
                    block, target = full.at[:, core, :, :, :, cols], place.cmate
            else:
                if s == 1:
                    block, target = full.at[pair, :, y, x, :, cols], place.pmate
                elif s == 2:
                    block, target = full.at[:, :, y, x, :, cols], first
                elif s == 3:
                    block, target = (full.at[:, :, :, x, :, cols] if odd else full.at[:, :, y, :, :, cols]), second
            if s < 4:
                started[group, odd, s] = [remote(block, block, sends.at[group, odd, s - 1], recvs.at[group, odd, s - 1], target)]

    pair_copies = []

    def to(target, src, dst):
        at = len(pair_copies)
        pair_copies.append(remote(src, dst, mate_send.at[at], mate_recv.at[at], target))
        return pair_copies[-1]

    def weights(column, count, part=None):
        cols = pl.ds(column * width, count * width)
        block = full[:, :, :, :, :, cols] if part is None else full[part, :, :, :, :, cols]
        return block.reshape(-1, count * width)

    out_copies = []

    def keep(src, dst):
        out_copies.append(pltpu.make_async_copy(src, dst, out_sem.at[len(out_copies)]))
        out_copies[-1].start()

    for part in range(2):
        aff_own[:, part * width : (part + 1) * width] = aff[:, part, :]
    padded = emb_own.shape[0]
    choose = lax.broadcasted_iota(jnp.int32, (padded, slots), 0) == lax.broadcasted_iota(jnp.int32, (padded, slots), 1)
    emb_own[...] = dot(choose.astype(LOW), emb[...]).astype(LOW)
    own_parameters(gains, shifts, biases, par_own)
    average = group_average(width)
    place.meet()
    stage(0, 0)
    par_copy = Swap(place, par_own, par, swap_sem.at[0])
    emb_copy = Share(place, emb_own, emb_all, share_sem.at[0])
    normal0, _ = normalize(img[...].astype(jnp.float32).reshape(shape), average)
    scaled = normal0 * par_own[0:1] + par_own[3:4]
    hidden_own[...] = (scaled * sigmoid(scaled)).reshape(-1, width).astype(LOW)
    hidden0_copy = Share(place, hidden_own, hall0, share_sem.at[1])
    branch_low = (slot_mask(counts, slots, width)[:, None] * cot[...].reshape(shape)).reshape(-1, width).astype(LOW)
    for step in range(1, len(groups) + 4 * LAG):
        stage(step, 0)
        for s in (4, 3, 2, 1):
            stage(step - s * LAG, s)
        group = step - 4 * LAG
        if group < 0:
            continue
        column, count = groups[group][:2]
        cols = pl.ds(column * width, count * width)
        keep(full.at[:, :, :, :, :, cols], full_out.at[:, :, :, :, :, cols])
        if column < AFF:
            if column == CONV0:
                par_copy.wait_recv()
                emb_copy.wait_recv()
                hidden0_copy.wait_recv()
                keep(par, par_out)
                keep(emb_all, emb_all_out)
                keep(hall0, hall0_out)
            convolve_row(both(hall0), weights(column, 3), column // 3, sums, column == CONV0)
        if column == AFF:
            changes = dot(both(emb_all), weights(AFF, 2)) + jnp.concatenate([par[11:12], par[12:13]], axis=1)
            modulation[...] = changes
            keep(modulation, modulation_out)
        if column == CONV0 + 6:
            conv_out0 = (convolve_end(sums) + par[6:7]).reshape(shape)
            normal, scale = normalize(conv_out0, average)
            scaled = (normal * par[1:2] + par[4:5]) * (1.0 + changes[:slots, None, :width]) + changes[:slots, None, width:]
            hall1[level] = (scaled * sigmoid(scaled)).reshape(-1, width).astype(LOW)
            hidden1_copy = to(place.mate, hall1.at[level], hall1.at[level])
            normal1[...] = normal.reshape(-1, width)
            scale1[...] = scale
            keep(normal1, normal1_out)
            keep(scale1, scale1_out)
        if CONV1 <= column < PROJ:
            convolve_row(hall1[level], weights(column, 3, level), (column - CONV1) // 3, sums, column == CONV1)
        if column == CONV1 + 6:
            hidden1_copy.wait_recv()
            keep(hall1, hall1_out)
            for row_tap in range(3):
                convolve_row(hall1[1 - level], weights(CONV1 + 3 * row_tap, 3, 1 - level), row_tap, sums)
            conv_own[...] = convolve_end(sums).astype(LOW)
            conv_copy = Swap(place, conv_own, conv_in, swap_sem.at[1])
        if column == PROJ:
            ag_send[...] = dot(branch_low, weights(PROJ, 1, 1 - core), NT).astype(LOW)
            ag_copy = to(place.cmate, ag_send, ag_recv)
            ag_own[...] = dot(branch_low, weights(PROJ, 1, core), NT)
    conv_copy.wait_recv()
    total = img[...].astype(jnp.float32) + (conv_in[...].astype(jnp.float32) + par_own[7:8])
    normal, scale = normalize(total.reshape(shape), average)
    nall[core] = (normal * par_own[2:3] + par_own[5:6]).reshape(-1, width).astype(LOW)
    normed_copy = to(place.cmate, nall.at[core], nall.at[core])
    residual[...] = total
    normal2[...] = normal.reshape(-1, width)
    scale2[...] = scale
    keep(residual, residual_out)
    keep(normal2, normal2_out)
    keep(scale2, scale2_out)
    bias = jnp.concatenate([par_own[8:9], jnp.zeros((1, width), jnp.float32), par_own[9:10]], axis=1)
    wide[...] = dot(nall[core], weights(QKV, 3, core)) + bias
    ag_copy.wait_recv()
    ag_low[...] = (ag_own[...] + ag_recv[...].astype(jnp.float32)).astype(LOW)
    normed_copy.wait_recv()
    keep(nall, nall_out)
    projected[...] = (wide[...] + dot(nall[1 - core], weights(QKV, 3, 1 - core))).astype(LOW)
    attention(slots, projected, ag_low, attended, pgrad)
    keep(pgrad, pgrad_out)
    keep(attended, attended_out)
    for copies in list(started.values()) + [pair_copies, [par_copy, emb_copy, hidden0_copy, conv_copy]]:
        for copy in copies:
            copy.wait_send()
    for copy in out_copies:
        copy.wait()


def backward_kernel(
    counts, img, gains, shifts, biases, cot,
    full, hall0_in, hall1_in, normal1_in, scale1_in, modulation_in, emb_all_in, par_in,
    nall_in, attended_in, residual_in, normal2_in, scale2_in, pgrad_in,
    block_out, img_grad, emb_grad, gains_grad, shifts_grad, biases_grad, conv_grad, aff_grad, qkv_grad, proj_grad,
    hall0, hall1, normal1, scale1, modulation, emb_all, par, nall, normal2, scale2, pgrad,
    work, r0, r1, r2, last, wbuf, qbuf, abuf, pbuf, taps, aall, rgrad, own_half, mate_out, mate_in, ret_in, low_own, low_in,
    emb_out, emb_in, emb_sum, emb_end, branch, par_own, small_here, small_there, small, small_in,
    load_sem, sends, recvs, swap_sem, small_send, small_recv, mate_send, mate_recv, end_sem, ret_sem,
):
    place = Place()
    pair, level, y, x, core = place.pair, place.level, place.y, place.x, place.core
    width = img.shape[1]
    slots = scale1.shape[0]
    shape = (slots, PIXELS, width)
    place.greet()
    loads = []

    def load(src, dst):
        loads.append(pltpu.make_async_copy(src, dst, load_sem.at[len(loads)]))
        loads[-1].start()
        return loads[-1]

    def load_weights(column, count, dst):
        return load(full.at[:, :, :, :, :, pl.ds(column * width, count * width)], dst)

    pgrad_load = load(pgrad_in, pgrad)
    qkv_load = load_weights(QKV, 3, qbuf)
    attended_load = load(attended_in, aall.at[core])
    normed_loads = [load(nall_in, nall), load(normal2_in, normal2), load(scale2_in, scale2)]
    conv1_loads = [load_weights(CONV1, 9, wbuf), load(hall1_in, hall1)]
    middle_loads = [load(normal1_in, normal1), load(scale1_in, scale1), load(modulation_in, modulation), load(par_in, par)]
    conv0_loads = [load(hall0_in, hall0), load(emb_all_in, emb_all), load_weights(AFF, 2, abuf)]
    end_loads = [load_weights(PROJ, 1, pbuf)]
    pair_copies = []

    def to(at, target, src, dst):
        pair_copies.append(remote(src, dst, mate_send.at[at], mate_recv.at[at], target))
        return pair_copies[-1]

    groups = {
        "qkv": (0, QKV, 3, False), "proj": (1, PROJ, 1, False),
        "conv1a": (2, CONV1, 3, True), "conv1b": (3, CONV1 + 3, 3, True), "conv1c": (4, CONV1 + 6, 3, True),
        "conv0a": (5, CONV0, 3, True), "conv0b": (6, CONV0 + 3, 3, True), "conv0c": (7, CONV0 + 6, 3, True), "aff": (8, AFF, 2, True),
    }
    started = {}

    def deliver(start, size, value):
        column, offset = start // width, start % width
        while size:
            now = min(size, width - offset)
            part, value = value[:, :now], value[:, now:]
            if column < AFF or CONV1 <= column < PROJ:
                tap = column if column < AFF else column - CONV1 + 9
                conv_grad[tap // 9, tap % 9, :, offset : offset + now] = part
            else:
                ref, first = (aff_grad, AFF) if column < CONV1 else (proj_grad, PROJ) if column < QKV else (qkv_grad, QKV)
                if ref is proj_grad:
                    ref[:, offset : offset + now] = part
                elif ref is qkv_grad:
                    ref[column - first, :, offset : offset + now] = part
                else:
                    ref[:, column - first, offset : offset + now] = part
            column, offset, size = column + 1, 0, size - now

    def add(at, cols, received):
        total = work[at + (slice(None), cols)].astype(jnp.float32) + received.astype(jnp.float32)
        work[at + (slice(None), cols)] = total.astype(LOW)

    def stage(name, s):
        group, column, count, wide_way = groups[name]
        for start, size, odd in halves(column * width, count * width):
            cols = pl.ds(start, size)
            for copy in started.get((group, odd, s - 1), []):
                copy.wait_recv()
            first, second = (place.ymate, place.xmate) if odd else (place.xmate, place.ymate)
            if wide_way:
                if s == 0:
                    src, dst, target = work.at[:, 1 - core, :, :, :, cols], r0.at[:, :, :, :, cols], place.cmate
                elif s == 1:
                    for pp in range(2):
                        for yy in range(2):
                            for xx in range(2):
                                add((pp, core, yy, xx), cols, r0[pp, yy, xx, :, cols])
                    src = work.at[:, core, 1 - y, :, :, cols] if odd else work.at[:, core, :, 1 - x, :, cols]
                    dst, target = r1.at[:, :, :, cols], first
                elif s == 2:
                    for pp in range(2):
                        for other in range(2):
                            add((pp, core, y, other) if odd else (pp, core, other, x), cols, r1[pp, other, :, cols])
                    src = work.at[:, core, y, 1 - x, :, cols] if odd else work.at[:, core, 1 - y, x, :, cols]
                    dst, target = r2.at[:, :, cols], second
                elif s == 3:
                    for pp in range(2):
                        add((pp, core, y, x), cols, r2[pp, :, cols])
                    far = remote(
                        work.at[1 - pair, core, y, x, :, cols], last.at[1, :, cols], sends.at[group, odd, 3], recvs.at[group, odd, 3], place.far
                    )
                    started[group, odd, 3] = [
                        far, Swap(place, work.at[pair, core, y, x, :, cols], last.at[0, :, cols], swap_sem.at[group, odd])
                    ]
                    continue
                else:
                    deliver(start, size, last[0, :, cols].astype(jnp.float32) + last[1, :, cols].astype(jnp.float32))
                    continue
            else:
                if s == 0:
                    src = work.at[:, :, 1 - y, :, :, cols] if odd else work.at[:, :, :, 1 - x, :, cols]
                    dst, target = r0.at[:, :, :, :, cols], first
                elif s == 1:
                    for pp in range(2):
                        for ll in range(2):
                            for other in range(2):
                                add((pp, ll, y, other) if odd else (pp, ll, other, x), cols, r0[pp, ll, other, :, cols])
                    src = work.at[:, :, y, 1 - x, :, cols] if odd else work.at[:, :, 1 - y, x, :, cols]
                    dst, target = r1.at[:, :, :, cols], second
                elif s == 2:
                    for pp in range(2):
                        for ll in range(2):
                            add((pp, ll, y, x), cols, r1[pp, ll, :, cols])
                    src, dst, target = work.at[1 - pair, :, y, x, :, cols], r2.at[:, :, cols], place.pmate
                elif s == 3:
                    for ll in range(2):
                        add((pair, ll, y, x), cols, r2[ll, :, cols])
                    src, dst, target = work.at[pair, 1 - level, y, x, :, cols], last.at[1, :, cols], place.mate
                else:
                    deliver(start, size, work[pair, level, y, x, :, cols].astype(jnp.float32) + last[1, :, cols].astype(jnp.float32))
                    continue
            started[group, odd, s] = [remote(src, dst, sends.at[group, odd, s], recvs.at[group, odd, s], target)]

    def weight_grad(name, source, grad):
        group, column, count, _ = groups[name]
        for part in range(2):
            product = dot(source[part], grad, TN).astype(LOW)
            work[part, :, :, :, :, pl.ds(column * width, count * width)] = product.reshape(2, 2, 2, -1, count * width)
        stage(name, 0)

    def channels(ref, part):
        return ref[part].reshape(-1, ref.shape[-1])

    def column_sum(values):
        return jnp.sum(values.reshape(-1, values.shape[-1]), axis=0, keepdims=True)

    def three(part):
        return taps[:, pl.ds(part * 3 * width, 3 * width)]

    average = group_average(width)
    own_parameters(gains, shifts, biases, par_own)
    small_here[...] = jnp.zeros_like(small_here)
    small_there[...] = jnp.zeros_like(small_there)
    place.meet()
    attended_load.wait()
    attended_copy = to(0, place.cmate, aall.at[core], aall.at[core])
    pgrad_load.wait()
    qkv_load.wait()
    mate_out[0] = dot(pgrad[...], channels(qbuf, 1 - core), NT).astype(LOW)
    normed_copy = to(1, place.cmate, mate_out.at[0], mate_in.at[0])
    own_half[...] = dot(pgrad[...], channels(qbuf, core), NT)
    mask = slot_mask(counts, slots, width)
    branch[...] = (mask[:, None] * cot[...].reshape(shape)).reshape(-1, width).astype(LOW)
    for load_now in normed_loads:
        load_now.wait()
    normed_copy.wait_recv()
    normed_grad = (own_half[...] + mate_in[0].astype(jnp.float32)).reshape(shape)
    normal = normal2[...].reshape(shape)
    residual_grad = normalize_back(normed_grad * par_own[2:3], normal, scale2[...], average) + mask[:, None] * cot[...].reshape(shape)
    residual_grad = residual_grad.reshape(-1, width)
    low_own[...] = residual_grad.astype(LOW)
    low_copy = Swap(place, low_own, low_in, end_sem.at[0])
    rgrad[...] = residual_grad
    small_here[2:3] = column_sum(normed_grad * normal)
    small_here[5:6] = column_sum(normed_grad)
    weight_grad("qkv", nall, pgrad[...])
    attended_copy.wait_recv()
    weight_grad("proj", aall, branch[...])
    small_here[7:8] = column_sum(low_own[...].astype(jnp.float32))
    small_here[8:9] = column_sum(pgrad[:, :width].astype(jnp.float32))
    small_here[9:10] = column_sum(pgrad[:, 2 * width :].astype(jnp.float32))
    small_here[10:11] = column_sum(branch[...].astype(jnp.float32))
    low_copy.wait_recv()
    spread_taps(low_in[...].astype(jnp.float32), taps)
    for load_now in conv1_loads:
        load_now.wait()
    mate_out[1] = dot(taps[...], channels(wbuf, 1 - level), NT).astype(LOW)
    hidden1_copy = to(2, place.mate, mate_out.at[1], mate_in.at[1])
    weight_grad("conv1a", hall1, three(0))
    stage("qkv", 1)
    weight_grad("conv1b", hall1, three(1))
    stage("conv1a", 1)
    stage("proj", 1)
    weight_grad("conv1c", hall1, three(2))
    stage("conv1b", 1)
    own_half[...] = dot(taps[...], channels(wbuf, level), NT)
    conv0_loads.append(load_weights(CONV0, 9, wbuf))
    stage("conv1c", 1)
    stage("qkv", 2)
    stage("conv1a", 2)
    for load_now in middle_loads:
        load_now.wait()
    hidden1_copy.wait_recv()
    hidden1_grad = (own_half[...] + mate_in[1].astype(jnp.float32)).reshape(shape)
    normal = normal1[...].reshape(shape)
    changes = modulation[...]
    change = 1.0 + changes[:slots, None, :width]
    inner = normal * par[1:2] + par[4:5]
    grad = hidden1_grad * silu_slope(inner * change + changes[:slots, None, width:])
    modulation_grad = jnp.concatenate([jnp.sum(grad * inner, axis=1), jnp.sum(grad, axis=1)], axis=1)
    grad = grad * change
    small_there[1:2] = column_sum(grad * normal)
    small_there[4:5] = column_sum(grad)
    conv0_low = normalize_back(grad * par[1:2], normal, scale1[...], average).astype(LOW).astype(jnp.float32)
    conv0_low = conv0_low.reshape(-1, width)
    small_there[6:7] = column_sum(conv0_low)
    spread_taps(conv0_low, taps)
    end_loads.append(load(residual_in, own_half))
    modulation_low = jnp.concatenate(
        [modulation_grad, jnp.zeros((modulation.shape[0] - slots, 2 * width), jnp.float32)], axis=0
    ).astype(LOW)
    modulation_sum = column_sum(modulation_low.astype(jnp.float32))
    small_there[11:12] = modulation_sum[:, :width]
    small_there[12:13] = modulation_sum[:, width:]
    for load_now in conv0_loads:
        load_now.wait()
    for copy in (normed_copy, hidden1_copy):
        copy.wait_send()
    pair_copies[:] = [copy for copy in pair_copies if copy is not normed_copy and copy is not hidden1_copy]
    back = Return(place, mate_out, ret_in, ret_sem)
    mate_out[1 - core] = dot(taps[...], channels(wbuf, 1 - core), NT).astype(LOW)
    back.start_other()
    weight_grad("conv0a", hall0, three(0))
    stage("conv1b", 2)
    mate_out[core] = dot(taps[...], channels(wbuf, core), NT).astype(LOW)
    back.start_own()
    small_swap = Swap(place, small_there, small_in.at[4], end_sem.at[1])
    weight_grad("conv0b", hall0, three(1))
    stage("conv0a", 1)
    stage("proj", 2)
    weight_grad("conv0c", hall0, three(2))
    stage("conv1c", 2)
    stage("conv0b", 1)
    weight_grad("aff", emb_all, modulation_low)
    emb_out[...] = dot(modulation_low, channels(abuf, 1 - level), NT).astype(LOW)
    emb_copy = to(3, place.mate, emb_out, emb_in)
    emb_own = dot(modulation_low, channels(abuf, level), NT)
    stage("qkv", 3)
    stage("conv1a", 3)
    stage("conv0c", 1)
    stage("conv0a", 2)
    stage("aff", 1)
    stage("conv1b", 3)
    stage("proj", 3)
    for load_now in end_loads:
        load_now.wait()
    joined = dot(both(aall), pbuf[...].reshape(-1, width)) + par_own[10:11]
    block = mask[:, None] * (own_half[...] + joined).reshape(shape)
    block_out[...] = block.reshape(-1, width).astype(LOW)
    stage("conv0b", 2)
    stage("conv1c", 3)
    emb_copy.wait_recv()
    emb_sum[...] = (emb_own + emb_in[...].astype(jnp.float32)).astype(LOW)
    emb_end_copy = Swap(place, emb_sum, emb_end, end_sem.at[2])
    stage("conv0c", 2)
    stage("aff", 2)
    normal, scale = normalize(img[...].astype(jnp.float32).reshape(shape), average)
    slope = silu_slope(normal * par_own[0:1] + par_own[3:4])
    stage("conv0a", 3)
    back.wait_recv()
    grad = (ret_in[0].astype(jnp.float32) + ret_in[1].astype(jnp.float32)).reshape(shape) * slope
    small_here[0:1] = column_sum(grad * normal)
    small_here[3:4] = column_sum(grad)
    small_swap.wait_recv()
    small[0] = small_here[...] + small_in[4]
    small_copies = []

    def small_step(at, target):
        small_copies.append(remote(small.at[at], small_in.at[at], small_send.at[at], small_recv.at[at], target))

    def small_add(at):
        small_copies[at].wait_recv()
        small[at + 1] = small[at] + small_in[at]

    small_step(0, place.mate)
    images_part = normalize_back(grad * par_own[0:1], normal, scale, average)
    img_grad[...] = (images_part.reshape(-1, width) + rgrad[...]).astype(LOW)
    small_add(0)
    small_step(1, place.pmate)
    stage("qkv", 4)
    stage("conv1a", 4)
    stage("conv0b", 3)
    small_add(1)
    small_step(2, place.xmate)
    stage("conv1b", 4)
    stage("proj", 4)
    stage("conv0c", 3)
    small_add(2)
    small_step(3, place.ymate)
    stage("aff", 3)
    stage("conv1c", 4)
    stage("conv0a", 4)
    emb_end_copy.wait_recv()
    emb_grad[...] = emb_end[...][:slots]
    stage("conv0b", 4)
    small_add(3)
    gains_grad[...] = small[4, 0:3]
    shifts_grad[...] = small[4, 3:6]
    biases_grad[...] = small[4, 6:13]
    stage("conv0c", 4)
    stage("aff", 4)
    for copies in list(started.values()) + [pair_copies, small_copies, [low_copy, back, small_swap, emb_end_copy]]:
        for copy in copies:
            copy.wait_send()


def finish_kernel(*refs):
    count = len(refs) // 3
    given, returned, held, sems = refs[:count], refs[count : 2 * count], refs[2 * count : 3 * count], refs[-1]
    into = [pltpu.make_async_copy(given[at], held[at], sems.at[0, at]) for at in range(count)]
    out = [pltpu.make_async_copy(held[at], returned[at], sems.at[1, at]) for at in range(count)]
    for copy in into:
        copy.start()
    for at in range(count):
        into[at].wait()
        out[at].start()
    for copy in out:
        copy.wait()


def fast_body(
    images, embedding, counts, norm_gains, norm_shifts, lin_biases, conv_weights, aff_weights, qkv_weights, proj_weights, cotangent
):
    slots, _, width = images.shape
    rows = slots * PIXELS
    depth = conv_weights.shape[2]
    padded = -(-slots // 16) * 16
    low, f32 = LOW, jnp.float32
    vmem, anyw = pl.BlockSpec(memory_space=pltpu.VMEM), pl.BlockSpec(memory_space=pl.ANY)
    smem = pl.BlockSpec(memory_space=pltpu.SMEM)
    dma, buf, shape = pltpu.SemaphoreType.DMA, pltpu.VMEM, jax.ShapeDtypeStruct

    def whole(columns):
        return GRID + (depth, columns * width)

    pair = (2, rows, width)
    one = (rows, width)
    par = (16, width)
    few = (padded, width)
    middle = [
        (pair, low), (pair, low), (one, f32), ((slots, width), f32), ((padded, 2 * width), f32), ((2,) + few, low), (par, f32),
        (pair, low), (one, low), (one, f32), (one, f32), ((slots, width), f32), ((rows, 3 * width), low),
    ]
    img, cot = images.reshape(one), cotangent.reshape(one)
    kept = pl.pallas_call(
        forward_kernel,
        name="gather_forward",
        out_shape=[shape(whole(24), low)] + [shape(*each) for each in middle],
        in_specs=[smem] + [vmem] * 7 + [anyw] * 3,
        out_specs=[anyw] * 14,
        scratch_shapes=[buf(whole(24), low)] + [buf(*each) for each in middle] + [
            buf((3, rows, width), f32), buf((rows, 3 * width), f32), buf((rows, 3 * width), low), buf(one, f32),
            buf(one, low), buf(one, low), buf(one, low), buf(few, low), buf(par, f32),
            buf(one, low), buf(one, low), buf(one, low), buf((depth, 2 * width), low),
            dma((9, 3, 3)), dma((9, 3)), dma((9, 3)), dma((9, 2, 3)), dma((9, 2, 3)), dma((2, 3)), dma((2, 6)), dma((3,)), dma((3,)), dma((22,)),
        ],
        compiler_params=pltpu.CompilerParams(collective_id=0, has_side_effects=True, vmem_limit_bytes=60 * 2**20),
    )(counts, img, embedding, norm_gains, norm_shifts, lin_biases, cot, aff_weights, jnp.transpose(qkv_weights, (1, 0, 2)), conv_weights, proj_weights)
    outs = [
        shape(one, low), shape(one, low), shape(embedding.shape, low), shape(norm_gains.shape, f32), shape(norm_shifts.shape, f32),
        shape(lin_biases.shape, f32), shape(conv_weights.shape, f32), shape(aff_weights.shape, f32), shape((3, depth, width), f32),
        shape(proj_weights.shape, f32),
    ]
    results = pl.pallas_call(
        backward_kernel,
        name="backward_scatter",
        out_shape=outs,
        in_specs=[smem] + [vmem] * 5 + [anyw] * 14,
        out_specs=[vmem] * 10,
        scratch_shapes=[buf(*each) for at, each in enumerate(middle) if at not in (8, 9)] + [
            buf(whole(24), low), buf((2, 2, 2, depth, 24 * width), low), buf((2, 2, depth, 24 * width), low),
            buf((2, depth, 24 * width), low), buf((2, depth, 24 * width), low),
            buf(whole(9), low), buf(whole(3), low), buf(whole(2), low), buf(whole(1), low),
            buf((rows, 9 * width), low), buf(pair, low), buf(one, f32), buf(one, f32),
            buf(pair, low), buf(pair, low), buf(pair, low), buf(one, low), buf(one, low),
            buf(few, low), buf(few, low), buf(few, low), buf(few, low),
            buf(one, low), buf(par, f32), buf(par, f32), buf(par, f32), buf((5,) + par, f32), buf((5,) + par, f32),
            dma((18,)), dma((9, 2, 4)), dma((9, 2, 4)), dma((9, 2, 3)), dma((4,)), dma((4,)), dma((4,)), dma((4,)), dma((3, 3)), dma((5,)),
        ],
        compiler_params=pltpu.CompilerParams(collective_id=1, has_side_effects=True, vmem_limit_bytes=63 * 2**20),
    )(counts, img, norm_gains, norm_shifts, lin_biases, cot, *kept)
    ends = pl.pallas_call(
        finish_kernel,
        name="finish",
        out_shape=outs,
        in_specs=[anyw] * 10,
        out_specs=[anyw] * 10,
        scratch_shapes=[buf(each.shape, each.dtype) for each in outs] + [dma((2, 10))],
    )(*results)
    return (
        ends[0].reshape(images.shape), ends[1].reshape(images.shape), *ends[2:8], jnp.transpose(ends[8], (1, 0, 2)), ends[9]
    )


def solution(mesh):
    return jax.shard_map(
        fast_body if mesh.shape["dp"] == 16 else body,
        mesh=mesh,
        in_specs=(
            P("dp", None, "tensor"),
            P("dp", "tensor"),
            P("dp"),
            P(None, "tensor"),
            P(None, "tensor"),
            P(None, "tensor"),
            P(None, None, "dp", "tensor"),
            P("dp", None, "tensor"),
            P("dp", None, "tensor"),
            P("dp", "tensor"),
            P("dp", None, "tensor"),
        ),
        out_specs=(
            P("dp", None, "tensor"),
            P("dp", None, "tensor"),
            P("dp", "tensor"),
            P(None, "tensor"),
            P(None, "tensor"),
            P(None, "tensor"),
            P(None, None, "dp", "tensor"),
            P("dp", None, "tensor"),
            P("dp", None, "tensor"),
            P("dp", "tensor"),
        ),
        check_vma=False,
    )
```

```python
import math
import types

import jax
import jax.numpy as jnp
from jax import lax
from jax.experimental import pallas as pl
from jax.experimental.pallas import tpu as pltpu
from jax.sharding import PartitionSpec as P

C = 768
HEAD_DIM = 64
GROUPS = 32
SIDE = 8
PIXELS = 64
GROUP_SIZE = C // GROUPS
LOW = jnp.bfloat16
MESH = pl.DeviceIdType.MESH
NT = (((1,), (1,)), ((), ()))
TN = (((0,), (0,)), ((), ()))
GRID = (2, 2, 2, 2)


def group_norm(values, gain_vec, shift_vec):
    batch_size = values.shape[0]
    grouped = values.reshape(batch_size, PIXELS, -1, C // GROUPS)
    centre = jnp.mean(grouped, axis=(1, 3), keepdims=True)
    spread = jnp.mean(jnp.square(grouped - centre), axis=(1, 3), keepdims=True)
    normal = ((grouped - centre) * lax.rsqrt(spread + 1e-05)).reshape(values.shape)
    return normal * gain_vec + shift_vec


def first_norm(values, gain_vec, shift_vec):
    return jax.nn.silu(group_norm(values, gain_vec, shift_vec))


def middle(conv_values, modulation, gain_vec, shift_vec):
    scaled = (
        group_norm(conv_values, gain_vec, shift_vec) * (1.0 + modulation[:, 0:1])
        + modulation[:, 1:2]
    )
    return jax.nn.silu(scaled)


def windows(source):
    slot_count = source.shape[0]
    padded = jnp.pad(source.reshape(slot_count, SIDE, SIDE, -1), ((0, 0), (1, 1), (1, 1), (0, 0)))
    found = []
    for tap_index in range(9):
        row_shift = tap_index // 3
        col_shift = tap_index % 3
        found.append(
            padded[:, row_shift : row_shift + SIDE, col_shift : col_shift + SIDE].reshape(
                slot_count * PIXELS, -1
            )
        )
    return found


def convolve(source, kernel):
    slot_count = source.shape[0]
    summed = jnp.zeros((slot_count * PIXELS, kernel.shape[2]), jnp.float32)
    for tap_index, window in enumerate(windows(source)):
        summed = summed + jnp.dot(window, kernel[tap_index], preferred_element_type=jnp.float32)
    return summed.reshape(slot_count, PIXELS, -1)


def convolve_back(grad_low, kernel):
    slot_count = grad_low.shape[0]
    flattened = grad_low.reshape(slot_count * PIXELS, -1)
    summed = jnp.zeros((slot_count, SIDE + 2, SIDE + 2, kernel.shape[1]), jnp.float32)
    for tap_index in range(9):
        row_shift = tap_index // 3
        col_shift = tap_index % 3
        contrib = jnp.einsum(
            "rd,cd->rc", flattened, kernel[tap_index], preferred_element_type=jnp.float32
        )
        contrib = contrib.reshape(slot_count, SIDE, SIDE, -1)
        summed = summed + jnp.pad(
            contrib, ((0, 0), (row_shift, 2 - row_shift), (col_shift, 2 - col_shift), (0, 0))
        )
    return summed[:, 1 : SIDE + 1, 1 : SIDE + 1].reshape(slot_count, PIXELS, -1)


def conv_weight_grad(source, grad_low):
    slot_count = source.shape[0]
    flattened = grad_low.reshape(slot_count * PIXELS, -1)
    found = [
        jnp.einsum("rc,rd->cd", window, flattened, preferred_element_type=jnp.float32)
        for window in windows(source)
    ]
    return jnp.stack(found)


def gather_features(values_low):
    return lax.all_gather(values_low, "tensor", axis=2, tiled=True)


def back_features(partial_sum):
    return lax.psum_scatter(
        partial_sum.astype(jnp.bfloat16), "tensor", scatter_dimension=2, tiled=True
    ).astype(jnp.float32)


def body(
    images,
    embedding,
    counts,
    norm_gains,
    norm_shifts,
    lin_biases,
    conv_weights,
    aff_weights,
    qkv_weights,
    proj_weights,
    cotangent,
):
    slot_count = images.shape[0]
    score_scale = HEAD_DIM ** (-0.5)
    slot_mask = (jnp.arange(slot_count, dtype=jnp.int32) < counts[0]).astype(jnp.float32)
    conv_full = lax.all_gather(conv_weights, "dp", axis=2, tiled=True)
    aff_full, qkv_full, proj_full = (
        lax.all_gather(aff_weights, "dp", axis=0, tiled=True),
        lax.all_gather(qkv_weights, "dp", axis=0, tiled=True),
        lax.all_gather(proj_weights, "dp", axis=0, tiled=True),
    )
    images_f = images.astype(jnp.float32)
    hidden0 = first_norm(images_f, norm_gains[0], norm_shifts[0]).astype(jnp.bfloat16)
    hidden0_all, embed_all = (
        lax.all_gather(hidden0, "tensor", axis=2, tiled=True),
        lax.all_gather(embedding, "tensor", axis=1, tiled=True),
    )
    conv_out0 = convolve(hidden0_all, conv_full[0]) + lin_biases[0]
    modulation = (
        jnp.einsum("sc,cjd->sjd", embed_all, aff_full, preferred_element_type=jnp.float32)
        + lin_biases[5:7]
    )
    hidden1 = middle(conv_out0, modulation, norm_gains[1], norm_shifts[1]).astype(jnp.bfloat16)
    hidden1_all = gather_features(hidden1)
    residual = images_f + (convolve(hidden1_all, conv_full[1]) + lin_biases[1])
    normed = group_norm(residual, norm_gains[2], norm_shifts[2]).astype(jnp.bfloat16)
    normed_all = gather_features(normed)
    bias_rows = jnp.stack([lin_biases[2], jnp.zeros_like(lin_biases[2]), lin_biases[3]])
    projected = (
        jnp.einsum("spc,cjd->spjd", normed_all, qkv_full, preferred_element_type=jnp.float32)
        + bias_rows
    ).astype(jnp.bfloat16)
    head_shape = (slot_count, PIXELS, -1, HEAD_DIM)
    query_heads = projected[:, :, 0].reshape(head_shape)
    key_heads = projected[:, :, 1].reshape(head_shape)
    value_heads = projected[:, :, 2].reshape(head_shape)
    scores = (
        jnp.einsum("sqhd,skhd->shqk", query_heads, key_heads, preferred_element_type=jnp.float32)
        * score_scale
    )
    log_total = jax.scipy.special.logsumexp(scores, axis=-1, keepdims=True)
    probabilities = jnp.exp(scores - log_total)
    weights_low = probabilities.astype(jnp.bfloat16)
    attended = jnp.einsum(
        "shqk,skhd->sqhd", weights_low, value_heads, preferred_element_type=jnp.float32
    )
    attended = attended.reshape(slot_count, PIXELS, -1).astype(jnp.bfloat16)
    attended_all = gather_features(attended)
    branch = (
        jnp.einsum("spc,cd->spd", attended_all, proj_full, preferred_element_type=jnp.float32)
        + lin_biases[4]
    )
    block_output = (slot_mask[:, None, None] * (residual + branch)).astype(jnp.bfloat16)
    conv_back = lax.all_gather(conv_weights, "dp", axis=2, tiled=True)
    aff_back, qkv_back, proj_back = (
        lax.all_gather(aff_weights, "dp", axis=0, tiled=True),
        lax.all_gather(qkv_weights, "dp", axis=0, tiled=True),
        lax.all_gather(proj_weights, "dp", axis=0, tiled=True),
    )
    grad_branch = slot_mask[:, None, None] * cotangent
    branch_low = grad_branch.astype(jnp.bfloat16)
    proj_grad = jnp.einsum(
        "spc,spd->cd", attended_all, branch_low, preferred_element_type=jnp.float32
    )
    proj_bias_grad = jnp.sum(branch_low.astype(jnp.float32), axis=(0, 1))
    attended_grad = back_features(
        jnp.einsum("spd,cd->spc", branch_low, proj_back, preferred_element_type=jnp.float32)
    )
    attended_low = attended_grad.astype(jnp.bfloat16).reshape(head_shape)
    grad_probs = jnp.einsum(
        "sqhd,skhd->shqk", attended_low, value_heads, preferred_element_type=jnp.float32
    )
    value_grad = jnp.einsum(
        "shqk,sqhd->skhd", weights_low, attended_low, preferred_element_type=jnp.float32
    )
    score_grad = probabilities * (
        grad_probs - jnp.sum(grad_probs * probabilities, axis=-1, keepdims=True)
    )
    score_low = score_grad.astype(jnp.bfloat16)
    query_grad = (
        jnp.einsum("shqk,skhd->sqhd", score_low, key_heads, preferred_element_type=jnp.float32)
        * score_scale
    )
    key_grad = (
        jnp.einsum("shqk,sqhd->skhd", score_low, query_heads, preferred_element_type=jnp.float32)
        * score_scale
    )
    flat_shape = (slot_count, PIXELS, -1)
    projected_grad = jnp.stack(
        [
            query_grad.reshape(flat_shape),
            key_grad.reshape(flat_shape),
            value_grad.reshape(flat_shape),
        ],
        axis=2,
    ).astype(jnp.bfloat16)
    qkv_grad = jnp.einsum(
        "spc,spjd->cjd", normed_all, projected_grad, preferred_element_type=jnp.float32
    )
    qkv_bias_grad = jnp.sum(projected_grad.astype(jnp.float32), axis=(0, 1))
    normed_grad = back_features(
        jnp.einsum("spjd,cjd->spc", projected_grad, qkv_back, preferred_element_type=jnp.float32)
    )
    norm_value, norm_pull = jax.vjp(group_norm, residual, norm_gains[2], norm_shifts[2])
    residual_grad, gain2_grad, shift2_grad = norm_pull(normed_grad)
    residual_grad = residual_grad + grad_branch
    conv1_low = residual_grad.astype(jnp.bfloat16)
    conv1_bias_grad = jnp.sum(conv1_low.astype(jnp.float32), axis=(0, 1))
    conv1_wgrad = conv_weight_grad(hidden1_all, conv1_low)
    hidden1_grad = back_features(convolve_back(conv1_low, conv_back[1]))
    middle_value, middle_pull = jax.vjp(
        middle, conv_out0, modulation, norm_gains[1], norm_shifts[1]
    )
    conv0_grad, modulation_grad, gain1_grad, shift1_grad = middle_pull(hidden1_grad)
    modulation_low = modulation_grad.astype(jnp.bfloat16)
    aff_bias_grad = jnp.sum(modulation_low.astype(jnp.float32), axis=0)
    aff_grad = jnp.einsum(
        "sc,sjd->cjd", embed_all, modulation_low, preferred_element_type=jnp.float32
    )
    embed_part = jnp.einsum(
        "sjd,cjd->sc", modulation_low, aff_back, preferred_element_type=jnp.float32
    )
    conv0_low = conv0_grad.astype(jnp.bfloat16)
    conv0_bias_grad = jnp.sum(conv0_low.astype(jnp.float32), axis=(0, 1))
    conv0_wgrad = conv_weight_grad(hidden0_all, conv0_low)
    hidden0_part = convolve_back(conv0_low, conv_back[0])
    hidden0_grad, embedding_sum = (
        lax.psum_scatter(
            hidden0_part.astype(jnp.bfloat16), "tensor", scatter_dimension=2, tiled=True
        ).astype(jnp.float32),
        lax.psum_scatter(
            embed_part.astype(jnp.bfloat16), "tensor", scatter_dimension=1, tiled=True
        ).astype(jnp.float32),
    )
    first_value, first_pull = jax.vjp(first_norm, images_f, norm_gains[0], norm_shifts[0])
    images_part, gain0_grad, shift0_grad = first_pull(hidden0_grad)
    images_grad = (images_part + residual_grad).astype(jnp.bfloat16)
    gains_local = jnp.stack([gain0_grad, gain1_grad, gain2_grad])
    shifts_local = jnp.stack([shift0_grad, shift1_grad, shift2_grad])
    biases_local = jnp.stack(
        [
            conv0_bias_grad,
            conv1_bias_grad,
            qkv_bias_grad[0],
            qkv_bias_grad[2],
            proj_bias_grad,
            aff_bias_grad[0],
            aff_bias_grad[1],
        ]
    )
    gains_grad, shifts_grad, biases_grad = lax.psum((gains_local, shifts_local, biases_local), "dp")
    conv_local = jnp.stack([conv0_wgrad, conv1_wgrad])
    conv_summed, aff_summed, qkv_summed, proj_summed = (
        lax.psum_scatter(conv_local, "dp", scatter_dimension=2, tiled=True),
        lax.psum_scatter(aff_grad, "dp", scatter_dimension=0, tiled=True),
        lax.psum_scatter(qkv_grad, "dp", scatter_dimension=0, tiled=True),
        lax.psum_scatter(proj_grad, "dp", scatter_dimension=0, tiled=True),
    )
    return (
        block_output,
        images_grad,
        embedding_sum.astype(jnp.bfloat16),
        gains_grad,
        shifts_grad,
        biases_grad,
        conv_summed,
        aff_summed,
        qkv_summed,
        proj_summed,
    )


def dot(left, right, dims=(((1,), (0,)), ((), ()))):
    return lax.dot_general(left, right, dims, preferred_element_type=jnp.float32)


def device(pair, level, y, x, core):
    return {"dp": ((2 * pair + level) * 2 + y) * 2 + x, "tensor": core}


class Place:
    def __init__(self):
        spot, core = lax.axis_index("dp"), lax.axis_index("tensor")
        self.pair, self.level = spot // 8, lax.rem(spot // 4, 2)
        self.y, self.x, self.core = lax.rem(spot // 2, 2), lax.rem(spot, 2), core
        pair, level, y, x = self.pair, self.level, self.y, self.x
        self.home = level == core
        self.away = level != core
        self.mate = device(pair, 1 - level, y, x, core)
        self.pmate = device(1 - pair, level, y, x, core)
        self.xmate = device(pair, level, y, 1 - x, core)
        self.ymate = device(pair, level, 1 - y, x, core)
        self.cmate = device(pair, level, y, x, 1 - core)
        self.swap = device(pair, core, y, x, level)
        self.far = device(1 - pair, core, y, x, level)

    def greet(self):
        barrier = pltpu.get_barrier_semaphore()
        for other in (self.mate, self.pmate, self.xmate, self.ymate, self.cmate, self.far):
            pl.semaphore_signal(barrier, inc=1, device_id=other, device_id_type=MESH)

        @pl.when(self.away)
        def _():
            pl.semaphore_signal(barrier, inc=1, device_id=self.swap, device_id_type=MESH)

    def meet(self):
        barrier = pltpu.get_barrier_semaphore()

        @pl.when(self.home)
        def _():
            pl.semaphore_wait(barrier, 6)

        @pl.when(self.away)
        def _():
            pl.semaphore_wait(barrier, 7)


class Swap:
    def __init__(self, place, src, dst, sems):
        self.place = place
        self.local = pltpu.make_async_copy(src, dst, sems.at[0])
        self.remote = remote_copy(src, dst, sems.at[1], sems.at[2], place.swap)
        pl.when(place.home)(self.local.start)
        pl.when(place.away)(self.remote.start)

    def wait_recv(self):
        pl.when(self.place.home)(self.local.wait)
        pl.when(self.place.away)(self.remote.wait_recv)

    def wait_send(self):
        pl.when(self.place.away)(self.remote.wait_send)


class Share:
    def __init__(self, place, src, dst_ref, sems):
        self.place = place
        core = place.core
        dst = dst_ref.at[core]
        self.near_copy = remote_copy(src, dst, sems.at[0], sems.at[1], place.cmate)
        self.mate_copy = remote_copy(src, dst, sems.at[2], sems.at[3 + core], place.mate)
        self.swap_copy = remote_copy(src, dst, sems.at[2], sems.at[3 + core], place.swap)
        self.local = pltpu.make_async_copy(src, dst, sems.at[5])
        self.others = [remote_copy(src, dst, sems.at[2], sems.at[3 + part], place.mate) for part in range(2)]

        @pl.when(place.home)
        def _():
            self.mate_copy.start()
            self.local.start()

        @pl.when(place.away)
        def _():
            self.swap_copy.start()
            self.near_copy.start()

    def wait_recv(self):
        @pl.when(self.place.home)
        def _():
            self.local.wait()
            self.near_copy.wait_recv()

        @pl.when(self.place.away)
        def _():
            self.others[0].wait_recv()
            self.others[1].wait_recv()

    def wait_send(self):
        self.mate_copy.wait_send()
        pl.when(self.place.away)(self.near_copy.wait_send)


class Return:
    def __init__(self, place, src_ref, dst_ref, sems):
        self.place, self.src_ref, self.dst_ref, self.sems = place, src_ref, dst_ref, sems
        core = place.core
        self.near_copy = remote_copy(src_ref.at[1 - core], dst_ref.at[0], sems.at[0], sems.at[1], place.cmate)
        self.swap_copy = remote_copy(src_ref.at[1 - core], dst_ref.at[1], sems.at[0], sems.at[2], place.swap)
        self.local = pltpu.make_async_copy(src_ref.at[core], dst_ref.at[0], sems.at[3])
        self.mate_copy = remote_copy(src_ref.at[core], dst_ref.at[1], sems.at[4], sems.at[2], place.mate)

    def start_other(self):
        pl.when(self.place.home)(self.near_copy.start)
        pl.when(self.place.away)(self.swap_copy.start)

    def start_own(self):
        pl.when(self.place.home)(self.local.start)
        pl.when(self.place.away)(self.mate_copy.start)

    def wait_recv(self):
        pl.when(self.place.home)(self.local.wait)
        pl.when(self.place.away)(self.near_copy.wait_recv)
        self.swap_copy.wait_recv()

    def wait_send(self):
        self.near_copy.wait_send()
        pl.when(self.place.away)(self.mate_copy.wait_send)


def halves(start, size):
    first = (size // 128 + 1) // 2 * 128
    return [(start, first, 0), (start + first, size - first, 1)]


def remote_copy(src, dst, send, recv, target):
    return pltpu.make_async_remote_copy(
        src_ref=src, dst_ref=dst, send_sem=send, recv_sem=recv, device_id=target, device_id_type=MESH
    )


def remote(src, dst, send, recv, target):
    copy = remote_copy(src, dst, send, recv, target)
    copy.start()
    return copy


def group_average(width):
    row = lax.broadcasted_iota(jnp.int32, (width, width), 0) // GROUP_SIZE
    col = lax.broadcasted_iota(jnp.int32, (width, width), 1) // GROUP_SIZE
    return jnp.where(row == col, 1.0 / (GROUP_SIZE * PIXELS), 0.0).astype(jnp.float32)


def group_mean(values, average):
    return lax.dot_general(
        jnp.sum(values, axis=1), average, (((1,), (0,)), ((), ())),
        precision=lax.Precision.HIGHEST, preferred_element_type=jnp.float32,
    )


def normalize(values, average):
    away = values - group_mean(values, average)[:, None]
    scale = lax.rsqrt(group_mean(away * away, average) + 1e-05)
    return away * scale[:, None], scale


def normalize_back(grad, normal, scale, average):
    return scale[:, None] * (
        grad - group_mean(grad, average)[:, None] - normal * group_mean(grad * normal, average)[:, None]
    )


def sigmoid(values):
    return 1.0 / (1.0 + jnp.exp(-values))


def silu_slope(values):
    gate = sigmoid(values)
    return gate * (1.0 + values * (1.0 - gate))


def shift_columns(values, step):
    moved = pltpu.roll(values, step % SIDE, 1)
    column = lax.broadcasted_iota(jnp.int32, values.shape, 1)
    return jnp.where(column == (0 if step == 1 else SIDE - 1), 0.0, moved)


def shift_rows(values, step):
    if step == 0:
        return values
    zero = jnp.zeros_like(values[:, :1])
    if step == 1:
        return jnp.concatenate([zero, values[:, : SIDE - 1]], axis=1)
    return jnp.concatenate([values[:, 1:], zero], axis=1)


def both(ref):
    return jnp.concatenate([ref[0], ref[1]], axis=1)


def convolve_row(source, weights, row_tap, sums, first=False):
    rows, width = sums.shape[1:]
    products = dot(source, weights)
    for col_tap in range(3):
        part = products[:, col_tap * width : (col_tap + 1) * width]
        part = shift_rows(part.reshape(-1, SIDE, SIDE, width), 1 - row_tap).reshape(rows, width)
        sums[col_tap] = part if first else sums[col_tap] + part


def convolve_end(sums, start, rows):
    width = sums.shape[2]
    grids = [sums[col_tap, start : start + rows].reshape(rows // SIDE, SIDE, width) for col_tap in range(3)]
    return (shift_columns(grids[0], 1) + grids[1] + shift_columns(grids[2], -1)).reshape(rows, width)


def spread_taps(grad, taps_ref, start=0):
    rows, width = grad.shape
    flat = grad.reshape(rows // SIDE, SIDE, width)
    for col_tap, grid in enumerate((shift_columns(flat, -1), flat, shift_columns(flat, 1))):
        for row_tap in range(3):
            moved = shift_rows(grid.reshape(-1, SIDE, SIDE, width), row_tap - 1)
            tap = row_tap * 3 + col_tap
            taps_ref[start : start + rows, tap * width : (tap + 1) * width] = moved.reshape(rows, width).astype(LOW)


def expand_heads(block, lane_head):
    heads = block.shape[1] // HEAD_DIM
    return jnp.concatenate([jnp.where(lane_head == h, block, jnp.zeros_like(block)) for h in range(heads)], axis=0)


def contract_heads(wide, lane_head):
    total = wide[:PIXELS]
    for h in range(1, wide.shape[1] // HEAD_DIM):
        total = jnp.where(lane_head == h, wide[h * PIXELS : (h + 1) * PIXELS], total)
    return total


def attention(first_slot, end_slot, projected, attended_grad, attended, projected_grad):
    width = attended.shape[1]
    scale = HEAD_DIM ** (-0.5)
    most = 4 * HEAD_DIM
    cells, heads, query, key, value, grad = [], [], [], [], [], []
    for slot in range(first_slot, end_slot):
        rows = slice(slot * PIXELS, (slot + 1) * PIXELS)
        for start in range(0, width, most):
            end = min(start + most, width)
            cells.append((rows, start, end))
            heads.append(lax.broadcasted_iota(jnp.int32, (PIXELS, end - start), 1) // HEAD_DIM)
            query.append(projected[rows, start:end])
            key.append(projected[rows, width + start : width + end])
            value.append(projected[rows, 2 * width + start : 2 * width + end])
            grad.append(attended_grad[rows, start:end])
    query_wide = [expand_heads(*each) for each in zip(query, heads)]
    scores = [dot(left, right, NT) * scale for left, right in zip(query_wide, key)]
    grad_wide = [expand_heads(*each) for each in zip(grad, heads)]
    grad_probs = [dot(left, right, NT) for left, right in zip(grad_wide, value)]
    powers = [jnp.exp(each - jnp.max(each, axis=1, keepdims=True)) for each in scores]
    probabilities = [each / jnp.sum(each, axis=1, keepdims=True) for each in powers]
    weights_low = [each.astype(LOW) for each in probabilities]
    attended_wide = [dot(left, right) for left, right in zip(weights_low, value)]
    value_grad = [dot(left, right, TN) for left, right in zip(weights_low, grad_wide)]
    score_low = [
        (prob * (each - jnp.sum(each * prob, axis=1, keepdims=True))).astype(LOW) for prob, each in zip(probabilities, grad_probs)
    ]
    query_grad = [dot(left, right) for left, right in zip(score_low, key)]
    key_grad = [dot(left, right, TN) * scale for left, right in zip(score_low, query_wide)]
    for at, (rows, start, end) in enumerate(cells):
        attended[rows, start:end] = contract_heads(attended_wide[at], heads[at]).astype(LOW)
        projected_grad[rows, start:end] = (contract_heads(query_grad[at], heads[at]) * scale).astype(LOW)
        projected_grad[rows, width + start : width + end] = key_grad[at].astype(LOW)
        projected_grad[rows, 2 * width + start : 2 * width + end] = value_grad[at].astype(LOW)


CONV0, AFF, CONV1, PROJ, QKV = 0, 9, 11, 20, 21


C0A, C0B, C0C, C1A, C1B, C1C, SCALE_SHIFT, OUTPUT, HEADS = range(9)

def own_parameters(gains, shifts, biases, par):
    par[...] = jnp.zeros_like(par)
    par[0:3] = gains[...]
    par[3:6] = shifts[...]
    par[6:13] = biases[...]


def slot_mask(counts, slots, width):
    return (lax.broadcasted_iota(jnp.int32, (slots, width), 0) < counts[0]).astype(jnp.float32)


def forward_kernel(
    counts, img, emb, gains, shifts, biases, cot, aff, qkv, conv, proj,
    full_out, hall0_out, hall1_out, normal1_out, scale1_out, modulation_out, emb_all_out, par_out,
    nall_out, attended_out, residual_out, normal2_out, scale2_out, pgrad_out,
    full, hall0, hall1, normal1, scale1, modulation, emb_all, par, nall, attended, residual, normal2, scale2, pgrad,
    sums, projected, branch_low, ag_own, ag_send, ag_recv, ag_low, emb_own, par_own, hidden_own, conv_own, conv_in, aff_own,
    first_local, first_send, first_recv, sends, recvs, swap_sem, share_sem, mate_send, mate_recv, out_sem,
):
    place = Place()
    pair, level, y, x, core = place.pair, place.level, place.y, place.x, place.core
    width = img.shape[1]
    slots = scale1.shape[0]
    shape = (slots, PIXELS, width)
    place.greet()
    groups = [
        (CONV0, 3, [(conv.at[0, tap], CONV0 + tap, 1) for tap in (0, 1, 2)], True),
        (CONV0 + 3, 3, [(conv.at[0, tap], CONV0 + tap, 1) for tap in (3, 4, 5)], True),
        (CONV0 + 6, 3, [(conv.at[0, tap], CONV0 + tap, 1) for tap in (6, 7, 8)], True),
        (CONV1, 3, [(conv.at[1, tap], CONV1 + tap, 1) for tap in (0, 1, 2)], True),
        (CONV1 + 3, 3, [(conv.at[1, tap], CONV1 + tap, 1) for tap in (3, 4, 5)], True),
        (CONV1 + 6, 3, [(conv.at[1, tap], CONV1 + tap, 1) for tap in (6, 7, 8)], True),
        (AFF, 2, [(aff_own, AFF, 2)], True),
        (PROJ, 1, [(proj, PROJ, 1)], False),
        (QKV, 3, [(qkv.at[part], QKV + part, 1) for part in range(3)], False),
    ]
    started = {}

    def stage(group, s):
        column, count, sources, wide_way = groups[group]
        if s == 0 and wide_way:
            found = []
            for at, (src, first, many) in enumerate(sources):
                dst = full.at[pair, level, y, x, :, pl.ds(first * width, many * width)]
                found.append(remote(src, dst, first_send.at[group, at], first_recv.at[group, at], place.far))
                found.append(Swap(place, src, dst, first_local.at[group, at]))
            started[group, 0] = found
            return
        if s == 0:
            started[group, 0], started[group, "local"] = [], []
            for at, (src, first, many) in enumerate(sources):
                dst = full.at[pair, level, y, x, :, pl.ds(first * width, many * width)]
                local = pltpu.make_async_copy(src, dst, first_local.at[group, at, 0])
                local.start()
                started[group, "local"].append(local)
                started[group, 0].append(remote(src, dst, first_send.at[group, at], first_recv.at[group, at], place.mate))
            return
        if s == 1:
            for copy in started[group, 0]:
                copy.wait_recv()
            for copy in started.pop((group, "local"), []):
                copy.wait()
        for start, size, odd in halves(column * width, count * width):
            cols = pl.ds(start, size)
            for copy in started.get((group, odd, s - 1), []):
                copy.wait_recv()
            first, second = (place.ymate, place.xmate) if odd else (place.xmate, place.ymate)
            if wide_way:
                if s == 1:
                    block, target = full.at[:, core, y, x, :, cols], first
                elif s == 2:
                    block, target = (full.at[:, core, :, x, :, cols] if odd else full.at[:, core, y, :, :, cols]), second
                elif s == 3:
                    block, target = full.at[:, core, :, :, :, cols], place.cmate
            else:
                if s == 1:
                    block, target = full.at[pair, :, y, x, :, cols], place.pmate
                elif s == 2:
                    block, target = full.at[:, :, y, x, :, cols], first
                elif s == 3:
                    block, target = (full.at[:, :, :, x, :, cols] if odd else full.at[:, :, y, :, :, cols]), second
            if s < 4:
                started[group, odd, s] = [remote(block, block, sends.at[group, odd, s - 1], recvs.at[group, odd, s - 1], target)]

    pair_copies = []

    def to(target, src, dst):
        at = len(pair_copies)
        pair_copies.append(remote(src, dst, mate_send.at[at], mate_recv.at[at], target))
        return pair_copies[-1]

    def weights(column, count, part=None):
        cols = pl.ds(column * width, count * width)
        block = full[:, :, :, :, :, cols] if part is None else full[part, :, :, :, :, cols]
        return block.reshape(-1, count * width)

    out_copies = []

    def keep(src, dst):
        out_copies.append(pltpu.make_async_copy(src, dst, out_sem.at[len(out_copies)]))
        out_copies[-1].start()

    average = group_average(width)
    rows = img.shape[0]
    near = (slots + 1) // 2
    parts = [(0, near), (near, slots)]
    spans = [pl.ds(first * PIXELS, (end - first) * PIXELS) for first, end in parts]
    held = types.SimpleNamespace(conv1=[None, None], normed=[None, None])

    def prepare():
        for part in range(2):
            aff_own[:, part * width : (part + 1) * width] = aff[:, part, :]
        padded = emb_own.shape[0]
        choose = lax.broadcasted_iota(jnp.int32, (padded, slots), 0) == lax.broadcasted_iota(jnp.int32, (padded, slots), 1)
        emb_own[...] = dot(choose.astype(LOW), emb[...]).astype(LOW)
        own_parameters(gains, shifts, biases, par_own)

    def start():
        held.par = Swap(place, par_own, par, swap_sem.at[0])
        held.emb = Share(place, emb_own, emb_all, share_sem.at[0])

    def hidden0_own():
        normal, _ = normalize(img[...].astype(jnp.float32).reshape(shape), average)
        scaled = normal * par_own[0:1] + par_own[3:4]
        hidden_own[...] = (scaled * sigmoid(scaled)).reshape(-1, width).astype(LOW)
        held.hidden0 = Share(place, hidden_own, hall0, share_sem.at[1])

    def branch_own():
        branch_low[...] = (slot_mask(counts, slots, width)[:, None] * cot[...].reshape(shape)).reshape(-1, width).astype(LOW)

    def hidden0_here():
        held.par.wait_recv()
        held.emb.wait_recv()
        held.hidden0.wait_recv()
        keep(par, par_out)
        keep(emb_all, emb_all_out)
        keep(hall0, hall0_out)

    def modulate():
        changes = dot(both(emb_all), weights(AFF, 2)) + jnp.concatenate([par[11:12], par[12:13]], axis=1)
        modulation[...] = changes
        keep(modulation, modulation_out)

    def middle():
        changes = modulation[...]
        conv_out0 = (convolve_end(sums, 0, rows) + par[6:7]).reshape(shape)
        normal, scale = normalize(conv_out0, average)
        scaled = (normal * par[1:2] + par[4:5]) * (1.0 + changes[:slots, None, :width]) + changes[:slots, None, width:]
        hall1[level] = (scaled * sigmoid(scaled)).reshape(-1, width).astype(LOW)
        held.hidden1 = to(place.mate, hall1.at[level], hall1.at[level])
        normal1[...] = normal.reshape(-1, width)
        scale1[...] = scale
        keep(normal1, normal1_out)
        keep(scale1, scale1_out)

    def hidden1_here():
        held.hidden1.wait_recv()
        keep(hall1, hall1_out)

    def conv1_end(part):
        conv_own[spans[part]] = convolve_end(sums, parts[part][0] * PIXELS, spans[part].size).astype(LOW)
        held.conv1[part] = Swap(place, conv_own.at[spans[part]], conv_in.at[spans[part]], swap_sem.at[1 + part])

    def attended_grad():
        ag_send[...] = dot(branch_low[...], weights(PROJ, 1, 1 - core), NT).astype(LOW)
        held.ag = to(place.cmate, ag_send, ag_recv)
        ag_own[...] = dot(branch_low[...], weights(PROJ, 1, core), NT)

    def attended_grad_sum():
        held.ag.wait_recv()
        ag_low[...] = (ag_own[...] + ag_recv[...].astype(jnp.float32)).astype(LOW)

    def residual_norm(part):
        held.conv1[part].wait_recv()
        span = spans[part]
        total = img[span].astype(jnp.float32) + (conv_in[span].astype(jnp.float32) + par_own[7:8])
        normal, scale = normalize(total.reshape(-1, PIXELS, width), average)
        nall[core, span] = (normal * par_own[2:3] + par_own[5:6]).reshape(-1, width).astype(LOW)
        held.normed[part] = to(place.cmate, nall.at[core, span], nall.at[core, span])
        residual[span] = total
        normal2[span] = normal.reshape(-1, width)
        scale2[parts[part][0] : parts[part][1]] = scale

    def project(part):
        span = spans[part]
        bias = jnp.concatenate([par_own[8:9], jnp.zeros((1, width), jnp.float32), par_own[9:10]], axis=1)
        own = dot(nall[core, span], weights(QKV, 3, core)) + bias
        held.normed[part].wait_recv()
        projected[span] = (own + dot(nall[1 - core, span], weights(QKV, 3, 1 - core))).astype(LOW)

    def attend(part):
        attention(*parts[part], projected, ag_low, attended, pgrad)

    def keep_norm():
        keep(residual, residual_out)
        keep(normal2, normal2_out)
        keep(scale2, scale2_out)

    def keep_normed():
        keep(nall, nall_out)

    def rows_here(tap):
        convolve_row(both(hall0), weights(CONV0 + 3 * tap, 3), tap, sums, tap == 0)

    def rows_own(tap):
        convolve_row(hall1[level], weights(CONV1 + 3 * tap, 3, level), tap, sums, tap == 0)

    def rows_other(tap):
        convolve_row(hall1[1 - level], weights(CONV1 + 3 * tap, 3, 1 - level), tap, sums)

    def stages(*steps):
        for group, s in steps:
            stage(group, s)
            if s == 4:
                cols = pl.ds(groups[group][0] * width, groups[group][1] * width)
                keep(full.at[:, :, :, :, :, cols], full_out.at[:, :, :, :, :, cols])

    prepare()
    place.meet()
    stages((C0A, 0))
    start()
    branch_own()
    stages((C0B, 0))
    hidden0_own()
    stages((SCALE_SHIFT, 0), (C0A, 1), (C0C, 0), (C0B, 1), (C1A, 0), (C0A, 2), (SCALE_SHIFT, 1), (C1B, 0))
    stages((C0B, 2), (C0C, 1), (C1C, 0), (C0A, 3), (SCALE_SHIFT, 2), (C1A, 1), (OUTPUT, 0), (C0B, 3))
    stages((C0C, 2), (C1B, 1), (HEADS, 0), (C0A, 4), (SCALE_SHIFT, 3), (C1A, 2), (C1C, 1))
    hidden0_here()
    rows_here(0)
    stages((C0B, 4), (C0C, 3), (C1B, 2), (OUTPUT, 1))
    rows_here(1)
    stages((SCALE_SHIFT, 4), (C1A, 3), (C1C, 2), (HEADS, 1))
    modulate()
    stages((C0C, 4), (C1B, 3), (OUTPUT, 2))
    rows_here(2)
    middle()
    stages((C1A, 4), (C1C, 3), (HEADS, 2))
    rows_own(0)
    stages((C1B, 4), (OUTPUT, 3))
    rows_own(1)
    stages((C1C, 4), (HEADS, 3))
    rows_own(2)
    hidden1_here()
    rows_other(0)
    rows_other(1)
    rows_other(2)
    conv1_end(0)
    conv1_end(1)
    stages((OUTPUT, 4))
    attended_grad()
    stages((HEADS, 4))
    residual_norm(0)
    residual_norm(1)
    attended_grad_sum()
    keep_norm()
    project(0)
    attend(0)
    project(1)
    keep_normed()
    attend(1)
    keep(pgrad, pgrad_out)
    keep(attended, attended_out)
    for copies in list(started.values()) + [pair_copies, [held.par, held.emb, held.hidden0, *held.conv1]]:
        for copy in copies:
            copy.wait_send()
    for copy in out_copies:
        copy.wait()


def backward_kernel(
    counts, img, gains, shifts, biases, cot,
    full, hall0_in, hall1_in, normal1_in, scale1_in, modulation_in, emb_all_in, par_in,
    nall_in, attended_in, residual_in, normal2_in, scale2_in, pgrad_in,
    block_out, img_grad, emb_grad, gains_grad, shifts_grad, biases_grad, conv_grad, aff_grad, qkv_grad, proj_grad,
    hall0, hall1, normal1, scale1, modulation, emb_all, par, nall, normal2, scale2, pgrad,
    work, r0, r1, r2, last, wbuf, qbuf, abuf, pbuf, taps, aall, rgrad, own_half, mate_out, mate_in, ret_in, low_own, low_in,
    emb_out, emb_in, emb_sum, emb_end, branch, par_own, small_here, small_there, small, small_in,
    load_sem, sends, recvs, swap_sem, small_send, small_recv, mate_send, mate_recv, end_sem, ret_sem,
):
    place = Place()
    pair, level, y, x, core = place.pair, place.level, place.y, place.x, place.core
    width = img.shape[1]
    slots = scale1.shape[0]
    shape = (slots, PIXELS, width)
    place.greet()
    loads = []

    def load(src, dst):
        loads.append(pltpu.make_async_copy(src, dst, load_sem.at[len(loads)]))
        loads[-1].start()
        return loads[-1]

    def load_weights(column, count, dst):
        return load(full.at[:, :, :, :, :, pl.ds(column * width, count * width)], dst)

    pgrad_load = load(pgrad_in, pgrad)
    qkv_load = load_weights(QKV, 3, qbuf)
    attended_load = load(attended_in, aall.at[core])
    normed_loads = [load(nall_in, nall), load(normal2_in, normal2), load(scale2_in, scale2)]
    conv1_loads = [load_weights(CONV1, 9, wbuf), load(hall1_in, hall1)]
    middle_loads = [load(normal1_in, normal1), load(scale1_in, scale1), load(modulation_in, modulation), load(par_in, par)]
    conv0_loads = [load(hall0_in, hall0), load(emb_all_in, emb_all), load_weights(AFF, 2, abuf)]
    end_loads = [load_weights(PROJ, 1, pbuf)]
    pair_copies = []

    def to(at, target, src, dst):
        pair_copies.append(remote(src, dst, mate_send.at[at], mate_recv.at[at], target))
        return pair_copies[-1]

    groups = (
        (CONV0, 3, True), (CONV0 + 3, 3, True), (CONV0 + 6, 3, True), (CONV1, 3, True), (CONV1 + 3, 3, True), (CONV1 + 6, 3, True),
        (AFF, 2, True), (PROJ, 1, False), (QKV, 3, False),
    )
    started = {}

    def deliver(start, size, value):
        column, offset = start // width, start % width
        while size:
            now = min(size, width - offset)
            part, value = value[:, :now], value[:, now:]
            if column < AFF or CONV1 <= column < PROJ:
                tap = column if column < AFF else column - CONV1 + 9
                conv_grad[tap // 9, tap % 9, :, offset : offset + now] = part
            else:
                ref, first = (aff_grad, AFF) if column < CONV1 else (proj_grad, PROJ) if column < QKV else (qkv_grad, QKV)
                if ref is proj_grad:
                    ref[:, offset : offset + now] = part
                elif ref is qkv_grad:
                    ref[column - first, :, offset : offset + now] = part
                else:
                    ref[:, column - first, offset : offset + now] = part
            column, offset, size = column + 1, 0, size - now

    def add(at, cols, received):
        total = work[at + (slice(None), cols)].astype(jnp.float32) + received.astype(jnp.float32)
        work[at + (slice(None), cols)] = total.astype(LOW)

    def stage(group, s):
        column, count, wide_way = groups[group]
        for start, size, odd in halves(column * width, count * width):
            cols = pl.ds(start, size)
            for copy in started.get((group, odd, s - 1), []):
                copy.wait_recv()
            first, second = (place.ymate, place.xmate) if odd else (place.xmate, place.ymate)
            if wide_way:
                if s == 0:
                    src, dst, target = work.at[:, 1 - core, :, :, :, cols], r0.at[:, :, :, :, cols], place.cmate
                elif s == 1:
                    for pp in range(2):
                        for yy in range(2):
                            for xx in range(2):
                                add((pp, core, yy, xx), cols, r0[pp, yy, xx, :, cols])
                    src = work.at[:, core, 1 - y, :, :, cols] if odd else work.at[:, core, :, 1 - x, :, cols]
                    dst, target = r1.at[:, :, :, cols], first
                elif s == 2:
                    for pp in range(2):
                        for other in range(2):
                            add((pp, core, y, other) if odd else (pp, core, other, x), cols, r1[pp, other, :, cols])
                    src = work.at[:, core, y, 1 - x, :, cols] if odd else work.at[:, core, 1 - y, x, :, cols]
                    dst, target = r2.at[:, :, cols], second
                elif s == 3:
                    for pp in range(2):
                        add((pp, core, y, x), cols, r2[pp, :, cols])
                    far = remote(
                        work.at[1 - pair, core, y, x, :, cols], last.at[1, :, cols], sends.at[group, odd, 3], recvs.at[group, odd, 3], place.far
                    )
                    started[group, odd, 3] = [
                        far, Swap(place, work.at[pair, core, y, x, :, cols], last.at[0, :, cols], swap_sem.at[group, odd])
                    ]
                    continue
                else:
                    deliver(start, size, last[0, :, cols].astype(jnp.float32) + last[1, :, cols].astype(jnp.float32))
                    continue
            else:
                if s == 0:
                    src = work.at[:, :, 1 - y, :, :, cols] if odd else work.at[:, :, :, 1 - x, :, cols]
                    dst, target = r0.at[:, :, :, :, cols], first
                elif s == 1:
                    for pp in range(2):
                        for ll in range(2):
                            for other in range(2):
                                add((pp, ll, y, other) if odd else (pp, ll, other, x), cols, r0[pp, ll, other, :, cols])
                    src = work.at[:, :, y, 1 - x, :, cols] if odd else work.at[:, :, 1 - y, x, :, cols]
                    dst, target = r1.at[:, :, :, cols], second
                elif s == 2:
                    for pp in range(2):
                        for ll in range(2):
                            add((pp, ll, y, x), cols, r1[pp, ll, :, cols])
                    src, dst, target = work.at[1 - pair, :, y, x, :, cols], r2.at[:, :, cols], place.pmate
                elif s == 3:
                    for ll in range(2):
                        add((pair, ll, y, x), cols, r2[ll, :, cols])
                    src, dst, target = work.at[pair, 1 - level, y, x, :, cols], last.at[1, :, cols], place.mate
                else:
                    deliver(start, size, work[pair, level, y, x, :, cols].astype(jnp.float32) + last[1, :, cols].astype(jnp.float32))
                    continue
            started[group, odd, s] = [remote(src, dst, sends.at[group, odd, s], recvs.at[group, odd, s], target)]

    def weight_grad(group, source, grad):
        column, count, _ = groups[group]
        for part in range(2):
            product = dot(source[part], grad, TN).astype(LOW)
            work[part, :, :, :, :, pl.ds(column * width, count * width)] = product.reshape(2, 2, 2, -1, count * width)
        stage(group, 0)

    def channels(ref, part):
        return ref[part].reshape(-1, ref.shape[-1])

    def column_sum(values):
        return jnp.sum(values.reshape(-1, values.shape[-1]), axis=0, keepdims=True)

    def three(part):
        return taps[:, pl.ds(part * 3 * width, 3 * width)]

    average = group_average(width)
    own_parameters(gains, shifts, biases, par_own)
    small_here[...] = jnp.zeros_like(small_here)
    small_there[...] = jnp.zeros_like(small_there)
    mask = slot_mask(counts, slots, width)
    held = types.SimpleNamespace(normed=[None, None], low=[None, None])

    near = (slots + 1) // 2
    parts = [(0, near), (near, slots)]
    spans = [pl.ds(first * PIXELS, (end - first) * PIXELS) for first, end in parts]

    def normed_other(part):
        if part == 0:
            pgrad_load.wait()
            qkv_load.wait()
        mate_out[0, spans[part]] = dot(pgrad[spans[part]], channels(qbuf, 1 - core), NT).astype(LOW)
        held.normed[part] = to(part, place.cmate, mate_out.at[0, spans[part]], mate_in.at[0, spans[part]])

    def attended_other():
        attended_load.wait()
        held.attended = to(4, place.cmate, aall.at[core], aall.at[core])

    def normed_own():
        own_half[...] = dot(pgrad[...], channels(qbuf, core), NT)
        branch[...] = (mask[:, None] * cot[...].reshape(shape)).reshape(-1, width).astype(LOW)

    def qkv_weights():
        normed_loads[0].wait()
        weight_grad(HEADS, nall, pgrad[...])

    def proj_weights():
        held.attended.wait_recv()
        weight_grad(OUTPUT, aall, branch[...])

    def residual_grads(part):
        if part == 0:
            for now in normed_loads[1:]:
                now.wait()
        held.normed[part].wait_recv()
        span, (first, end) = spans[part], parts[part]
        part_shape = (end - first, PIXELS, width)
        normed_grad = (own_half[span] + mate_in[0, span].astype(jnp.float32)).reshape(part_shape)
        normal = normal2[span].reshape(part_shape)
        residual_grad = normalize_back(normed_grad * par_own[2:3], normal, scale2[first:end], average)
        residual_grad = (residual_grad + mask[first:end, None] * cot[span].reshape(part_shape)).reshape(-1, width)
        low_own[span] = residual_grad.astype(LOW)
        held.low[part] = Swap(place, low_own.at[span], low_in.at[span], end_sem.at[3 * part])
        rgrad[span] = residual_grad
        small_here[2:3] = small_here[2:3] + column_sum(normed_grad * normal)
        small_here[5:6] = small_here[5:6] + column_sum(normed_grad)

    def first_sums():
        small_here[7:8] = column_sum(low_own[...].astype(jnp.float32))
        small_here[8:9] = column_sum(pgrad[:, :width].astype(jnp.float32))
        small_here[9:10] = column_sum(pgrad[:, 2 * width :].astype(jnp.float32))
        small_here[10:11] = column_sum(branch[...].astype(jnp.float32))

    def conv1_taps(part):
        held.low[part].wait_recv()
        spread_taps(low_in[spans[part]].astype(jnp.float32), taps, parts[part][0] * PIXELS)

    def hidden1_other():
        for now in conv1_loads:
            now.wait()
        mate_out[1] = dot(taps[...], channels(wbuf, 1 - level), NT).astype(LOW)
        held.hidden1 = to(2, place.mate, mate_out.at[1], mate_in.at[1])

    def hidden1_own():
        own_half[...] = dot(taps[...], channels(wbuf, level), NT)
        conv0_loads.append(load_weights(CONV0, 9, wbuf))

    def middle_back():
        for now in middle_loads:
            now.wait()
        held.hidden1.wait_recv()
        hidden1_grad = (own_half[...] + mate_in[1].astype(jnp.float32)).reshape(shape)
        end_loads.append(load(residual_in, own_half))
        normal = normal1[...].reshape(shape)
        changes = modulation[...]
        change = 1.0 + changes[:slots, None, :width]
        inner = normal * par[1:2] + par[4:5]
        grad = hidden1_grad * silu_slope(inner * change + changes[:slots, None, width:])
        modulation_grad = jnp.concatenate([jnp.sum(grad * inner, axis=1), jnp.sum(grad, axis=1)], axis=1)
        grad = grad * change
        conv0_low = normalize_back(grad * par[1:2], normal, scale1[...], average).astype(LOW).astype(jnp.float32)
        conv0_low = conv0_low.reshape(-1, width)
        spread_taps(conv0_low, taps)
        small_there[1:2] = column_sum(grad * normal)
        small_there[4:5] = column_sum(grad)
        small_there[6:7] = column_sum(conv0_low)
        rest = jnp.zeros((modulation.shape[0] - slots, 2 * width), jnp.float32)
        modulation_low = jnp.concatenate([modulation_grad, rest], axis=0).astype(LOW)
        modulation_sum = column_sum(modulation_low.astype(jnp.float32))
        small_there[11:12] = modulation_sum[:, :width]
        small_there[12:13] = modulation_sum[:, width:]
        held.modulation = modulation_low
        held.small = Swap(place, small_there, small_in.at[4], end_sem.at[1])

    def hidden0_other():
        for now in conv0_loads:
            now.wait()
        done = (*held.normed, held.hidden1)
        for copy in done:
            copy.wait_send()
        pair_copies[:] = [copy for copy in pair_copies if all(copy is not other for other in done)]
        held.back = Return(place, mate_out, ret_in, ret_sem)
        mate_out[1 - core] = dot(taps[...], channels(wbuf, 1 - core), NT).astype(LOW)
        held.back.start_other()

    def hidden0_own():
        mate_out[core] = dot(taps[...], channels(wbuf, core), NT).astype(LOW)
        held.back.start_own()

    def aff_part():
        weight_grad(SCALE_SHIFT, emb_all, held.modulation)
        emb_out[...] = dot(held.modulation, channels(abuf, 1 - level), NT).astype(LOW)
        held.emb = to(3, place.mate, emb_out, emb_in)
        held.emb_own = dot(held.modulation, channels(abuf, level), NT)

    def embedding_sum():
        held.emb.wait_recv()
        emb_sum[...] = (held.emb_own + emb_in[...].astype(jnp.float32)).astype(LOW)
        held.emb_end = Swap(place, emb_sum, emb_end, end_sem.at[2])

    def embedding_end():
        held.emb_end.wait_recv()
        emb_grad[...] = emb_end[...][:slots]

    def block_end():
        for now in end_loads:
            now.wait()
        joined = dot(both(aall), pbuf[...].reshape(-1, width)) + par_own[10:11]
        block = mask[:, None] * (own_half[...] + joined).reshape(shape)
        block_out[...] = block.reshape(-1, width).astype(LOW)

    small_copies = []

    def small_step(at, target):
        small_copies.append(remote(small.at[at], small_in.at[at], small_send.at[at], small_recv.at[at], target))

    def small_add(at):
        small_copies[at].wait_recv()
        small[at + 1] = small[at] + small_in[at]

    def images_end():
        normal, scale = normalize(img[...].astype(jnp.float32).reshape(shape), average)
        slope = silu_slope(normal * par_own[0:1] + par_own[3:4])
        held.back.wait_recv()
        grad = (ret_in[0].astype(jnp.float32) + ret_in[1].astype(jnp.float32)).reshape(shape) * slope
        small_here[0:1] = column_sum(grad * normal)
        small_here[3:4] = column_sum(grad)
        held.small.wait_recv()
        small[0] = small_here[...] + small_in[4]
        small_step(0, place.mate)
        images_part = normalize_back(grad * par_own[0:1], normal, scale, average)
        img_grad[...] = (images_part.reshape(-1, width) + rgrad[...]).astype(LOW)

    def small1():
        small_add(0)
        small_step(1, place.pmate)

    def small2():
        small_add(1)
        small_step(2, place.xmate)

    def small3():
        small_add(2)
        small_step(3, place.ymate)

    def small_end():
        small_add(3)
        gains_grad[...] = small[4, 0:3]
        shifts_grad[...] = small[4, 3:6]
        biases_grad[...] = small[4, 6:13]

    def conv_weight_grad(group):
        weight_grad(group, hall0 if group < C1A else hall1, three(group % 3))

    def stages(*steps):
        for group, s in steps:
            stage(group, s)

    place.meet()
    normed_other(0)
    normed_other(1)
    qkv_weights()
    attended_other()
    normed_own()
    residual_grads(0)
    residual_grads(1)
    proj_weights()
    first_sums()
    conv1_taps(0)
    conv1_taps(1)
    hidden1_other()
    conv_weight_grad(C1A)
    stages((HEADS, 1))
    conv_weight_grad(C1B)
    stages((C1A, 1), (OUTPUT, 1))
    conv_weight_grad(C1C)
    stages((C1B, 1))
    hidden1_own()
    stages((C1C, 1), (HEADS, 2), (C1A, 2))
    middle_back()
    hidden0_other()
    conv_weight_grad(C0A)
    stages((C1B, 2))
    hidden0_own()
    conv_weight_grad(C0B)
    stages((C0A, 1), (OUTPUT, 2))
    conv_weight_grad(C0C)
    stages((C1C, 2), (C0B, 1))
    aff_part()
    stages((HEADS, 3), (C1A, 3), (C0C, 1), (C0A, 2), (SCALE_SHIFT, 1), (C1B, 3), (OUTPUT, 3))
    block_end()
    stages((C0B, 2), (C1C, 3))
    embedding_sum()
    stages((C0C, 2), (SCALE_SHIFT, 2), (C0A, 3))
    images_end()
    small1()
    stages((HEADS, 4), (C1A, 4), (C0B, 3))
    small2()
    stages((C1B, 4), (OUTPUT, 4), (C0C, 3))
    small3()
    stages((SCALE_SHIFT, 3), (C1C, 4), (C0A, 4))
    embedding_end()
    stages((C0B, 4))
    small_end()
    stages((C0C, 4), (SCALE_SHIFT, 4))
    for copies in list(started.values()) + [pair_copies, small_copies, [*held.low, held.back, held.small, held.emb_end]]:
        for copy in copies:
            copy.wait_send()


def finish_kernel(*refs):
    count = len(refs) // 3
    given, returned, held, sems = refs[:count], refs[count : 2 * count], refs[2 * count : 3 * count], refs[-1]
    into = [pltpu.make_async_copy(given[at], held[at], sems.at[0, at]) for at in range(count)]
    out = [pltpu.make_async_copy(held[at], returned[at], sems.at[1, at]) for at in range(count)]
    for copy in into:
        copy.start()
    for at in range(count):
        into[at].wait()
        out[at].start()
    for copy in out:
        copy.wait()


def fast_body(
    images, embedding, counts, norm_gains, norm_shifts, lin_biases, conv_weights, aff_weights, qkv_weights, proj_weights, cotangent
):
    slots, _, width = images.shape
    rows = slots * PIXELS
    depth = conv_weights.shape[2]
    padded = -(-slots // 16) * 16
    low, f32 = LOW, jnp.float32
    vmem, anyw = pl.BlockSpec(memory_space=pltpu.VMEM), pl.BlockSpec(memory_space=pl.ANY)
    smem = pl.BlockSpec(memory_space=pltpu.SMEM)
    dma, buf, shape = pltpu.SemaphoreType.DMA, pltpu.VMEM, jax.ShapeDtypeStruct

    def whole(columns):
        return GRID + (depth, columns * width)

    pair = (2, rows, width)
    one = (rows, width)
    par = (16, width)
    few = (padded, width)
    middle = [
        (pair, low), (pair, low), (one, f32), ((slots, width), f32), ((padded, 2 * width), f32), ((2,) + few, low), (par, f32),
        (pair, low), (one, low), (one, f32), (one, f32), ((slots, width), f32), ((rows, 3 * width), low),
    ]
    img, cot = images.reshape(one), cotangent.reshape(one)
    kept = pl.pallas_call(
        forward_kernel,
        name="gather_forward",
        out_shape=[shape(whole(24), low)] + [shape(*each) for each in middle],
        in_specs=[smem] + [vmem] * 7 + [anyw] * 3,
        out_specs=[anyw] * 14,
        scratch_shapes=[buf(whole(24), low)] + [buf(*each) for each in middle] + [
            buf((3, rows, width), f32), buf((rows, 3 * width), low), buf(one, low), buf(one, f32),
            buf(one, low), buf(one, low), buf(one, low), buf(few, low), buf(par, f32),
            buf(one, low), buf(one, low), buf(one, low), buf((depth, 2 * width), low),
            dma((9, 3, 3)), dma((9, 3)), dma((9, 3)), dma((9, 2, 3)), dma((9, 2, 3)), dma((3, 3)), dma((2, 6)), dma((4,)), dma((4,)), dma((22,)),
        ],
        compiler_params=pltpu.CompilerParams(collective_id=0, has_side_effects=True, vmem_limit_bytes=60 * 2**20),
    )(counts, img, embedding, norm_gains, norm_shifts, lin_biases, cot, aff_weights, jnp.transpose(qkv_weights, (1, 0, 2)), conv_weights, proj_weights)
    outs = [
        shape(one, low), shape(one, low), shape(embedding.shape, low), shape(norm_gains.shape, f32), shape(norm_shifts.shape, f32),
        shape(lin_biases.shape, f32), shape(conv_weights.shape, f32), shape(aff_weights.shape, f32), shape((3, depth, width), f32),
        shape(proj_weights.shape, f32),
    ]
    results = pl.pallas_call(
        backward_kernel,
        name="backward_scatter",
        out_shape=outs,
        in_specs=[smem] + [vmem] * 5 + [anyw] * 14,
        out_specs=[vmem] * 10,
        scratch_shapes=[buf(*each) for at, each in enumerate(middle) if at not in (8, 9)] + [
            buf(whole(24), low), buf((2, 2, 2, depth, 24 * width), low), buf((2, 2, depth, 24 * width), low),
            buf((2, depth, 24 * width), low), buf((2, depth, 24 * width), low),
            buf(whole(9), low), buf(whole(3), low), buf(whole(2), low), buf(whole(1), low),
            buf((rows, 9 * width), low), buf(pair, low), buf(one, f32), buf(one, f32),
            buf(pair, low), buf(pair, low), buf(pair, low), buf(one, low), buf(one, low),
            buf(few, low), buf(few, low), buf(few, low), buf(few, low),
            buf(one, low), buf(par, f32), buf(par, f32), buf(par, f32), buf((5,) + par, f32), buf((5,) + par, f32),
            dma((18,)), dma((9, 2, 4)), dma((9, 2, 4)), dma((9, 2, 3)), dma((4,)), dma((4,)), dma((5,)), dma((5,)), dma((4, 3)), dma((5,)),
        ],
        compiler_params=pltpu.CompilerParams(collective_id=1, has_side_effects=True, vmem_limit_bytes=63 * 2**20),
    )(counts, img, norm_gains, norm_shifts, lin_biases, cot, *kept)
    ends = pl.pallas_call(
        finish_kernel,
        name="finish",
        out_shape=outs,
        in_specs=[anyw] * 10,
        out_specs=[anyw] * 10,
        scratch_shapes=[buf(each.shape, each.dtype) for each in outs] + [dma((2, 10))],
    )(*results)
    return (
        ends[0].reshape(images.shape), ends[1].reshape(images.shape), *ends[2:8], jnp.transpose(ends[8], (1, 0, 2)), ends[9]
    )


def solution(mesh):
    return jax.shard_map(
        fast_body if mesh.shape["dp"] == 16 else body,
        mesh=mesh,
        in_specs=(
            P("dp", None, "tensor"),
            P("dp", "tensor"),
            P("dp"),
            P(None, "tensor"),
            P(None, "tensor"),
            P(None, "tensor"),
            P(None, None, "dp", "tensor"),
            P("dp", None, "tensor"),
            P("dp", None, "tensor"),
            P("dp", "tensor"),
            P("dp", None, "tensor"),
        ),
        out_specs=(
            P("dp", None, "tensor"),
            P("dp", None, "tensor"),
            P("dp", "tensor"),
            P(None, "tensor"),
            P(None, "tensor"),
            P(None, "tensor"),
            P(None, None, "dp", "tensor"),
            P("dp", None, "tensor"),
            P("dp", None, "tensor"),
            P("dp", "tensor"),
        ),
        check_vma=False,
    )
```

```python
import math
import types

import jax
import jax.numpy as jnp
from jax import lax
from jax.experimental import pallas as pl
from jax.experimental.pallas import tpu as pltpu
from jax.sharding import PartitionSpec as P

C = 768
HEAD_DIM = 64
GROUPS = 32
SIDE = 8
PIXELS = 64
GROUP_SIZE = C // GROUPS
LOW = jnp.bfloat16
MESH = pl.DeviceIdType.MESH
NT = (((1,), (1,)), ((), ()))
TN = (((0,), (0,)), ((), ()))
GRID = (2, 2, 2, 2)


def group_norm(values, gain_vec, shift_vec):
    batch_size = values.shape[0]
    grouped = values.reshape(batch_size, PIXELS, -1, C // GROUPS)
    centre = jnp.mean(grouped, axis=(1, 3), keepdims=True)
    spread = jnp.mean(jnp.square(grouped - centre), axis=(1, 3), keepdims=True)
    normal = ((grouped - centre) * lax.rsqrt(spread + 1e-05)).reshape(values.shape)
    return normal * gain_vec + shift_vec


def first_norm(values, gain_vec, shift_vec):
    return jax.nn.silu(group_norm(values, gain_vec, shift_vec))


def middle(conv_values, modulation, gain_vec, shift_vec):
    scaled = (
        group_norm(conv_values, gain_vec, shift_vec) * (1.0 + modulation[:, 0:1])
        + modulation[:, 1:2]
    )
    return jax.nn.silu(scaled)


def windows(source):
    slot_count = source.shape[0]
    padded = jnp.pad(source.reshape(slot_count, SIDE, SIDE, -1), ((0, 0), (1, 1), (1, 1), (0, 0)))
    found = []
    for tap_index in range(9):
        row_shift = tap_index // 3
        col_shift = tap_index % 3
        found.append(
            padded[:, row_shift : row_shift + SIDE, col_shift : col_shift + SIDE].reshape(
                slot_count * PIXELS, -1
            )
        )
    return found


def convolve(source, kernel):
    slot_count = source.shape[0]
    summed = jnp.zeros((slot_count * PIXELS, kernel.shape[2]), jnp.float32)
    for tap_index, window in enumerate(windows(source)):
        summed = summed + jnp.dot(window, kernel[tap_index], preferred_element_type=jnp.float32)
    return summed.reshape(slot_count, PIXELS, -1)


def convolve_back(grad_low, kernel):
    slot_count = grad_low.shape[0]
    flattened = grad_low.reshape(slot_count * PIXELS, -1)
    summed = jnp.zeros((slot_count, SIDE + 2, SIDE + 2, kernel.shape[1]), jnp.float32)
    for tap_index in range(9):
        row_shift = tap_index // 3
        col_shift = tap_index % 3
        contrib = jnp.einsum(
            "rd,cd->rc", flattened, kernel[tap_index], preferred_element_type=jnp.float32
        )
        contrib = contrib.reshape(slot_count, SIDE, SIDE, -1)
        summed = summed + jnp.pad(
            contrib, ((0, 0), (row_shift, 2 - row_shift), (col_shift, 2 - col_shift), (0, 0))
        )
    return summed[:, 1 : SIDE + 1, 1 : SIDE + 1].reshape(slot_count, PIXELS, -1)


def conv_weight_grad(source, grad_low):
    slot_count = source.shape[0]
    flattened = grad_low.reshape(slot_count * PIXELS, -1)
    found = [
        jnp.einsum("rc,rd->cd", window, flattened, preferred_element_type=jnp.float32)
        for window in windows(source)
    ]
    return jnp.stack(found)


def gather_features(values_low):
    return lax.all_gather(values_low, "tensor", axis=2, tiled=True)


def back_features(partial_sum):
    return lax.psum_scatter(
        partial_sum.astype(jnp.bfloat16), "tensor", scatter_dimension=2, tiled=True
    ).astype(jnp.float32)


def body(
    images,
    embedding,
    counts,
    norm_gains,
    norm_shifts,
    lin_biases,
    conv_weights,
    aff_weights,
    qkv_weights,
    proj_weights,
    cotangent,
):
    slot_count = images.shape[0]
    score_scale = HEAD_DIM ** (-0.5)
    slot_mask = (jnp.arange(slot_count, dtype=jnp.int32) < counts[0]).astype(jnp.float32)
    conv_full = lax.all_gather(conv_weights, "dp", axis=2, tiled=True)
    aff_full, qkv_full, proj_full = (
        lax.all_gather(aff_weights, "dp", axis=0, tiled=True),
        lax.all_gather(qkv_weights, "dp", axis=0, tiled=True),
        lax.all_gather(proj_weights, "dp", axis=0, tiled=True),
    )
    images_f = images.astype(jnp.float32)
    hidden0 = first_norm(images_f, norm_gains[0], norm_shifts[0]).astype(jnp.bfloat16)
    hidden0_all, embed_all = (
        lax.all_gather(hidden0, "tensor", axis=2, tiled=True),
        lax.all_gather(embedding, "tensor", axis=1, tiled=True),
    )
    conv_out0 = convolve(hidden0_all, conv_full[0]) + lin_biases[0]
    modulation = (
        jnp.einsum("sc,cjd->sjd", embed_all, aff_full, preferred_element_type=jnp.float32)
        + lin_biases[5:7]
    )
    hidden1 = middle(conv_out0, modulation, norm_gains[1], norm_shifts[1]).astype(jnp.bfloat16)
    hidden1_all = gather_features(hidden1)
    residual = images_f + (convolve(hidden1_all, conv_full[1]) + lin_biases[1])
    normed = group_norm(residual, norm_gains[2], norm_shifts[2]).astype(jnp.bfloat16)
    normed_all = gather_features(normed)
    bias_rows = jnp.stack([lin_biases[2], jnp.zeros_like(lin_biases[2]), lin_biases[3]])
    projected = (
        jnp.einsum("spc,cjd->spjd", normed_all, qkv_full, preferred_element_type=jnp.float32)
        + bias_rows
    ).astype(jnp.bfloat16)
    head_shape = (slot_count, PIXELS, -1, HEAD_DIM)
    query_heads = projected[:, :, 0].reshape(head_shape)
    key_heads = projected[:, :, 1].reshape(head_shape)
    value_heads = projected[:, :, 2].reshape(head_shape)
    scores = (
        jnp.einsum("sqhd,skhd->shqk", query_heads, key_heads, preferred_element_type=jnp.float32)
        * score_scale
    )
    log_total = jax.scipy.special.logsumexp(scores, axis=-1, keepdims=True)
    probabilities = jnp.exp(scores - log_total)
    weights_low = probabilities.astype(jnp.bfloat16)
    attended = jnp.einsum(
        "shqk,skhd->sqhd", weights_low, value_heads, preferred_element_type=jnp.float32
    )
    attended = attended.reshape(slot_count, PIXELS, -1).astype(jnp.bfloat16)
    attended_all = gather_features(attended)
    branch = (
        jnp.einsum("spc,cd->spd", attended_all, proj_full, preferred_element_type=jnp.float32)
        + lin_biases[4]
    )
    block_output = (slot_mask[:, None, None] * (residual + branch)).astype(jnp.bfloat16)
    conv_back = lax.all_gather(conv_weights, "dp", axis=2, tiled=True)
    aff_back, qkv_back, proj_back = (
        lax.all_gather(aff_weights, "dp", axis=0, tiled=True),
        lax.all_gather(qkv_weights, "dp", axis=0, tiled=True),
        lax.all_gather(proj_weights, "dp", axis=0, tiled=True),
    )
    grad_branch = slot_mask[:, None, None] * cotangent
    branch_low = grad_branch.astype(jnp.bfloat16)
    proj_grad = jnp.einsum(
        "spc,spd->cd", attended_all, branch_low, preferred_element_type=jnp.float32
    )
    proj_bias_grad = jnp.sum(branch_low.astype(jnp.float32), axis=(0, 1))
    attended_grad = back_features(
        jnp.einsum("spd,cd->spc", branch_low, proj_back, preferred_element_type=jnp.float32)
    )
    attended_low = attended_grad.astype(jnp.bfloat16).reshape(head_shape)
    grad_probs = jnp.einsum(
        "sqhd,skhd->shqk", attended_low, value_heads, preferred_element_type=jnp.float32
    )
    value_grad = jnp.einsum(
        "shqk,sqhd->skhd", weights_low, attended_low, preferred_element_type=jnp.float32
    )
    score_grad = probabilities * (
        grad_probs - jnp.sum(grad_probs * probabilities, axis=-1, keepdims=True)
    )
    score_low = score_grad.astype(jnp.bfloat16)
    query_grad = (
        jnp.einsum("shqk,skhd->sqhd", score_low, key_heads, preferred_element_type=jnp.float32)
        * score_scale
    )
    key_grad = (
        jnp.einsum("shqk,sqhd->skhd", score_low, query_heads, preferred_element_type=jnp.float32)
        * score_scale
    )
    flat_shape = (slot_count, PIXELS, -1)
    projected_grad = jnp.stack(
        [
            query_grad.reshape(flat_shape),
            key_grad.reshape(flat_shape),
            value_grad.reshape(flat_shape),
        ],
        axis=2,
    ).astype(jnp.bfloat16)
    qkv_grad = jnp.einsum(
        "spc,spjd->cjd", normed_all, projected_grad, preferred_element_type=jnp.float32
    )
    qkv_bias_grad = jnp.sum(projected_grad.astype(jnp.float32), axis=(0, 1))
    normed_grad = back_features(
        jnp.einsum("spjd,cjd->spc", projected_grad, qkv_back, preferred_element_type=jnp.float32)
    )
    norm_value, norm_pull = jax.vjp(group_norm, residual, norm_gains[2], norm_shifts[2])
    residual_grad, gain2_grad, shift2_grad = norm_pull(normed_grad)
    residual_grad = residual_grad + grad_branch
    conv1_low = residual_grad.astype(jnp.bfloat16)
    conv1_bias_grad = jnp.sum(conv1_low.astype(jnp.float32), axis=(0, 1))
    conv1_wgrad = conv_weight_grad(hidden1_all, conv1_low)
    hidden1_grad = back_features(convolve_back(conv1_low, conv_back[1]))
    middle_value, middle_pull = jax.vjp(
        middle, conv_out0, modulation, norm_gains[1], norm_shifts[1]
    )
    conv0_grad, modulation_grad, gain1_grad, shift1_grad = middle_pull(hidden1_grad)
    modulation_low = modulation_grad.astype(jnp.bfloat16)
    aff_bias_grad = jnp.sum(modulation_low.astype(jnp.float32), axis=0)
    aff_grad = jnp.einsum(
        "sc,sjd->cjd", embed_all, modulation_low, preferred_element_type=jnp.float32
    )
    embed_part = jnp.einsum(
        "sjd,cjd->sc", modulation_low, aff_back, preferred_element_type=jnp.float32
    )
    conv0_low = conv0_grad.astype(jnp.bfloat16)
    conv0_bias_grad = jnp.sum(conv0_low.astype(jnp.float32), axis=(0, 1))
    conv0_wgrad = conv_weight_grad(hidden0_all, conv0_low)
    hidden0_part = convolve_back(conv0_low, conv_back[0])
    hidden0_grad, embedding_sum = (
        lax.psum_scatter(
            hidden0_part.astype(jnp.bfloat16), "tensor", scatter_dimension=2, tiled=True
        ).astype(jnp.float32),
        lax.psum_scatter(
            embed_part.astype(jnp.bfloat16), "tensor", scatter_dimension=1, tiled=True
        ).astype(jnp.float32),
    )
    first_value, first_pull = jax.vjp(first_norm, images_f, norm_gains[0], norm_shifts[0])
    images_part, gain0_grad, shift0_grad = first_pull(hidden0_grad)
    images_grad = (images_part + residual_grad).astype(jnp.bfloat16)
    gains_local = jnp.stack([gain0_grad, gain1_grad, gain2_grad])
    shifts_local = jnp.stack([shift0_grad, shift1_grad, shift2_grad])
    biases_local = jnp.stack(
        [
            conv0_bias_grad,
            conv1_bias_grad,
            qkv_bias_grad[0],
            qkv_bias_grad[2],
            proj_bias_grad,
            aff_bias_grad[0],
            aff_bias_grad[1],
        ]
    )
    gains_grad, shifts_grad, biases_grad = lax.psum((gains_local, shifts_local, biases_local), "dp")
    conv_local = jnp.stack([conv0_wgrad, conv1_wgrad])
    conv_summed, aff_summed, qkv_summed, proj_summed = (
        lax.psum_scatter(conv_local, "dp", scatter_dimension=2, tiled=True),
        lax.psum_scatter(aff_grad, "dp", scatter_dimension=0, tiled=True),
        lax.psum_scatter(qkv_grad, "dp", scatter_dimension=0, tiled=True),
        lax.psum_scatter(proj_grad, "dp", scatter_dimension=0, tiled=True),
    )
    return (
        block_output,
        images_grad,
        embedding_sum.astype(jnp.bfloat16),
        gains_grad,
        shifts_grad,
        biases_grad,
        conv_summed,
        aff_summed,
        qkv_summed,
        proj_summed,
    )


def dot(left, right, dims=(((1,), (0,)), ((), ()))):
    return lax.dot_general(left, right, dims, preferred_element_type=jnp.float32)


def device(pair, level, y, x, core):
    return {"dp": ((2 * pair + level) * 2 + y) * 2 + x, "tensor": core}


class Place:
    def __init__(self):
        spot, core = lax.axis_index("dp"), lax.axis_index("tensor")
        self.pair, self.level = spot // 8, lax.rem(spot // 4, 2)
        self.y, self.x, self.core = lax.rem(spot // 2, 2), lax.rem(spot, 2), core
        pair, level, y, x = self.pair, self.level, self.y, self.x
        self.home = level == core
        self.away = level != core
        self.mate = device(pair, 1 - level, y, x, core)
        self.pmate = device(1 - pair, level, y, x, core)
        self.xmate = device(pair, level, y, 1 - x, core)
        self.ymate = device(pair, level, 1 - y, x, core)
        self.cmate = device(pair, level, y, x, 1 - core)
        self.swap = device(pair, core, y, x, level)
        self.far = device(1 - pair, core, y, x, level)

    def greet(self):
        barrier = pltpu.get_barrier_semaphore()
        for other in (self.mate, self.pmate, self.xmate, self.ymate, self.cmate, self.far):
            pl.semaphore_signal(barrier, inc=1, device_id=other, device_id_type=MESH)

        @pl.when(self.away)
        def _():
            pl.semaphore_signal(barrier, inc=1, device_id=self.swap, device_id_type=MESH)

    def meet(self):
        barrier = pltpu.get_barrier_semaphore()

        @pl.when(self.home)
        def _():
            pl.semaphore_wait(barrier, 6)

        @pl.when(self.away)
        def _():
            pl.semaphore_wait(barrier, 7)


class Swap:
    def __init__(self, place, src, dst, sems):
        self.place = place
        self.local = pltpu.make_async_copy(src, dst, sems.at[0])
        self.remote = remote_copy(src, dst, sems.at[1], sems.at[2], place.swap)
        pl.when(place.home)(self.local.start)
        pl.when(place.away)(self.remote.start)

    def wait_recv(self):
        pl.when(self.place.home)(self.local.wait)
        pl.when(self.place.away)(self.remote.wait_recv)

    def wait_send(self):
        pl.when(self.place.away)(self.remote.wait_send)


class Share:
    def __init__(self, place, src, dst_ref, sems):
        self.place = place
        core = place.core
        dst = dst_ref.at[core]
        self.near_copy = remote_copy(src, dst, sems.at[0], sems.at[1], place.cmate)
        self.mate_copy = remote_copy(src, dst, sems.at[2], sems.at[3 + core], place.mate)
        self.swap_copy = remote_copy(src, dst, sems.at[2], sems.at[3 + core], place.swap)
        self.local = pltpu.make_async_copy(src, dst, sems.at[5])
        self.others = [remote_copy(src, dst, sems.at[2], sems.at[3 + part], place.mate) for part in range(2)]

        @pl.when(place.home)
        def _():
            self.mate_copy.start()
            self.local.start()

        @pl.when(place.away)
        def _():
            self.swap_copy.start()
            self.near_copy.start()

    def wait_recv(self):
        @pl.when(self.place.home)
        def _():
            self.local.wait()
            self.near_copy.wait_recv()

        @pl.when(self.place.away)
        def _():
            self.others[0].wait_recv()
            self.others[1].wait_recv()

    def wait_send(self):
        self.mate_copy.wait_send()
        pl.when(self.place.away)(self.near_copy.wait_send)


class Return:
    def __init__(self, place, src_ref, dst_ref, sems):
        self.place, self.src_ref, self.dst_ref, self.sems = place, src_ref, dst_ref, sems
        core = place.core
        self.near_copy = remote_copy(src_ref.at[1 - core], dst_ref.at[0], sems.at[0], sems.at[1], place.cmate)
        self.swap_copy = remote_copy(src_ref.at[1 - core], dst_ref.at[1], sems.at[0], sems.at[2], place.swap)
        self.local = pltpu.make_async_copy(src_ref.at[core], dst_ref.at[0], sems.at[3])
        self.mate_copy = remote_copy(src_ref.at[core], dst_ref.at[1], sems.at[4], sems.at[2], place.mate)

    def start_other(self):
        pl.when(self.place.home)(self.near_copy.start)
        pl.when(self.place.away)(self.swap_copy.start)

    def start_own(self):
        pl.when(self.place.home)(self.local.start)
        pl.when(self.place.away)(self.mate_copy.start)

    def wait_recv(self):
        pl.when(self.place.home)(self.local.wait)
        pl.when(self.place.away)(self.near_copy.wait_recv)
        self.swap_copy.wait_recv()

    def wait_send(self):
        self.near_copy.wait_send()
        pl.when(self.place.away)(self.mate_copy.wait_send)


def halves(start, size):
    first = (size // 128 + 1) // 2 * 128
    return [(start, first, 0), (start + first, size - first, 1)]


def remote_copy(src, dst, send, recv, target):
    return pltpu.make_async_remote_copy(
        src_ref=src, dst_ref=dst, send_sem=send, recv_sem=recv, device_id=target, device_id_type=MESH
    )


def remote(src, dst, send, recv, target):
    copy = remote_copy(src, dst, send, recv, target)
    copy.start()
    return copy


def group_average(width):
    row = lax.broadcasted_iota(jnp.int32, (width, width), 0) // GROUP_SIZE
    col = lax.broadcasted_iota(jnp.int32, (width, width), 1) // GROUP_SIZE
    return jnp.where(row == col, 1.0 / (GROUP_SIZE * PIXELS), 0.0).astype(jnp.float32)


def group_mean(values, average):
    return lax.dot_general(
        jnp.sum(values, axis=1), average, (((1,), (0,)), ((), ())),
        precision=lax.Precision.HIGHEST, preferred_element_type=jnp.float32,
    )


def normalize(values, average):
    away = values - group_mean(values, average)[:, None]
    scale = lax.rsqrt(group_mean(away * away, average) + 1e-05)
    return away * scale[:, None], scale


def normalize_back(grad, normal, scale, average):
    return scale[:, None] * (
        grad - group_mean(grad, average)[:, None] - normal * group_mean(grad * normal, average)[:, None]
    )


def sigmoid(values):
    return 1.0 / (1.0 + jnp.exp(-values))


def silu_slope(values):
    gate = sigmoid(values)
    return gate * (1.0 + values * (1.0 - gate))


def shift_columns(values, step):
    moved = pltpu.roll(values, step % SIDE, 1)
    column = lax.broadcasted_iota(jnp.int32, values.shape, 1)
    return jnp.where(column == (0 if step == 1 else SIDE - 1), 0.0, moved)


def shift_rows(values, step):
    if step == 0:
        return values
    zero = jnp.zeros_like(values[:, :1])
    if step == 1:
        return jnp.concatenate([zero, values[:, : SIDE - 1]], axis=1)
    return jnp.concatenate([values[:, 1:], zero], axis=1)


def both(ref):
    return jnp.concatenate([ref[0], ref[1]], axis=1)


def convolve_row(source, weights, row_tap, sums, first=False):
    rows, width = sums.shape[1:]
    products = dot(source, weights)
    for col_tap in range(3):
        part = products[:, col_tap * width : (col_tap + 1) * width]
        part = shift_rows(part.reshape(-1, SIDE, SIDE, width), 1 - row_tap).reshape(rows, width)
        sums[col_tap] = part if first else sums[col_tap] + part


def convolve_end(sums, start, rows):
    width = sums.shape[2]
    grids = [sums[col_tap, start : start + rows].reshape(rows // SIDE, SIDE, width) for col_tap in range(3)]
    return (shift_columns(grids[0], 1) + grids[1] + shift_columns(grids[2], -1)).reshape(rows, width)


def spread_taps(grad, taps_ref, start=0):
    rows, width = grad.shape
    flat = grad.reshape(rows // SIDE, SIDE, width)
    for col_tap, grid in enumerate((shift_columns(flat, -1), flat, shift_columns(flat, 1))):
        for row_tap in range(3):
            moved = shift_rows(grid.reshape(-1, SIDE, SIDE, width), row_tap - 1)
            tap = row_tap * 3 + col_tap
            taps_ref[start : start + rows, tap * width : (tap + 1) * width] = moved.reshape(rows, width).astype(LOW)


def expand_heads(block, lane_head):
    heads = block.shape[1] // HEAD_DIM
    return jnp.concatenate([jnp.where(lane_head == h, block, jnp.zeros_like(block)) for h in range(heads)], axis=0)


def contract_heads(wide, lane_head):
    total = wide[:PIXELS]
    for h in range(1, wide.shape[1] // HEAD_DIM):
        total = jnp.where(lane_head == h, wide[h * PIXELS : (h + 1) * PIXELS], total)
    return total


def attention(first_slot, end_slot, projected, attended_grad, attended, projected_grad):
    width = attended.shape[1]
    scale = HEAD_DIM ** (-0.5)
    most = 4 * HEAD_DIM
    cells, heads, query, key, value, grad = [], [], [], [], [], []
    for slot in range(first_slot, end_slot):
        rows = slice(slot * PIXELS, (slot + 1) * PIXELS)
        for start in range(0, width, most):
            end = min(start + most, width)
            cells.append((rows, start, end))
            heads.append(lax.broadcasted_iota(jnp.int32, (PIXELS, end - start), 1) // HEAD_DIM)
            query.append(projected[rows, start:end])
            key.append(projected[rows, width + start : width + end])
            value.append(projected[rows, 2 * width + start : 2 * width + end])
            grad.append(attended_grad[rows, start:end])
    query_wide = [expand_heads(*each) for each in zip(query, heads)]
    scores = [dot(left, right, NT) * scale for left, right in zip(query_wide, key)]
    grad_wide = [expand_heads(*each) for each in zip(grad, heads)]
    grad_probs = [dot(left, right, NT) for left, right in zip(grad_wide, value)]
    powers = [jnp.exp(each - jnp.max(each, axis=1, keepdims=True)) for each in scores]
    probabilities = [each / jnp.sum(each, axis=1, keepdims=True) for each in powers]
    weights_low = [each.astype(LOW) for each in probabilities]
    attended_wide = [dot(left, right) for left, right in zip(weights_low, value)]
    value_grad = [dot(left, right, TN) for left, right in zip(weights_low, grad_wide)]
    score_low = [
        (prob * (each - jnp.sum(each * prob, axis=1, keepdims=True))).astype(LOW) for prob, each in zip(probabilities, grad_probs)
    ]
    query_grad = [dot(left, right) for left, right in zip(score_low, key)]
    key_grad = [dot(left, right, TN) * scale for left, right in zip(score_low, query_wide)]
    for at, (rows, start, end) in enumerate(cells):
        attended[rows, start:end] = contract_heads(attended_wide[at], heads[at]).astype(LOW)
        projected_grad[rows, start:end] = (contract_heads(query_grad[at], heads[at]) * scale).astype(LOW)
        projected_grad[rows, width + start : width + end] = key_grad[at].astype(LOW)
        projected_grad[rows, 2 * width + start : 2 * width + end] = value_grad[at].astype(LOW)


CONV0, AFF, CONV1, PROJ, QKV = 0, 9, 11, 20, 21


C0A, C0B, C0C, C1A, C1B, C1C, SCALE_SHIFT, OUTPUT, HEADS = range(9)

def own_parameters(gains, shifts, biases, par):
    par[...] = jnp.zeros_like(par)
    par[0:3] = gains[...]
    par[3:6] = shifts[...]
    par[6:13] = biases[...]


def slot_mask(counts, slots, width):
    return (lax.broadcasted_iota(jnp.int32, (slots, width), 0) < counts[0]).astype(jnp.float32)


def forward_kernel(
    counts, img_in, emb, gains, shifts, biases, cot_in, aff, qkv, conv, proj,
    full_out, hall0_out, hall1_out, normal1_out, scale1_out, modulation_out, emb_all_out, par_out,
    nall_out, attended_out, residual_out, normal2_out, scale2_out, pgrad_out,
    full, hall0, hall1, normal1, scale1, modulation, emb_all, par, nall, attended, residual, normal2, scale2, pgrad,
    sums, projected, branch_low, ag_own, ag_send, ag_recv, ag_low, emb_own, par_own, hidden_own, conv_own, conv_in, aff_own,
    img, cot, in_sem, first_local, first_send, first_recv, sends, recvs, swap_sem, share_sem, mate_send, mate_recv, out_sem,
):
    place = Place()
    pair, level, y, x, core = place.pair, place.level, place.y, place.x, place.core
    width = img.shape[1]
    slots = scale1.shape[0]
    shape = (slots, PIXELS, width)
    place.greet()
    img_load = pltpu.make_async_copy(img_in, img, in_sem.at[0])
    cot_load = pltpu.make_async_copy(cot_in, cot, in_sem.at[1])
    img_load.start()
    cot_load.start()
    groups = [
        (CONV0, 3, [(conv.at[0, tap], CONV0 + tap, 1) for tap in (0, 1, 2)], True),
        (CONV0 + 3, 3, [(conv.at[0, tap], CONV0 + tap, 1) for tap in (3, 4, 5)], True),
        (CONV0 + 6, 3, [(conv.at[0, tap], CONV0 + tap, 1) for tap in (6, 7, 8)], True),
        (CONV1, 3, [(conv.at[1, tap], CONV1 + tap, 1) for tap in (0, 1, 2)], True),
        (CONV1 + 3, 3, [(conv.at[1, tap], CONV1 + tap, 1) for tap in (3, 4, 5)], True),
        (CONV1 + 6, 3, [(conv.at[1, tap], CONV1 + tap, 1) for tap in (6, 7, 8)], True),
        (AFF, 2, [(aff_own, AFF, 2)], True),
        (PROJ, 1, [(proj, PROJ, 1)], False),
        (QKV, 3, [(qkv.at[part], QKV + part, 1) for part in range(3)], False),
    ]
    started = {}

    def stage(group, s):
        column, count, sources, wide_way = groups[group]
        if s == 0 and wide_way:
            found = []
            for at, (src, first, many) in enumerate(sources):
                dst = full.at[pair, level, y, x, :, pl.ds(first * width, many * width)]
                found.append(remote(src, dst, first_send.at[group, at], first_recv.at[group, at], place.far))
                found.append(Swap(place, src, dst, first_local.at[group, at]))
            started[group, 0] = found
            return
        if s == 0:
            started[group, 0], started[group, "local"] = [], []
            for at, (src, first, many) in enumerate(sources):
                dst = full.at[pair, level, y, x, :, pl.ds(first * width, many * width)]
                local = pltpu.make_async_copy(src, dst, first_local.at[group, at, 0])
                local.start()
                started[group, "local"].append(local)
                started[group, 0].append(remote(src, dst, first_send.at[group, at], first_recv.at[group, at], place.mate))
            return
        if s == 1:
            for copy in started[group, 0]:
                copy.wait_recv()
            for copy in started.pop((group, "local"), []):
                copy.wait()
        for start, size, odd in halves(column * width, count * width):
            cols = pl.ds(start, size)
            for copy in started.get((group, odd, s - 1), []):
                copy.wait_recv()
            first, second = (place.ymate, place.xmate) if odd else (place.xmate, place.ymate)
            if wide_way:
                if s == 1:
                    block, target = full.at[:, core, y, x, :, cols], first
                elif s == 2:
                    block, target = (full.at[:, core, :, x, :, cols] if odd else full.at[:, core, y, :, :, cols]), second
                elif s == 3:
                    block, target = full.at[:, core, :, :, :, cols], place.cmate
            else:
                if s == 1:
                    block, target = full.at[pair, :, y, x, :, cols], place.pmate
                elif s == 2:
                    block, target = full.at[:, :, y, x, :, cols], first
                elif s == 3:
                    block, target = (full.at[:, :, :, x, :, cols] if odd else full.at[:, :, y, :, :, cols]), second
            if s < 4:
                started[group, odd, s] = [remote(block, block, sends.at[group, odd, s - 1], recvs.at[group, odd, s - 1], target)]

    pair_copies = []

    def to(target, src, dst):
        at = len(pair_copies)
        pair_copies.append(remote(src, dst, mate_send.at[at], mate_recv.at[at], target))
        return pair_copies[-1]

    def weights(column, count, part=None):
        cols = pl.ds(column * width, count * width)
        block = full[:, :, :, :, :, cols] if part is None else full[part, :, :, :, :, cols]
        return block.reshape(-1, count * width)

    out_copies = []

    def keep(src, dst):
        out_copies.append(pltpu.make_async_copy(src, dst, out_sem.at[len(out_copies)]))
        out_copies[-1].start()

    average = group_average(width)
    rows = img.shape[0]
    near = (slots + 1) // 2
    parts = [(0, near), (near, slots)]
    spans = [pl.ds(first * PIXELS, (end - first) * PIXELS) for first, end in parts]
    held = types.SimpleNamespace(conv1=[None, None], normed=[None, None])

    def prepare():
        for part in range(2):
            aff_own[:, part * width : (part + 1) * width] = aff[:, part, :]
        padded = emb_own.shape[0]
        choose = lax.broadcasted_iota(jnp.int32, (padded, slots), 0) == lax.broadcasted_iota(jnp.int32, (padded, slots), 1)
        emb_own[...] = dot(choose.astype(LOW), emb[...]).astype(LOW)
        own_parameters(gains, shifts, biases, par_own)

    def start():
        held.par = Swap(place, par_own, par, swap_sem.at[0])
        held.emb = Share(place, emb_own, emb_all, share_sem.at[0])

    def hidden0_own():
        img_load.wait()
        normal, _ = normalize(img[...].astype(jnp.float32).reshape(shape), average)
        scaled = normal * par_own[0:1] + par_own[3:4]
        hidden_own[...] = (scaled * sigmoid(scaled)).reshape(-1, width).astype(LOW)
        held.hidden0 = Share(place, hidden_own, hall0, share_sem.at[1])

    def branch_own():
        cot_load.wait()
        branch_low[...] = (slot_mask(counts, slots, width)[:, None] * cot[...].reshape(shape)).reshape(-1, width).astype(LOW)

    def hidden0_here():
        held.par.wait_recv()
        held.emb.wait_recv()
        held.hidden0.wait_recv()
        keep(par, par_out)
        keep(emb_all, emb_all_out)
        keep(hall0, hall0_out)

    def modulate():
        changes = dot(both(emb_all), weights(AFF, 2)) + jnp.concatenate([par[11:12], par[12:13]], axis=1)
        modulation[...] = changes
        keep(modulation, modulation_out)

    def middle():
        changes = modulation[...]
        conv_out0 = (convolve_end(sums, 0, rows) + par[6:7]).reshape(shape)
        normal, scale = normalize(conv_out0, average)
        scaled = (normal * par[1:2] + par[4:5]) * (1.0 + changes[:slots, None, :width]) + changes[:slots, None, width:]
        hall1[level] = (scaled * sigmoid(scaled)).reshape(-1, width).astype(LOW)
        held.hidden1 = to(place.mate, hall1.at[level], hall1.at[level])
        normal1[...] = normal.reshape(-1, width)
        scale1[...] = scale
        keep(normal1, normal1_out)
        keep(scale1, scale1_out)

    def hidden1_here():
        held.hidden1.wait_recv()
        keep(hall1, hall1_out)

    def conv1_end(part):
        conv_own[spans[part]] = convolve_end(sums, parts[part][0] * PIXELS, spans[part].size).astype(LOW)
        held.conv1[part] = Swap(place, conv_own.at[spans[part]], conv_in.at[spans[part]], swap_sem.at[1 + part])

    def attended_grad():
        ag_send[...] = dot(branch_low[...], weights(PROJ, 1, 1 - core), NT).astype(LOW)
        held.ag = to(place.cmate, ag_send, ag_recv)
        ag_own[...] = dot(branch_low[...], weights(PROJ, 1, core), NT)

    def attended_grad_sum():
        held.ag.wait_recv()
        ag_low[...] = (ag_own[...] + ag_recv[...].astype(jnp.float32)).astype(LOW)

    def residual_norm(part):
        held.conv1[part].wait_recv()
        span = spans[part]
        total = img[span].astype(jnp.float32) + (conv_in[span].astype(jnp.float32) + par_own[7:8])
        normal, scale = normalize(total.reshape(-1, PIXELS, width), average)
        nall[core, span] = (normal * par_own[2:3] + par_own[5:6]).reshape(-1, width).astype(LOW)
        held.normed[part] = to(place.cmate, nall.at[core, span], nall.at[core, span])
        residual[span] = total
        normal2[span] = normal.reshape(-1, width)
        scale2[parts[part][0] : parts[part][1]] = scale

    def project(part):
        span = spans[part]
        bias = jnp.concatenate([par_own[8:9], jnp.zeros((1, width), jnp.float32), par_own[9:10]], axis=1)
        own = dot(nall[core, span], weights(QKV, 3, core)) + bias
        held.normed[part].wait_recv()
        projected[span] = (own + dot(nall[1 - core, span], weights(QKV, 3, 1 - core))).astype(LOW)

    def attend(part):
        attention(*parts[part], projected, ag_low, attended, pgrad)

    def keep_norm():
        keep(residual, residual_out)
        keep(normal2, normal2_out)
        keep(scale2, scale2_out)

    def keep_normed():
        keep(nall, nall_out)

    def rows_here(tap):
        convolve_row(both(hall0), weights(CONV0 + 3 * tap, 3), tap, sums, tap == 0)

    def rows_own(tap):
        convolve_row(hall1[level], weights(CONV1 + 3 * tap, 3, level), tap, sums, tap == 0)

    def rows_other(tap):
        convolve_row(hall1[1 - level], weights(CONV1 + 3 * tap, 3, 1 - level), tap, sums)

    def stages(*steps):
        for group, s in steps:
            stage(group, s)
            if s == 4:
                cols = pl.ds(groups[group][0] * width, groups[group][1] * width)
                keep(full.at[:, :, :, :, :, cols], full_out.at[:, :, :, :, :, cols])

    prepare()
    place.meet()
    stages((C0A, 0))
    start()
    branch_own()
    stages((C0B, 0))
    hidden0_own()
    stages((SCALE_SHIFT, 0), (C0A, 1), (C0C, 0), (C0B, 1), (C1A, 0), (C0A, 2), (SCALE_SHIFT, 1), (C1B, 0))
    stages((C0B, 2), (C0C, 1), (C1C, 0), (C0A, 3), (SCALE_SHIFT, 2), (C1A, 1), (OUTPUT, 0), (C0B, 3))
    stages((C0C, 2), (C1B, 1), (HEADS, 0), (C0A, 4), (SCALE_SHIFT, 3), (C1A, 2), (C1C, 1))
    hidden0_here()
    rows_here(0)
    stages((C0B, 4), (C0C, 3), (C1B, 2), (OUTPUT, 1))
    rows_here(1)
    stages((SCALE_SHIFT, 4), (C1A, 3), (C1C, 2), (HEADS, 1))
    modulate()
    stages((C0C, 4), (C1B, 3), (OUTPUT, 2))
    rows_here(2)
    middle()
    stages((C1A, 4), (C1C, 3), (HEADS, 2))
    rows_own(0)
    stages((C1B, 4), (OUTPUT, 3))
    rows_own(1)
    stages((C1C, 4), (HEADS, 3))
    rows_own(2)
    hidden1_here()
    rows_other(0)
    rows_other(1)
    rows_other(2)
    conv1_end(0)
    conv1_end(1)
    stages((OUTPUT, 4))
    attended_grad()
    stages((HEADS, 4))
    residual_norm(0)
    residual_norm(1)
    attended_grad_sum()
    keep_norm()
    project(0)
    attend(0)
    project(1)
    keep_normed()
    attend(1)
    keep(pgrad, pgrad_out)
    keep(attended, attended_out)
    for copies in list(started.values()) + [pair_copies, [held.par, held.emb, held.hidden0, *held.conv1]]:
        for copy in copies:
            copy.wait_send()
    for copy in out_copies:
        copy.wait()


def backward_kernel(
    counts, img_in, gains, shifts, biases, cot_in,
    full, hall0_in, hall1_in, normal1_in, scale1_in, modulation_in, emb_all_in, par_in,
    nall_in, attended_in, residual_in, normal2_in, scale2_in, pgrad_in,
    block_out, img_grad, emb_grad, gains_grad, shifts_grad, biases_grad, conv_grad, aff_grad, qkv_grad, proj_grad,
    hall0, hall1, normal1, scale1, modulation, emb_all, par, nall, normal2, scale2, pgrad,
    work, r0, r1, r2, last, wbuf, qbuf, abuf, pbuf, taps, aall, rgrad, own_half, mate_out, mate_in, ret_in, low_own, low_in,
    emb_out, emb_in, emb_sum, emb_end, branch, par_own, small_here, small_there, small, small_in,
    img, cot, load_sem, sends, recvs, swap_sem, small_send, small_recv, mate_send, mate_recv, end_sem, ret_sem,
):
    place = Place()
    pair, level, y, x, core = place.pair, place.level, place.y, place.x, place.core
    width = img.shape[1]
    slots = scale1.shape[0]
    shape = (slots, PIXELS, width)
    place.greet()
    loads = []

    def load(src, dst):
        loads.append(pltpu.make_async_copy(src, dst, load_sem.at[len(loads)]))
        loads[-1].start()
        return loads[-1]

    def load_weights(column, count, dst):
        return load(full.at[:, :, :, :, :, pl.ds(column * width, count * width)], dst)

    pgrad_load = load(pgrad_in, pgrad)
    qkv_load = load_weights(QKV, 3, qbuf)
    cot_load = load(cot_in, cot)
    attended_load = load(attended_in, aall.at[core])
    normed_loads = [load(nall_in, nall), load(normal2_in, normal2), load(scale2_in, scale2)]
    conv1_loads = [load_weights(CONV1, 9, wbuf), load(hall1_in, hall1)]
    middle_loads = [load(normal1_in, normal1), load(scale1_in, scale1), load(modulation_in, modulation), load(par_in, par)]
    conv0_loads = [load(hall0_in, hall0), load(emb_all_in, emb_all), load_weights(AFF, 2, abuf)]
    end_loads = [load_weights(PROJ, 1, pbuf), load(img_in, img)]
    pair_copies = []

    def to(at, target, src, dst):
        pair_copies.append(remote(src, dst, mate_send.at[at], mate_recv.at[at], target))
        return pair_copies[-1]

    groups = (
        (CONV0, 3, True), (CONV0 + 3, 3, True), (CONV0 + 6, 3, True), (CONV1, 3, True), (CONV1 + 3, 3, True), (CONV1 + 6, 3, True),
        (AFF, 2, True), (PROJ, 1, False), (QKV, 3, False),
    )
    started = {}

    def deliver(start, size, value):
        column, offset = start // width, start % width
        while size:
            now = min(size, width - offset)
            part, value = value[:, :now], value[:, now:]
            if column < AFF or CONV1 <= column < PROJ:
                tap = column if column < AFF else column - CONV1 + 9
                conv_grad[tap // 9, tap % 9, :, offset : offset + now] = part
            else:
                ref, first = (aff_grad, AFF) if column < CONV1 else (proj_grad, PROJ) if column < QKV else (qkv_grad, QKV)
                if ref is proj_grad:
                    ref[:, offset : offset + now] = part
                elif ref is qkv_grad:
                    ref[column - first, :, offset : offset + now] = part
                else:
                    ref[:, column - first, offset : offset + now] = part
            column, offset, size = column + 1, 0, size - now

    def add(at, cols, received):
        total = work[at + (slice(None), cols)].astype(jnp.float32) + received.astype(jnp.float32)
        work[at + (slice(None), cols)] = total.astype(LOW)

    def stage(group, s):
        column, count, wide_way = groups[group]
        for start, size, odd in halves(column * width, count * width):
            cols = pl.ds(start, size)
            for copy in started.get((group, odd, s - 1), []):
                copy.wait_recv()
            first, second = (place.ymate, place.xmate) if odd else (place.xmate, place.ymate)
            if wide_way:
                if s == 0:
                    src, dst, target = work.at[:, 1 - core, :, :, :, cols], r0.at[:, :, :, :, cols], place.cmate
                elif s == 1:
                    for pp in range(2):
                        for yy in range(2):
                            for xx in range(2):
                                add((pp, core, yy, xx), cols, r0[pp, yy, xx, :, cols])
                    src = work.at[:, core, 1 - y, :, :, cols] if odd else work.at[:, core, :, 1 - x, :, cols]
                    dst, target = r1.at[:, :, :, cols], first
                elif s == 2:
                    for pp in range(2):
                        for other in range(2):
                            add((pp, core, y, other) if odd else (pp, core, other, x), cols, r1[pp, other, :, cols])
                    src = work.at[:, core, y, 1 - x, :, cols] if odd else work.at[:, core, 1 - y, x, :, cols]
                    dst, target = r2.at[:, :, cols], second
                elif s == 3:
                    for pp in range(2):
                        add((pp, core, y, x), cols, r2[pp, :, cols])
                    far = remote(
                        work.at[1 - pair, core, y, x, :, cols], last.at[1, :, cols], sends.at[group, odd, 3], recvs.at[group, odd, 3], place.far
                    )
                    started[group, odd, 3] = [
                        far, Swap(place, work.at[pair, core, y, x, :, cols], last.at[0, :, cols], swap_sem.at[group, odd])
                    ]
                    continue
                else:
                    deliver(start, size, last[0, :, cols].astype(jnp.float32) + last[1, :, cols].astype(jnp.float32))
                    continue
            else:
                if s == 0:
                    src = work.at[:, :, 1 - y, :, :, cols] if odd else work.at[:, :, :, 1 - x, :, cols]
                    dst, target = r0.at[:, :, :, :, cols], first
                elif s == 1:
                    for pp in range(2):
                        for ll in range(2):
                            for other in range(2):
                                add((pp, ll, y, other) if odd else (pp, ll, other, x), cols, r0[pp, ll, other, :, cols])
                    src = work.at[:, :, y, 1 - x, :, cols] if odd else work.at[:, :, 1 - y, x, :, cols]
                    dst, target = r1.at[:, :, :, cols], second
                elif s == 2:
                    for pp in range(2):
                        for ll in range(2):
                            add((pp, ll, y, x), cols, r1[pp, ll, :, cols])
                    src, dst, target = work.at[1 - pair, :, y, x, :, cols], r2.at[:, :, cols], place.pmate
                elif s == 3:
                    for ll in range(2):
                        add((pair, ll, y, x), cols, r2[ll, :, cols])
                    src, dst, target = work.at[pair, 1 - level, y, x, :, cols], last.at[1, :, cols], place.mate
                else:
                    deliver(start, size, work[pair, level, y, x, :, cols].astype(jnp.float32) + last[1, :, cols].astype(jnp.float32))
                    continue
            started[group, odd, s] = [remote(src, dst, sends.at[group, odd, s], recvs.at[group, odd, s], target)]

    def weight_grad(group, source, grad):
        column, count, _ = groups[group]
        for part in range(2):
            product = dot(source[part], grad, TN).astype(LOW)
            work[part, :, :, :, :, pl.ds(column * width, count * width)] = product.reshape(2, 2, 2, -1, count * width)
        stage(group, 0)

    def channels(ref, part):
        return ref[part].reshape(-1, ref.shape[-1])

    def column_sum(values):
        return jnp.sum(values.reshape(-1, values.shape[-1]), axis=0, keepdims=True)

    def three(part):
        return taps[:, pl.ds(part * 3 * width, 3 * width)]

    average = group_average(width)
    own_parameters(gains, shifts, biases, par_own)
    small_here[...] = jnp.zeros_like(small_here)
    small_there[...] = jnp.zeros_like(small_there)
    mask = slot_mask(counts, slots, width)
    held = types.SimpleNamespace(normed=[None, None], low=[None, None])

    near = (slots + 1) // 2
    parts = [(0, near), (near, slots)]
    spans = [pl.ds(first * PIXELS, (end - first) * PIXELS) for first, end in parts]

    def normed_other(part):
        if part == 0:
            pgrad_load.wait()
            qkv_load.wait()
        mate_out[0, spans[part]] = dot(pgrad[spans[part]], channels(qbuf, 1 - core), NT).astype(LOW)
        held.normed[part] = to(part, place.cmate, mate_out.at[0, spans[part]], mate_in.at[0, spans[part]])

    def attended_other():
        attended_load.wait()
        held.attended = to(4, place.cmate, aall.at[core], aall.at[core])

    def normed_own():
        cot_load.wait()
        own_half[...] = dot(pgrad[...], channels(qbuf, core), NT)
        branch[...] = (mask[:, None] * cot[...].reshape(shape)).reshape(-1, width).astype(LOW)

    def qkv_weights():
        normed_loads[0].wait()
        weight_grad(HEADS, nall, pgrad[...])

    def proj_weights():
        held.attended.wait_recv()
        weight_grad(OUTPUT, aall, branch[...])

    def residual_grads(part):
        if part == 0:
            for now in normed_loads[1:]:
                now.wait()
        held.normed[part].wait_recv()
        span, (first, end) = spans[part], parts[part]
        part_shape = (end - first, PIXELS, width)
        normed_grad = (own_half[span] + mate_in[0, span].astype(jnp.float32)).reshape(part_shape)
        normal = normal2[span].reshape(part_shape)
        residual_grad = normalize_back(normed_grad * par_own[2:3], normal, scale2[first:end], average)
        residual_grad = (residual_grad + mask[first:end, None] * cot[span].reshape(part_shape)).reshape(-1, width)
        low_own[span] = residual_grad.astype(LOW)
        held.low[part] = Swap(place, low_own.at[span], low_in.at[span], end_sem.at[3 * part])
        rgrad[span] = residual_grad
        small_here[2:3] = small_here[2:3] + column_sum(normed_grad * normal)
        small_here[5:6] = small_here[5:6] + column_sum(normed_grad)

    def first_sums():
        small_here[7:8] = column_sum(low_own[...].astype(jnp.float32))
        small_here[8:9] = column_sum(pgrad[:, :width].astype(jnp.float32))
        small_here[9:10] = column_sum(pgrad[:, 2 * width :].astype(jnp.float32))
        small_here[10:11] = column_sum(branch[...].astype(jnp.float32))

    def conv1_taps(part):
        held.low[part].wait_recv()
        spread_taps(low_in[spans[part]].astype(jnp.float32), taps, parts[part][0] * PIXELS)

    def hidden1_other():
        for now in conv1_loads:
            now.wait()
        mate_out[1] = dot(taps[...], channels(wbuf, 1 - level), NT).astype(LOW)
        held.hidden1 = to(2, place.mate, mate_out.at[1], mate_in.at[1])

    def hidden1_own():
        own_half[...] = dot(taps[...], channels(wbuf, level), NT)
        conv0_loads.append(load_weights(CONV0, 9, wbuf))

    def middle_back():
        for now in middle_loads:
            now.wait()
        held.hidden1.wait_recv()
        hidden1_grad = (own_half[...] + mate_in[1].astype(jnp.float32)).reshape(shape)
        end_loads.append(load(residual_in, own_half))
        normal = normal1[...].reshape(shape)
        changes = modulation[...]
        change = 1.0 + changes[:slots, None, :width]
        inner = normal * par[1:2] + par[4:5]
        grad = hidden1_grad * silu_slope(inner * change + changes[:slots, None, width:])
        modulation_grad = jnp.concatenate([jnp.sum(grad * inner, axis=1), jnp.sum(grad, axis=1)], axis=1)
        grad = grad * change
        conv0_low = normalize_back(grad * par[1:2], normal, scale1[...], average).astype(LOW).astype(jnp.float32)
        conv0_low = conv0_low.reshape(-1, width)
        spread_taps(conv0_low, taps)
        small_there[1:2] = column_sum(grad * normal)
        small_there[4:5] = column_sum(grad)
        small_there[6:7] = column_sum(conv0_low)
        rest = jnp.zeros((modulation.shape[0] - slots, 2 * width), jnp.float32)
        modulation_low = jnp.concatenate([modulation_grad, rest], axis=0).astype(LOW)
        modulation_sum = column_sum(modulation_low.astype(jnp.float32))
        small_there[11:12] = modulation_sum[:, :width]
        small_there[12:13] = modulation_sum[:, width:]
        held.modulation = modulation_low
        held.small = Swap(place, small_there, small_in.at[4], end_sem.at[1])

    def hidden0_other():
        for now in conv0_loads:
            now.wait()
        done = (*held.normed, held.hidden1)
        for copy in done:
            copy.wait_send()
        pair_copies[:] = [copy for copy in pair_copies if all(copy is not other for other in done)]
        held.back = Return(place, mate_out, ret_in, ret_sem)
        mate_out[1 - core] = dot(taps[...], channels(wbuf, 1 - core), NT).astype(LOW)
        held.back.start_other()

    def hidden0_own():
        mate_out[core] = dot(taps[...], channels(wbuf, core), NT).astype(LOW)
        held.back.start_own()

    def aff_part():
        weight_grad(SCALE_SHIFT, emb_all, held.modulation)
        emb_out[...] = dot(held.modulation, channels(abuf, 1 - level), NT).astype(LOW)
        held.emb = to(3, place.mate, emb_out, emb_in)
        held.emb_own = dot(held.modulation, channels(abuf, level), NT)

    def embedding_sum():
        held.emb.wait_recv()
        emb_sum[...] = (held.emb_own + emb_in[...].astype(jnp.float32)).astype(LOW)
        held.emb_end = Swap(place, emb_sum, emb_end, end_sem.at[2])

    def embedding_end():
        held.emb_end.wait_recv()
        emb_grad[...] = emb_end[...][:slots]

    def block_end():
        for now in end_loads:
            now.wait()
        joined = dot(both(aall), pbuf[...].reshape(-1, width)) + par_own[10:11]
        block = mask[:, None] * (own_half[...] + joined).reshape(shape)
        block_out[...] = block.reshape(-1, width).astype(LOW)

    small_copies = []

    def small_step(at, target):
        small_copies.append(remote(small.at[at], small_in.at[at], small_send.at[at], small_recv.at[at], target))

    def small_add(at):
        small_copies[at].wait_recv()
        small[at + 1] = small[at] + small_in[at]

    def images_end():
        normal, scale = normalize(img[...].astype(jnp.float32).reshape(shape), average)
        slope = silu_slope(normal * par_own[0:1] + par_own[3:4])
        held.back.wait_recv()
        grad = (ret_in[0].astype(jnp.float32) + ret_in[1].astype(jnp.float32)).reshape(shape) * slope
        small_here[0:1] = column_sum(grad * normal)
        small_here[3:4] = column_sum(grad)
        held.small.wait_recv()
        small[0] = small_here[...] + small_in[4]
        small_step(0, place.mate)
        images_part = normalize_back(grad * par_own[0:1], normal, scale, average)
        img_grad[...] = (images_part.reshape(-1, width) + rgrad[...]).astype(LOW)

    def small1():
        small_add(0)
        small_step(1, place.pmate)

    def small2():
        small_add(1)
        small_step(2, place.xmate)

    def small3():
        small_add(2)
        small_step(3, place.ymate)

    def small_end():
        small_add(3)
        gains_grad[...] = small[4, 0:3]
        shifts_grad[...] = small[4, 3:6]
        biases_grad[...] = small[4, 6:13]

    def conv_weight_grad(group):
        weight_grad(group, hall0 if group < C1A else hall1, three(group % 3))

    def stages(*steps):
        for group, s in steps:
            stage(group, s)

    place.meet()
    normed_other(0)
    normed_other(1)
    qkv_weights()
    attended_other()
    normed_own()
    residual_grads(0)
    residual_grads(1)
    proj_weights()
    first_sums()
    conv1_taps(0)
    conv1_taps(1)
    hidden1_other()
    conv_weight_grad(C1A)
    stages((HEADS, 1))
    conv_weight_grad(C1B)
    stages((C1A, 1), (OUTPUT, 1))
    conv_weight_grad(C1C)
    stages((C1B, 1))
    hidden1_own()
    stages((C1C, 1), (HEADS, 2), (C1A, 2))
    middle_back()
    hidden0_other()
    conv_weight_grad(C0A)
    stages((C1B, 2))
    hidden0_own()
    conv_weight_grad(C0B)
    stages((C0A, 1), (OUTPUT, 2))
    conv_weight_grad(C0C)
    stages((C1C, 2), (C0B, 1))
    aff_part()
    stages((HEADS, 3), (C1A, 3), (C0C, 1), (C0A, 2), (SCALE_SHIFT, 1), (C1B, 3), (OUTPUT, 3))
    block_end()
    stages((C0B, 2), (C1C, 3))
    embedding_sum()
    stages((C0C, 2), (SCALE_SHIFT, 2), (C0A, 3))
    images_end()
    small1()
    stages((HEADS, 4), (C1A, 4), (C0B, 3))
    small2()
    stages((C1B, 4), (OUTPUT, 4), (C0C, 3))
    small3()
    stages((SCALE_SHIFT, 3), (C1C, 4), (C0A, 4))
    embedding_end()
    stages((C0B, 4))
    small_end()
    stages((C0C, 4), (SCALE_SHIFT, 4))
    for copies in list(started.values()) + [pair_copies, small_copies, [*held.low, held.back, held.small, held.emb_end]]:
        for copy in copies:
            copy.wait_send()


def finish_kernel(*refs):
    count = len(refs) // 3
    given, returned, held, sems = refs[:count], refs[count : 2 * count], refs[2 * count : 3 * count], refs[-1]
    into = [pltpu.make_async_copy(given[at], held[at], sems.at[0, at]) for at in range(count)]
    out = [pltpu.make_async_copy(held[at], returned[at], sems.at[1, at]) for at in range(count)]
    for copy in into:
        copy.start()
    for at in range(count):
        into[at].wait()
        out[at].start()
    for copy in out:
        copy.wait()


def fast_body(
    images, embedding, counts, norm_gains, norm_shifts, lin_biases, conv_weights, aff_weights, qkv_weights, proj_weights, cotangent
):
    slots, _, width = images.shape
    rows = slots * PIXELS
    depth = conv_weights.shape[2]
    padded = -(-slots // 16) * 16
    low, f32 = LOW, jnp.float32
    vmem, anyw = pl.BlockSpec(memory_space=pltpu.VMEM), pl.BlockSpec(memory_space=pl.ANY)
    smem = pl.BlockSpec(memory_space=pltpu.SMEM)
    dma, buf, shape = pltpu.SemaphoreType.DMA, pltpu.VMEM, jax.ShapeDtypeStruct

    def whole(columns):
        return GRID + (depth, columns * width)

    pair = (2, rows, width)
    one = (rows, width)
    par = (16, width)
    few = (padded, width)
    middle = [
        (pair, low), (pair, low), (one, f32), ((slots, width), f32), ((padded, 2 * width), f32), ((2,) + few, low), (par, f32),
        (pair, low), (one, low), (one, f32), (one, f32), ((slots, width), f32), ((rows, 3 * width), low),
    ]
    img, cot = images.reshape(one), cotangent.reshape(one)
    kept = pl.pallas_call(
        forward_kernel,
        name="gather_forward",
        out_shape=[shape(whole(24), low)] + [shape(*each) for each in middle],
        in_specs=[smem, anyw] + [vmem] * 4 + [anyw, vmem] + [anyw] * 3,
        out_specs=[anyw] * 14,
        scratch_shapes=[buf(whole(24), low)] + [buf(*each) for each in middle] + [
            buf((3, rows, width), f32), buf((rows, 3 * width), low), buf(one, low), buf(one, f32),
            buf(one, low), buf(one, low), buf(one, low), buf(few, low), buf(par, f32),
            buf(one, low), buf(one, low), buf(one, low), buf((depth, 2 * width), low),
            buf(one, low), buf(one, f32), dma((2,)), dma((9, 3, 3)), dma((9, 3)), dma((9, 3)), dma((9, 2, 3)), dma((9, 2, 3)), dma((3, 3)), dma((2, 6)), dma((4,)), dma((4,)), dma((22,)),
        ],
        compiler_params=pltpu.CompilerParams(collective_id=0, has_side_effects=True, vmem_limit_bytes=60 * 2**20),
    )(counts, img, embedding, norm_gains, norm_shifts, lin_biases, cot, aff_weights, jnp.transpose(qkv_weights, (1, 0, 2)), conv_weights, proj_weights)
    outs = [
        shape(one, low), shape(one, low), shape(embedding.shape, low), shape(norm_gains.shape, f32), shape(norm_shifts.shape, f32),
        shape(lin_biases.shape, f32), shape(conv_weights.shape, f32), shape(aff_weights.shape, f32), shape((3, depth, width), f32),
        shape(proj_weights.shape, f32),
    ]
    results = pl.pallas_call(
        backward_kernel,
        name="backward_scatter",
        out_shape=outs,
        in_specs=[smem, anyw] + [vmem] * 3 + [anyw] * 15,
        out_specs=[vmem] * 10,
        scratch_shapes=[buf(*each) for at, each in enumerate(middle) if at not in (8, 9)] + [
            buf(whole(24), low), buf((2, 2, 2, depth, 24 * width), low), buf((2, 2, depth, 24 * width), low),
            buf((2, depth, 24 * width), low), buf((2, depth, 24 * width), low),
            buf(whole(9), low), buf(whole(3), low), buf(whole(2), low), buf(whole(1), low),
            buf((rows, 9 * width), low), buf(pair, low), buf(one, f32), buf(one, f32),
            buf(pair, low), buf(pair, low), buf(pair, low), buf(one, low), buf(one, low),
            buf(few, low), buf(few, low), buf(few, low), buf(few, low),
            buf(one, low), buf(par, f32), buf(par, f32), buf(par, f32), buf((5,) + par, f32), buf((5,) + par, f32),
            buf(one, low), buf(one, f32), dma((20,)), dma((9, 2, 4)), dma((9, 2, 4)), dma((9, 2, 3)), dma((4,)), dma((4,)), dma((5,)), dma((5,)), dma((4, 3)), dma((5,)),
        ],
        compiler_params=pltpu.CompilerParams(collective_id=1, has_side_effects=True, vmem_limit_bytes=63 * 2**20),
    )(counts, img, norm_gains, norm_shifts, lin_biases, cot, *kept)
    ends = pl.pallas_call(
        finish_kernel,
        name="finish",
        out_shape=outs,
        in_specs=[anyw] * 10,
        out_specs=[anyw] * 10,
        scratch_shapes=[buf(each.shape, each.dtype) for each in outs] + [dma((2, 10))],
    )(*results)
    return (
        ends[0].reshape(images.shape), ends[1].reshape(images.shape), *ends[2:8], jnp.transpose(ends[8], (1, 0, 2)), ends[9]
    )


def solution(mesh):
    return jax.shard_map(
        fast_body if mesh.shape["dp"] == 16 else body,
        mesh=mesh,
        in_specs=(
            P("dp", None, "tensor"),
            P("dp", "tensor"),
            P("dp"),
            P(None, "tensor"),
            P(None, "tensor"),
            P(None, "tensor"),
            P(None, None, "dp", "tensor"),
            P("dp", None, "tensor"),
            P("dp", None, "tensor"),
            P("dp", "tensor"),
            P("dp", None, "tensor"),
        ),
        out_specs=(
            P("dp", None, "tensor"),
            P("dp", None, "tensor"),
            P("dp", "tensor"),
            P(None, "tensor"),
            P(None, "tensor"),
            P(None, "tensor"),
            P(None, None, "dp", "tensor"),
            P("dp", None, "tensor"),
            P("dp", None, "tensor"),
            P("dp", "tensor"),
        ),
        check_vma=False,
    )
```
